32 devices in a mesh: dp: 8 (over y, x, core), mp: 4 (over z).
Axes of the slice: x: 2, y: 2, z: 4, core: 2. Of those that a mesh axis runs over, the one named last changes fastest.
Arguments:
- tokens: float32 [8192, 1536], P(('dp', 'mp')), may hold values from -62 to 62
- attn_gain: float32 [1536], replicated, may hold values from 0.1 to 1.9
- w_query: float32 [1536, 1536], P('dp', 'mp'), may hold values from -0.15625 to 0.15625
- w_key: float32 [1536, 512], P('dp', 'mp'), may hold values from -0.15625 to 0.15625
- w_value: float32 [1536, 512], P('dp', 'mp'), may hold values from -0.15625 to 0.15625
- w_out: float32 [1536, 1536], P('mp', 'dp'), may hold values from -1.75 to 1.75
- moe_gain: float32 [1536], replicated, may hold values from 0.1 to 1.9
- w_router: float32 [1536, 16], P('dp'), may hold values from -0.109375 to 0.109375
- w_gate: float32 [16, 1536, 1024], P(None, 'dp', 'mp'), may hold values from -0.15625 to 0.15625
- w_up: float32 [16, 1536, 1024], P(None, 'dp', 'mp'), may hold values from -0.15625 to 0.15625
- w_down: float32 [16, 1024, 1536], P('dp', 'mp'), may hold values from -0.1875 to 0.1875
- seq_lengths: int32 [8, 3], P('dp'), may hold values from 1 to 512, 1024 in all within a row
- deal_order: int32 [8192], replicated, may hold values from 0 to 8191, as said below
- expert_ids: int32 [8192, 2], P('dp'), may hold values from 0 to 15, all different within a row; in each aligned block of 1024 rows (0 to 1023, 1024 to 2047, ...) at most 256 rows name the same one
- out_grad: float32 [8192, 1536], P(('dp', 'mp')), may hold values from -6 to 6
Outputs:
- block_out: float32 [8192, 1536], P(('dp', 'mp'))
- tokens_grad: float32 [8192, 1536], P(('dp', 'mp'))
- attn_gain_grad: float32 [1536], replicated
- w_query_grad: float32 [1536, 1536], P('dp', 'mp')
- w_key_grad: float32 [1536, 512], P('dp', 'mp')
- w_value_grad: float32 [1536, 512], P('dp', 'mp')
- w_out_grad: float32 [1536, 1536], P('mp', 'dp')
- moe_gain_grad: float32 [1536], replicated
- w_router_grad: float32 [1536, 16], P('dp')
- w_gate_grad: float32 [16, 1536, 1024], P(None, 'dp', 'mp')
- w_up_grad: float32 [16, 1536, 1024], P(None, 'dp', 'mp')
- w_down_grad: float32 [16, 1024, 1536], P('dp', 'mp')
The draws below stay inside these ranges and needn't reach their ends.
Inputs may be any that keep to these rules, and one draw needn't show every extreme that they name: `seq_lengths`: each row holds 3 lengths summing to 1024, the largest exactly 512. `deal_order`: a permutation of all rows; each block of 1024 dealt rows takes exactly 32 rows from every aligned span of 256 initial rows. `expert_ids`: the two experts of a row differ; within each aligned block of 1024 rows no expert is named by more than 256 rows, and one is named by exactly 256 in some blocks.
All inputs are finite; a program needn't handle non-finite values.
Results may differ from the reference program's by a relative error of at most 0.017.
Values may be sent and summed in bfloat16 or wider, within the bound.
A program may use at most 256 MiB of HBM per device.

```python
import math
import jax
import jax.numpy as jnp
import numpy as np
from jax import lax

D = 1536
HQ = 24
HD = 64
KVH = 8
FF = 1024
E = 16
SEQS = 3
TOK_G = 1024
LMAX = 512
CAP = 256
GROUPS = 8
TOKENS = 8192
N_MP = 4


def draw_tokens(key, part):
    key = jax.random.fold_in(key, 11)
    first_key, second_key, third_key = jax.random.split(key, 3)
    ramp = jnp.exp(jnp.linspace(math.log(0.4), math.log(4.0), D))
    jitter = jnp.exp(jax.random.uniform(second_key, (D,), minval=-0.25, maxval=0.25))
    row_scale = jnp.exp(jax.random.uniform(third_key, (TOKENS, 1), minval=math.log(0.3), maxval=math.log(3.0)))
    base = jnp.clip(jax.random.normal(first_key, (TOKENS, D)), -4.0, 4.0)
    return (base * ramp[None, :] * jitter[None, :] * row_scale).astype(jnp.float32)


def draw_deal_order(key, part):
    key = jax.random.fold_in(key, 23)
    first_key, second_key = jax.random.split(key)
    groups = TOKENS // TOK_G
    spans = groups * N_MP
    span_rows = TOK_G // N_MP
    per_peer = span_rows // groups
    base = jnp.broadcast_to(jnp.arange(span_rows, dtype=jnp.int32)[None, :], (spans, span_rows))
    shuffled = jax.random.permutation(first_key, base, axis=1, independent=True)
    shuffled = shuffled + (jnp.arange(spans, dtype=jnp.int32) * span_rows)[:, None]
    dealt = shuffled.reshape(spans, groups, per_peer).transpose(1, 0, 2).reshape(groups, TOK_G)
    dealt = jax.random.permutation(second_key, dealt, axis=1, independent=True)
    return dealt.reshape(-1).astype(jnp.int32)


def levels(own_key, dims, cuts, low, high):
    def one(axis_at, shards_of):
        steps = jax.random.uniform(jax.random.fold_in(jax.random.fold_in(own_key, 6), axis_at), (shards_of,), jnp.float32, low / len(cuts), high / len(cuts))
        return jnp.repeat(jnp.exp(steps), dims[axis_at] // shards_of).reshape((-1,) + (1,) * (len(dims) - axis_at - 1))

    level = one(*cuts[0])
    for cut in cuts[1:]:
        level = level * one(*cut)
    return level


def split_up(amount, total, bound, lean):
    weights = [(1 << 20) // math.isqrt(rank ** lean) + 1 for rank in range(2, amount + 1)]
    spare, counts = total - bound - (amount - 1), [1] * (amount - 1)
    while spare > 0:
        candidates = [i for i in range(amount - 1) if counts[i] < bound]
        pool, budget = sum([weights[i] for i in candidates]), spare
        for i in candidates:
            more = min(bound - counts[i], max(1, budget * weights[i] // pool), spare)
            counts[i] = counts[i] + more
            spare = spare - more
    return np.array([bound] + counts)


def ragged(rng, count, total, most, lean):
    if count == 2:
        one = jax.random.randint(rng, (), max(1, total - most), min(most, total - 1) + 1)
        return jnp.stack([one, total - one])
    sizes = jnp.asarray(split_up(count, total, most, lean), jnp.int32)
    twos = (count - 1) // 2
    donor, taker = sizes[1:1 + 2 * twos:2], sizes[2:2 + 2 * twos:2]
    room = jnp.minimum(donor - 1, most - taker)
    passed = jax.random.randint(jax.random.fold_in(rng, 1), (twos,), 0, 1 << 20) % (room + 1)
    sizes = sizes.at[1:1 + 2 * twos:2].set(donor - passed).at[2:2 + 2 * twos:2].set(taker + passed)
    return sizes[jax.random.permutation(jax.random.fold_in(rng, 2), count)]


def routed_block(own_key, own, number, rows, amount, top, limit, lean):
    sequence = jax.random.permutation(own_key, amount)
    packed, ordinary = load_shares(amount, rows * top, limit, lean, True), load_shares(amount, rows * top, limit, lean, False)
    places = jnp.arange(amount)

    def named(sizes, turn):
        used = int((sizes > 0).sum())
        fixed = max(1, used // 4)
        moved = fixed + (places - fixed + turn * (used - fixed)) % max(1, amount - fixed)
        return jnp.zeros((amount,), jnp.int32).at[sequence[jnp.where(places < fixed, places, moved)]].set(jnp.asarray(sizes, jnp.int32))

    sizes = jnp.where(number % 4 == 0, named(packed, number // 4), named(ordinary, number - number // 4 - 1))
    mixed = jax.random.permutation(jax.random.fold_in(own, 3), amount)
    donor, sink = mixed[0:amount // 2 * 2:2], mixed[1:amount // 2 * 2:2]
    slack = jnp.minimum(sizes[donor] - 1, limit - sizes[sink]) // 2
    slack = jnp.where((donor == sequence[0]) | (sink == sequence[0]) | (sizes[sink] == 0), 0, jnp.maximum(slack, 0))
    moved = jax.random.randint(jax.random.fold_in(own, 4), (amount // 2,), 0, 1 << 20) % (slack + 1)
    sizes = sizes.at[donor].add(-moved).at[sink].add(moved)
    items = jnp.searchsorted(jnp.cumsum(sizes), jnp.arange(rows * top), side="right").astype(jnp.int32)
    listing = items.reshape(top, rows).T
    listing = listing[jax.random.permutation(jax.random.fold_in(own, 1), rows)]
    turn = jax.random.randint(jax.random.fold_in(own, 2), (rows, 1), 0, top)
    return jnp.take_along_axis(listing, (jnp.arange(top)[None, :] + turn) % top, axis=1)


def load_shares(count, total, reach, lean, full):
    loads = [(1 << 20) // math.isqrt(grade ** lean) + 1 for grade in range(1, count + 1)]
    largest = reach if full else min(reach, max(-(-total // count), total * loads[0] // sum(loads)))
    least = 1 if total - largest >= count - 1 else 0
    counts, surplus = [largest] + [least] * (count - 1), total - largest - least * (count - 1)
    while surplus > 0:
        candidates = [i for i in range(1, count) if counts[i] < largest] or [i for i in range(1, count) if counts[i] < reach]
        pool, left = sum([loads[i] for i in candidates]), surplus
        for i in candidates:
            addition = min(reach - counts[i], max(1, left * loads[i] // pool), surplus)
            counts[i] = counts[i] + addition
            surplus = surplus - addition
    return np.array(counts)


def normal_values(rng, dims, spread, reach, shards=(), kind=jnp.bfloat16):
    factor_of = levels(rng, dims, shards, -0.22, 0.18) if shards else 1.0
    array = jax.random.normal(rng, dims, jnp.float32) * spread * factor_of
    return jnp.minimum(jnp.maximum(array, -reach), reach).astype(kind)


def setup_inputs(seed: int = 0) -> dict:
    arg_keys = jax.random.split(jax.random.key(seed), 16)
    tokens = draw_tokens(jax.random.fold_in(arg_keys[15], 71), 0)
    attn_gain = jnp.clip(1.0 + 0.18 * jax.random.normal(arg_keys[1], (D,), jnp.float32), 0.1, 1.9)
    w_query = normal_values(arg_keys[2], (D, HQ * HD), D ** -0.5, 0.15625, ((0, 8), (1, 4)), jnp.float32)
    w_key = normal_values(arg_keys[3], (D, KVH * HD), D ** -0.5, 0.15625, ((0, 8), (1, 4)), jnp.float32)
    w_value = normal_values(arg_keys[4], (D, KVH * HD), D ** -0.5, 0.15625, ((0, 8), (1, 4)), jnp.float32)
    w_out = normal_values(arg_keys[5], (HQ * HD, D), (HQ * HD * 4 // LMAX) ** -0.5, 1.75, ((0, 4), (1, 8)), jnp.float32)
    moe_gain = jnp.clip(1.0 + 0.18 * jax.random.normal(arg_keys[6], (D,), jnp.float32), 0.1, 1.9)
    w_router = normal_values(arg_keys[7], (D, E), (2 * D) ** -0.5, 0.109375, ((0, 8),), jnp.float32)
    w_gate = normal_values(arg_keys[8], (E, D, FF), D ** -0.5, 0.15625, ((1, 8), (2, 4)), jnp.float32)
    w_up = normal_values(arg_keys[9], (E, D, FF), D ** -0.5, 0.15625, ((1, 8), (2, 4)), jnp.float32)
    w_down = normal_values(arg_keys[10], (E, FF, D), FF ** -0.5, 0.1875, ((0, 8), (1, 4)), jnp.float32)
    seq_lengths = jax.vmap(lambda own: ragged(own, SEQS, TOK_G, LMAX, 2))(jax.random.split(arg_keys[11], GROUPS)).reshape((GROUPS, SEQS)).astype(jnp.int32)
    deal_order = draw_deal_order(jax.random.fold_in(arg_keys[15], 71), 0)
    expert_ids_keys = jax.random.split(jax.random.fold_in(arg_keys[13], 1), TOKENS // TOK_G)
    expert_ids_turns = jax.random.permutation(jax.random.fold_in(arg_keys[13], 3), TOKENS // TOK_G)
    expert_ids = jax.vmap(lambda own, number: routed_block(jax.random.fold_in(arg_keys[13], 2), own, number, TOK_G, E, 2, CAP, 1))(expert_ids_keys, expert_ids_turns).reshape((TOKENS, 2))
    out_grad = normal_values(arg_keys[14], (TOKENS, D), 1.0, 6.0, ((0, 32),), jnp.float32)
    return dict(tokens=tokens, attn_gain=attn_gain, w_query=w_query, w_key=w_key, w_value=w_value, w_out=w_out, moe_gain=moe_gain, w_router=w_router, w_gate=w_gate, w_up=w_up, w_down=w_down, seq_lengths=seq_lengths, deal_order=deal_order, expert_ids=expert_ids, out_grad=out_grad)


EPS = 1e-05
HIGH = lax.Precision.HIGHEST

@jax.custom_vjp
def low(v):
    return lax.optimization_barrier(v.astype(jnp.bfloat16)).astype(jnp.float32)

@jax.custom_vjp
def low_back(v):
    return v

def low_keep(v):
    return (low(v), None)

def low_pass(kept, grad):
    return (grad,)

def back_keep(v):
    return (v, None)

def back_low(kept, grad):
    return (low(grad),)
low.defvjp(low_keep, low_pass)
low_back.defvjp(back_keep, back_low)

def rms_norm(values, gain):
    scale = lax.rsqrt(lax.optimization_barrier(jnp.mean(values * values, axis=-1, keepdims=True)) + EPS)
    return values * scale * gain

def segment_of(lengths):
    ends = jnp.cumsum(lengths).astype(jnp.int32)
    places = jnp.arange(TOK_G, dtype=jnp.int32)
    return lax.optimization_barrier(jnp.sum((places[:, None] >= ends[None, :]).astype(jnp.int32), axis=1))

def group_attention(query, key, value, lengths):
    segment = segment_of(lengths)
    places = jnp.arange(TOK_G, dtype=jnp.int32)
    allowed = (segment[:, None] == segment[None, :]) & (places[None, :] <= places[:, None])
    share = HQ // KVH
    query_h = query.reshape(TOK_G, KVH, share, HD)
    key_h = key.reshape(TOK_G, KVH, HD)
    value_h = value.reshape(TOK_G, KVH, HD)
    scores = jnp.einsum('qgsd,tgd->gsqt', query_h, key_h, precision=HIGH) * HD ** (-0.5)
    scores = low_back(scores)
    scores = jnp.where(allowed, scores, -1e+30)
    probs = jax.nn.softmax(scores, axis=-1)
    mixed = jnp.einsum('gsqt,tgd->qgsd', low(probs), value_h, precision=HIGH)
    return mixed.reshape(TOK_G, HQ * HD)

def slot_table(expert_ids):
    flat = expert_ids.reshape(-1)
    hits = (flat[:, None] == jnp.arange(E, dtype=jnp.int32)[None, :]).astype(jnp.int32)
    rank = lax.optimization_barrier(jnp.sum((jnp.cumsum(hits, axis=0) - hits) * hits, axis=1))
    return (flat * CAP + rank).astype(jnp.int32)

def group_experts(rows, gates, expert_ids, gate_w, up_w, down_w):
    slots = slot_table(expert_ids)
    owner = jnp.zeros((E * CAP,), jnp.int32).at[slots].set(jnp.arange(2 * TOK_G, dtype=jnp.int32) // 2)
    buffer = rows[owner].reshape(E, CAP, D)
    gate_part = low_back(jnp.einsum('ecd,edf->ecf', buffer, gate_w, precision=HIGH))
    up_part = low_back(jnp.einsum('ecd,edf->ecf', buffer, up_w, precision=HIGH))
    hidden = low(jax.nn.silu(gate_part) * up_part)
    each = low_back(jnp.einsum('ecf,efd->ecd', hidden, down_w, precision=HIGH)).reshape(E * CAP, D)
    picked = each[slots].reshape(TOK_G, 2, D)
    return lax.optimization_barrier(jnp.sum(picked * gates[:, :, None], axis=1))

def block_forward(tokens, attn_gain, w_query, w_key, w_value, w_out, moe_gain, w_router, w_gate, w_up, w_down, seq_lengths, deal_order, expert_ids):
    groups = TOKENS // TOK_G
    first = low(rms_norm(tokens, attn_gain))
    query = low_back(low(jnp.dot(first, low(w_query), precision=HIGH)))
    key = low_back(low(jnp.dot(first, low(w_key), precision=HIGH)))
    value = low_back(low(jnp.dot(first, low(w_value), precision=HIGH)))
    attend = jax.checkpoint(group_attention)
    mix = lax.map(lambda item: attend(item[0], item[1], item[2], item[3]), (query.reshape(groups, TOK_G, HQ * HD), key.reshape(groups, TOK_G, KVH * HD), value.reshape(groups, TOK_G, KVH * HD), seq_lengths))
    mix = low_back(low(mix.reshape(TOKENS, HQ * HD)))
    middle = tokens + low_back(jnp.dot(mix, low(w_out), precision=HIGH))
    second = low(rms_norm(middle, moe_gain))
    dealt = second[deal_order]
    logits = low_back(jnp.dot(dealt, low(w_router), precision=HIGH))
    chosen = jnp.take_along_axis(logits, expert_ids, axis=1)
    gates = jax.nn.softmax(chosen, axis=1)
    gate_w, up_w, down_w = (low(w_gate), low(w_up), low(w_down))
    expert_step = jax.checkpoint(group_experts)
    moe = lax.map(lambda item: expert_step(item[0], item[1], item[2], gate_w, up_w, down_w), (dealt.reshape(groups, TOK_G, D), gates.reshape(groups, TOK_G, 2), expert_ids.reshape(groups, TOK_G, 2)))
    moe = moe.reshape(TOKENS, D)
    home = jnp.zeros_like(moe).at[deal_order].set(moe)
    return middle + low_back(home)

def reference(tokens, attn_gain, w_query, w_key, w_value, w_out, moe_gain, w_router, w_gate, w_up, w_down, seq_lengths, deal_order, expert_ids, out_grad):

    def forward(a, b, c, d, e, f, g, h, i, j, k):
        return block_forward(a, b, c, d, e, f, g, h, i, j, k, seq_lengths, deal_order, expert_ids)
    block_out, pull = jax.vjp(forward, tokens.astype(jnp.float32), attn_gain.astype(jnp.float32), w_query.astype(jnp.float32), w_key.astype(jnp.float32), w_value.astype(jnp.float32), w_out.astype(jnp.float32), moe_gain.astype(jnp.float32), w_router.astype(jnp.float32), w_gate.astype(jnp.float32), w_up.astype(jnp.float32), w_down.astype(jnp.float32))
    grads = pull(out_grad.astype(jnp.float32))
    return (block_out, grads[0], grads[1], grads[2], grads[3], grads[4], grads[5], grads[6], grads[7], grads[8], grads[9], grads[10])
```

```python
import functools

import jax
import jax.numpy as jnp
from jax import lax
from jax.experimental import pallas as pl
from jax.experimental.pallas import tpu as pltpu
from jax.sharding import PartitionSpec as P

D = 1536
HD = 64
E = 16
CAP = 256


EPS = 1e-05


def full_rows(values):
    return lax.all_gather(values, "mp", axis=0, tiled=True)


def row_share(partial_value):
    return lax.psum_scatter(partial_value, "mp", scatter_dimension=0, tiled=True)


def norm_apply(values, gain):
    energy = jnp.mean(values * values, axis=1)
    scale = lax.rsqrt(energy + EPS)
    normed = values * scale[:, None] * gain[None, :]
    return (scale, normed.astype(jnp.bfloat16))


def norm_back(values, gain, scale, grad_normed):
    weighted = grad_normed * gain[None, :]
    inner = jnp.mean(weighted * values, axis=1)
    grad_in = scale[:, None] * weighted - values * (scale * scale * scale * inner)[:, None]
    gain_grad = jnp.sum(grad_normed * values * scale[:, None], axis=0)
    return (grad_in, gain_grad)


def deal_tables(deal_order, expert_ids, block):
    groups = lax.axis_size("dp")
    parts = lax.axis_size("mp")
    me_index = lax.axis_index("dp")
    part_index = lax.axis_index("mp")
    shard = block // parts
    own = (me_index * parts + part_index) * shard + jnp.arange(shard, dtype=jnp.int32)
    spots = jnp.arange(deal_order.shape[0], dtype=jnp.int32)
    dealt = jnp.sum(jnp.where(deal_order[:, None] == own[None, :], spots[:, None], 0), axis=0)
    home = jnp.sum((dealt[:, None] < dealt[None, :]).astype(jnp.int32), axis=0)
    mine = lax.dynamic_slice_in_dim(deal_order, me_index * block, block, 0)
    anchor = (mine % block) // shard * groups + mine // block
    key = anchor * block + jnp.arange(block, dtype=jnp.int32)
    arrival = jnp.sum((key[:, None] < key[None, :]).astype(jnp.int32), axis=0)
    pair = expert_ids[:, 0] * E + expert_ids[:, 1]
    hits = arrival[:, None] == jnp.arange(block, dtype=jnp.int32)[None, :]
    code = jnp.sum(jnp.where(hits, pair[:, None], 0), axis=0)
    order = jnp.sum(jnp.where(home[:, None] == jnp.arange(shard, dtype=jnp.int32)[None, :],
                              jnp.arange(shard, dtype=jnp.int32)[:, None], 0), axis=0)
    counts = jnp.sum((expert_ids.reshape(-1)[:, None] == jnp.arange(E, dtype=jnp.int32)[None, :]).astype(jnp.int32), axis=0)
    return (home, order, code[None, :], counts)


def to_dealt(values, order):
    moved = lax.all_to_all(values[order], "dp", split_axis=0, concat_axis=0, tiled=True)
    return full_rows(moved)


def to_home(stretch, home):
    moved = lax.all_to_all(stretch, "dp", split_axis=0, concat_axis=0, tiled=True)
    return moved[home].astype(jnp.float32)


def segment_of(lengths, rows):
    ends = jnp.cumsum(lengths)
    places = jnp.arange(rows, dtype=jnp.int32)
    return jnp.sum((places[:, None] >= ends[None, :]).astype(jnp.int32), axis=1)


def visible(segment, start, finish):
    query_pos = jnp.arange(start, finish, dtype=jnp.int32)
    key_pos = jnp.arange(finish, dtype=jnp.int32)
    same = segment[start:finish][:, None] == segment[:finish][None, :]
    return same & (key_pos[None, :] <= query_pos[:, None])


def block_scores(query, key, segment, start, block, heads_kv, share):
    finish = start + block
    query_rows = query[start:finish].reshape(block, heads_kv, share, HD)
    key_rows = key[:finish].reshape(finish, heads_kv, HD)
    scores = jnp.einsum(
        "qgsd,tgd->gsqt", query_rows, key_rows, preferred_element_type=jnp.float32
    ) * HD ** (-0.5)
    return (query_rows, key_rows, jnp.where(visible(segment, start, finish), scores, -1e30))


def attend_forward(query, key, value, segment):
    rows = query.shape[0]
    heads_kv = key.shape[1] // HD
    share = query.shape[1] // key.shape[1]
    block = min(512, rows)
    outputs, totals = ([], [])
    for start in range(0, rows, block):
        finish = start + block
        query_rows, key_rows, masked = block_scores(
            query, key, segment, start, block, heads_kv, share
        )
        value_rows = value[:finish].reshape(finish, heads_kv, HD)
        highest = jnp.max(masked, axis=-1, keepdims=True)
        raised = jnp.exp(masked - highest)
        total = jnp.sum(raised, axis=-1, keepdims=True)
        probs = (raised / total).astype(jnp.bfloat16)
        mixed = jnp.einsum("gsqt,tgd->qgsd", probs, value_rows, preferred_element_type=jnp.float32)
        outputs.append(mixed.reshape(block, -1))
        totals.append(highest + jnp.log(total))
    return (jnp.concatenate(outputs, axis=0), totals)


def attend_back(query, key, value, segment, grad_mix, totals):
    rows = query.shape[0]
    heads_kv = key.shape[1] // HD
    share = query.shape[1] // key.shape[1]
    block = min(512, rows)
    scale = HD ** (-0.5)
    grad_query = []
    grad_key = jnp.zeros((rows, heads_kv, HD), jnp.float32)
    grad_value = jnp.zeros((rows, heads_kv, HD), jnp.float32)
    for number, start in enumerate(range(0, rows, block)):
        finish = start + block
        query_rows, key_rows, masked = block_scores(
            query, key, segment, start, block, heads_kv, share
        )
        value_rows = value[:finish].reshape(finish, heads_kv, HD)
        probs = jnp.exp(masked - totals[number])
        grad_rows = grad_mix[start:finish].reshape(block, heads_kv, share, HD)
        grad_probs = jnp.einsum(
            "qgsd,tgd->gsqt", grad_rows, value_rows, preferred_element_type=jnp.float32
        )
        inner = jnp.sum(probs * grad_probs, axis=-1, keepdims=True)
        grad_scores = (probs * (grad_probs - inner)).astype(jnp.bfloat16)
        piece = (
            jnp.einsum("gsqt,tgd->qgsd", grad_scores, key_rows, preferred_element_type=jnp.float32)
            * scale
        )
        grad_query.append(piece.reshape(block, -1))
        grad_key = grad_key.at[:finish].add(
            jnp.einsum(
                "gsqt,qgsd->tgd", grad_scores, query_rows, preferred_element_type=jnp.float32
            )
            * scale
        )
        grad_value = grad_value.at[:finish].add(
            jnp.einsum(
                "gsqt,qgsd->tgd",
                probs.astype(jnp.bfloat16),
                grad_rows,
                preferred_element_type=jnp.float32,
            )
        )
    grad_query = jnp.concatenate(grad_query, axis=0).astype(jnp.bfloat16)
    return (
        grad_query,
        grad_key.reshape(rows, -1).astype(jnp.bfloat16),
        grad_value.reshape(rows, -1).astype(jnp.bfloat16),
    )


def mm(a, b, dims=((1,), (0,))):
    return lax.dot_general(a, b, (dims, ((), ())), preferred_element_type=jnp.float32)


NT = ((1,), (1,))
TN = ((0,), (0,))


def expert_step(width, e, refs):
    (second, grad, gate_w, up_w, down_w, gate_out, up_out, down_out, rank, gates, dots, mixed, back) = refs
    rows = second.shape[0]
    low = jnp.bfloat16
    place = lax.broadcasted_iota(jnp.int32, (width, rows), 0).astype(jnp.float32)
    hit = place == rank[pl.ds(e, 1), :]
    pick = jnp.where(hit, 1.0, 0.0).astype(low)
    gate = jnp.sum(jnp.where(hit, gates[pl.ds(e, 1), :], 0.0), axis=1, keepdims=True)
    x = mm(pick, second[...]).astype(low)
    grad_rows = mm(pick, grad[...])
    gate_part = mm(x, gate_w[0])
    up_part = mm(x, up_w[0])
    sigma = jax.nn.sigmoid(gate_part)
    hidden = (gate_part * sigma * up_part).astype(low)
    each = mm(hidden, down_w[0])
    dot = jnp.sum(grad_rows * each, axis=1, keepdims=True)
    dots[pl.ds(e, 1), :] = jnp.sum(jnp.where(hit, dot, 0.0), axis=0, keepdims=True)
    mixed[...] += mm(pick, (each * gate).astype(low), TN)
    grad_each = (grad_rows * gate).astype(low)
    grad_hidden = mm(grad_each, down_w[0], NT)
    grad_gate = (grad_hidden * up_part * sigma * (1.0 + gate_part * (1.0 - sigma))).astype(low)
    grad_up = (grad_hidden * gate_part * sigma).astype(low)
    down_out[0] = mm(hidden, grad_each, TN).astype(low)
    gate_out[0] = mm(x, grad_gate, TN).astype(low)
    up_out[0] = mm(x, grad_up, TN).astype(low)
    back_rows = mm(grad_gate, gate_w[0], NT) + mm(grad_up, up_w[0], NT)
    back[...] += mm(pick, back_rows.astype(low), TN)


def expert_kernel(counts, code, router, second, grad, gate_w, up_w, down_w,
                  mixed_out, back_out, gate_out, up_out, down_out, router_out,
                  rank, gates, dots, mixed, back):
    e = pl.program_id(0)
    rows = second.shape[0]
    low = jnp.bfloat16
    expert = lax.broadcasted_iota(jnp.int32, (E, rows), 0)
    first_id = code[...] // E
    second_id = code[...] % E
    picks = [jnp.where(expert == ids, 1.0, 0.0) for ids in (first_id, second_id)]

    @pl.when(e == 0)
    def _():
        logits = mm(router[...], second[...], NT)
        chosen = [jnp.sum(pick * logits, axis=0, keepdims=True) for pick in picks]
        top = jnp.maximum(chosen[0], chosen[1])
        raised = [jnp.exp(value - top) for value in chosen]
        total = raised[0] + raised[1]
        gates[...] = picks[0] * (raised[0] / total) + picks[1] * (raised[1] / total)
        hits = picks[0] + picks[1]
        earlier = lax.broadcasted_iota(jnp.int32, (rows, rows), 0) < lax.broadcasted_iota(
            jnp.int32, (rows, rows), 1
        )
        before = mm(hits.astype(low), jnp.where(earlier, 1.0, 0.0).astype(low))
        rank[...] = jnp.where(hits > 0.0, before, -1.0)
        mixed[...] = jnp.zeros_like(mixed)
        back[...] = jnp.zeros_like(back)

    refs = (second, grad, gate_w, up_w, down_w, gate_out, up_out, down_out, rank, gates, dots, mixed, back)
    count = counts[e]

    @pl.when(count <= CAP // 2)
    def _():
        expert_step(CAP // 2, e, refs)

    @pl.when(count > CAP // 2)
    def _():
        expert_step(CAP, e, refs)

    @pl.when(e == E - 1)
    def _():
        grad_gates = [jnp.sum(pick * dots[...], axis=0, keepdims=True) for pick in picks]
        own = [jnp.sum(pick * gates[...], axis=0, keepdims=True) for pick in picks]
        inner = own[0] * grad_gates[0] + own[1] * grad_gates[1]
        grad_logits = picks[0] * (own[0] * (grad_gates[0] - inner)) + picks[1] * (
            own[1] * (grad_gates[1] - inner)
        )
        grad_logits = grad_logits.astype(low)
        router_out[...] = mm(grad_logits, second[...])
        mixed_out[...] = mixed[...].astype(low)
        back_out[...] = (back[...] + mm(grad_logits, router[...], TN)).astype(low)


def experts(second, grad, code, counts, router, gate_w, up_w, down_w):
    rows = second.shape[0]
    hidden = gate_w.shape[2]
    low = jnp.bfloat16
    whole = lambda e, *_: (0, 0)
    by_expert = lambda e, *_: (e, 0, 0)
    wide = pl.BlockSpec((1, D, hidden), by_expert)
    tall = pl.BlockSpec((1, hidden, D), by_expert)
    block = pl.BlockSpec((rows, D), whole)
    return pl.pallas_call(
        expert_kernel,
        grid_spec=pltpu.PrefetchScalarGridSpec(
            num_scalar_prefetch=1,
            grid=(E,),
            in_specs=[
                pl.BlockSpec((1, rows), whole),
                pl.BlockSpec((E, D), whole),
                block,
                block,
                wide,
                wide,
                tall,
            ],
            out_specs=[block, block, wide, wide, tall, pl.BlockSpec((E, D), whole)],
            scratch_shapes=[
                pltpu.VMEM((E, rows), jnp.float32),
                pltpu.VMEM((E, rows), jnp.float32),
                pltpu.VMEM((E, rows), jnp.float32),
                pltpu.VMEM((rows, D), jnp.float32),
                pltpu.VMEM((rows, D), jnp.float32),
            ],
        ),
        out_shape=[
            jax.ShapeDtypeStruct((rows, D), low),
            jax.ShapeDtypeStruct((rows, D), low),
            jax.ShapeDtypeStruct((E, D, hidden), low),
            jax.ShapeDtypeStruct((E, D, hidden), low),
            jax.ShapeDtypeStruct((E, hidden, D), low),
            jax.ShapeDtypeStruct((E, D), jnp.float32),
        ],
        compiler_params=pltpu.CompilerParams(
            dimension_semantics=("arbitrary",), vmem_limit_bytes=58 * 2**20
        ),
        cost_estimate=pl.CostEstimate(
            flops=E * CAP * D * (18 * hidden + 8 * rows),
            bytes_accessed=12 * E * D * hidden + 8 * rows * D,
            transcendentals=E * CAP * hidden,
        ),
    )(counts, code, router, second, grad, gate_w, up_w, down_w)


def body(
    tokens,
    attn_gain,
    w_query,
    w_key,
    w_value,
    w_out,
    moe_gain,
    w_router,
    w_gate,
    w_up,
    w_down,
    seq_lengths,
    deal_order,
    expert_ids,
    out_grad,
):
    rows = tokens.shape[0] * lax.axis_size("mp")
    low_type = jnp.bfloat16
    query_w, key_w, value_w, out_w, router_w, gate_w, up_w, down_w = (
        lax.all_gather(w_query.astype(low_type), "dp", axis=0, tiled=True),
        lax.all_gather(w_key.astype(low_type), "dp", axis=0, tiled=True),
        lax.all_gather(w_value.astype(low_type), "dp", axis=0, tiled=True),
        lax.all_gather(w_out.astype(low_type), "dp", axis=1, tiled=True),
        lax.all_gather(w_router.astype(low_type), "dp", axis=0, tiled=True),
        lax.all_gather(w_gate.astype(low_type), "dp", axis=1, tiled=True),
        lax.all_gather(w_up.astype(low_type), "dp", axis=1, tiled=True),
        lax.all_gather(w_down.astype(low_type), "dp", axis=0, tiled=True),
    )
    home, order, code, counts = deal_tables(deal_order, expert_ids, rows)
    segment = segment_of(seq_lengths[0], rows)
    scale_one, normed_one = norm_apply(tokens, attn_gain)
    first_full = full_rows(normed_one)
    query = jnp.dot(first_full, query_w, preferred_element_type=jnp.float32).astype(low_type)
    key = jnp.dot(first_full, key_w, preferred_element_type=jnp.float32).astype(low_type)
    value = jnp.dot(first_full, value_w, preferred_element_type=jnp.float32).astype(low_type)
    mix, totals = attend_forward(query, key, value, segment)
    mix = mix.astype(low_type)
    middle = tokens + row_share(jnp.dot(mix, out_w, preferred_element_type=jnp.float32).astype(low_type)).astype(jnp.float32)
    scale_two, normed_two = norm_apply(middle, moe_gain)
    second_full = to_dealt(normed_two, order)
    grad_full = to_dealt(out_grad.astype(low_type), order)
    mixed, back, grad_gate_all, grad_up_all, grad_down_all, grad_router = experts(
        second_full, grad_full, code, counts, router_w.T, gate_w, up_w, down_w
    )
    grad_normed_two = to_home(row_share(back), home)
    block_out = middle + to_home(row_share(mixed), home)
    grad_middle_norm, grad_moe_gain = norm_back(middle, moe_gain, scale_two, grad_normed_two)
    grad_middle = out_grad + grad_middle_norm
    grad_attn_full = full_rows(grad_middle.astype(low_type))
    grad_mix = jnp.einsum(
        "td,hd->th", grad_attn_full, out_w, preferred_element_type=jnp.float32
    ).astype(low_type)
    grad_out_w = jnp.einsum("th,td->hd", mix, grad_attn_full, preferred_element_type=jnp.float32)
    grad_query, grad_key, grad_value = attend_back(query, key, value, segment, grad_mix, totals)
    grad_first = jnp.einsum("th,dh->td", grad_query, query_w, preferred_element_type=jnp.float32)
    grad_first = grad_first + jnp.einsum(
        "th,dh->td", grad_key, key_w, preferred_element_type=jnp.float32
    )
    grad_first = grad_first + jnp.einsum(
        "th,dh->td", grad_value, value_w, preferred_element_type=jnp.float32
    )
    grad_query_w = jnp.einsum(
        "td,th->dh", first_full, grad_query, preferred_element_type=jnp.float32
    )
    grad_key_w = jnp.einsum("td,th->dh", first_full, grad_key, preferred_element_type=jnp.float32)
    grad_value_w = jnp.einsum(
        "td,th->dh", first_full, grad_value, preferred_element_type=jnp.float32
    )
    grad_tokens_norm, grad_attn_gain = norm_back(
        tokens, attn_gain, scale_one, row_share(grad_first.astype(low_type)).astype(jnp.float32)
    )
    tokens_grad = grad_middle + grad_tokens_norm
    attn_gain_sum, moe_gain_sum, router_total = lax.psum(
        (grad_attn_gain, grad_moe_gain, grad_router), ("dp", "mp")
    )
    width = w_router.shape[0]
    router_sum = lax.dynamic_slice_in_dim(router_total, lax.axis_index("dp") * width, width, 1).T
    query_sum, key_sum, value_sum, out_sum, gate_sum, up_sum, down_sum = (
        lax.psum_scatter(
            grad_query_w.astype(jnp.bfloat16), "dp", scatter_dimension=0, tiled=True
        ).astype(jnp.float32),
        lax.psum_scatter(
            grad_key_w.astype(jnp.bfloat16), "dp", scatter_dimension=0, tiled=True
        ).astype(jnp.float32),
        lax.psum_scatter(
            grad_value_w.astype(jnp.bfloat16), "dp", scatter_dimension=0, tiled=True
        ).astype(jnp.float32),
        lax.psum_scatter(
            grad_out_w.astype(jnp.bfloat16), "dp", scatter_dimension=1, tiled=True
        ).astype(jnp.float32),
        lax.psum_scatter(
            grad_gate_all.astype(jnp.bfloat16), "dp", scatter_dimension=1, tiled=True
        ).astype(jnp.float32),
        lax.psum_scatter(
            grad_up_all.astype(jnp.bfloat16), "dp", scatter_dimension=1, tiled=True
        ).astype(jnp.float32),
        lax.psum_scatter(
            grad_down_all.astype(jnp.bfloat16), "dp", scatter_dimension=0, tiled=True
        ).astype(jnp.float32),
    )
    return (
        block_out,
        tokens_grad,
        attn_gain_sum,
        query_sum,
        key_sum,
        value_sum,
        out_sum,
        moe_gain_sum,
        router_sum,
        gate_sum,
        up_sum,
        down_sum,
    )


def solution(mesh):
    return jax.shard_map(
        body,
        mesh=mesh,
        in_specs=(
            P(("dp", "mp"), None),
            P(),
            P("dp", "mp"),
            P("dp", "mp"),
            P("dp", "mp"),
            P("mp", "dp"),
            P(),
            P("dp", None),
            P(None, "dp", "mp"),
            P(None, "dp", "mp"),
            P("dp", "mp", None),
            P("dp", None),
            P(),
            P("dp", None),
            P(("dp", "mp"), None),
        ),
        out_specs=(
            P(("dp", "mp"), None),
            P(("dp", "mp"), None),
            P(),
            P("dp", "mp"),
            P("dp", "mp"),
            P("dp", "mp"),
            P("mp", "dp"),
            P(),
            P("dp", None),
            P(None, "dp", "mp"),
            P(None, "dp", "mp"),
            P("dp", "mp", None),
        ),
        check_vma=False,
    )
```

```python
import functools

import jax
import jax.numpy as jnp
from jax import lax
from jax.experimental import pallas as pl
from jax.experimental.pallas import tpu as pltpu
from jax.sharding import PartitionSpec as P

D = 1536
HD = 64
E = 16
CAP = 256
MESH = pl.DeviceIdType.MESH


EPS = 1e-05


def full_rows(values):
    return lax.all_gather(values, "mp", axis=0, tiled=True)


def row_share(partial_value):
    return lax.psum_scatter(partial_value, "mp", scatter_dimension=0, tiled=True)


def norm_apply(values, gain):
    energy = jnp.mean(values * values, axis=1)
    scale = lax.rsqrt(energy + EPS)
    normed = values * scale[:, None] * gain[None, :]
    return (scale, normed.astype(jnp.bfloat16))


def norm_back(values, gain, scale, grad_normed):
    weighted = grad_normed * gain[None, :]
    inner = jnp.mean(weighted * values, axis=1)
    grad_in = scale[:, None] * weighted - values * (scale * scale * scale * inner)[:, None]
    gain_grad = jnp.sum(grad_normed * values * scale[:, None], axis=0)
    return (grad_in, gain_grad)


def deal_tables(deal_order, expert_ids, block):
    groups = lax.axis_size("dp")
    parts = lax.axis_size("mp")
    me_index = lax.axis_index("dp")
    part_index = lax.axis_index("mp")
    shard = block // parts
    own = (me_index * parts + part_index) * shard + jnp.arange(shard, dtype=jnp.int32)
    spots = jnp.arange(deal_order.shape[0], dtype=jnp.int32)
    dealt = jnp.sum(jnp.where(deal_order[:, None] == own[None, :], spots[:, None], 0), axis=0)
    home = jnp.sum((dealt[:, None] < dealt[None, :]).astype(jnp.int32), axis=0)
    mine = lax.dynamic_slice_in_dim(deal_order, me_index * block, block, 0)
    anchor = (mine % block) // shard * groups + mine // block
    key = anchor * block + jnp.arange(block, dtype=jnp.int32)
    arrival = jnp.sum((key[:, None] < key[None, :]).astype(jnp.int32), axis=0)
    pair = expert_ids[:, 0] * E + expert_ids[:, 1]
    hits = arrival[:, None] == jnp.arange(block, dtype=jnp.int32)[None, :]
    code = jnp.sum(jnp.where(hits, pair[:, None], 0), axis=0)
    counts = jnp.sum((expert_ids.reshape(-1)[:, None] == jnp.arange(E, dtype=jnp.int32)[None, :]).astype(jnp.int32), axis=0)
    return (home, code[None, :], counts)


def to_home(stretch, home):
    moved = lax.all_to_all(stretch, "dp", split_axis=0, concat_axis=0, tiled=True)
    return moved[home].astype(jnp.float32)


def segment_of(lengths, rows):
    ends = jnp.cumsum(lengths)
    places = jnp.arange(rows, dtype=jnp.int32)
    return jnp.sum((places[:, None] >= ends[None, :]).astype(jnp.int32), axis=1)


def visible(segment, start, finish):
    query_pos = jnp.arange(start, finish, dtype=jnp.int32)
    key_pos = jnp.arange(finish, dtype=jnp.int32)
    same = segment[start:finish][:, None] == segment[:finish][None, :]
    return same & (key_pos[None, :] <= query_pos[:, None])


def block_scores(query, key, segment, start, block, heads_kv, share):
    finish = start + block
    query_rows = query[start:finish].reshape(block, heads_kv, share, HD)
    key_rows = key[:finish].reshape(finish, heads_kv, HD)
    scores = jnp.einsum(
        "qgsd,tgd->gsqt", query_rows, key_rows, preferred_element_type=jnp.float32
    ) * HD ** (-0.5)
    return (query_rows, key_rows, jnp.where(visible(segment, start, finish), scores, -1e30))


def attend_totals(query, key, segment):
    rows = query.shape[0]
    heads_kv = key.shape[1] // HD
    share = query.shape[1] // key.shape[1]
    block = min(512, rows)
    totals = []
    for start in range(0, rows, block):
        _, _, masked = block_scores(query, key, segment, start, block, heads_kv, share)
        totals.append(jax.nn.logsumexp(masked, axis=-1, keepdims=True))
    return totals


def attend_back(query, key, value, segment, grad_mix, totals):
    rows = query.shape[0]
    heads_kv = key.shape[1] // HD
    share = query.shape[1] // key.shape[1]
    block = min(512, rows)
    scale = HD ** (-0.5)
    grad_query = []
    grad_key = jnp.zeros((rows, heads_kv, HD), jnp.float32)
    grad_value = jnp.zeros((rows, heads_kv, HD), jnp.float32)
    for number, start in enumerate(range(0, rows, block)):
        finish = start + block
        query_rows, key_rows, masked = block_scores(
            query, key, segment, start, block, heads_kv, share
        )
        value_rows = value[:finish].reshape(finish, heads_kv, HD)
        probs = jnp.exp(masked - totals[number])
        grad_rows = grad_mix[start:finish].reshape(block, heads_kv, share, HD)
        grad_probs = jnp.einsum(
            "qgsd,tgd->gsqt", grad_rows, value_rows, preferred_element_type=jnp.float32
        )
        inner = jnp.sum(probs * grad_probs, axis=-1, keepdims=True)
        grad_scores = (probs * (grad_probs - inner)).astype(jnp.bfloat16)
        piece = (
            jnp.einsum("gsqt,tgd->qgsd", grad_scores, key_rows, preferred_element_type=jnp.float32)
            * scale
        )
        grad_query.append(piece.reshape(block, -1))
        grad_key = grad_key.at[:finish].add(
            jnp.einsum(
                "gsqt,qgsd->tgd", grad_scores, query_rows, preferred_element_type=jnp.float32
            )
            * scale
        )
        grad_value = grad_value.at[:finish].add(
            jnp.einsum(
                "gsqt,qgsd->tgd",
                probs.astype(jnp.bfloat16),
                grad_rows,
                preferred_element_type=jnp.float32,
            )
        )
    grad_query = jnp.concatenate(grad_query, axis=0).astype(jnp.bfloat16)
    return (
        grad_query,
        grad_key.reshape(rows, -1).astype(jnp.bfloat16),
        grad_value.reshape(rows, -1).astype(jnp.bfloat16),
    )


def mm(a, b, dims=((1,), (0,))):
    return lax.dot_general(a, b, (dims, ((), ())), preferred_element_type=jnp.float32)


NT = ((1,), (1,))
TN = ((0,), (0,))


def expert_step(width, e, refs):
    (second, grad, gate_w, up_w, down_w, gate_out, up_out, down_out, rank, gates, dots, mixed, back) = refs
    rows = second.shape[0]
    low = jnp.bfloat16
    place = lax.broadcasted_iota(jnp.int32, (width, rows), 0).astype(jnp.float32)
    hit = place == rank[pl.ds(e, 1), :]
    pick = jnp.where(hit, 1.0, 0.0).astype(low)
    gate = jnp.sum(jnp.where(hit, gates[pl.ds(e, 1), :], 0.0), axis=1, keepdims=True)
    x = mm(pick, second[...]).astype(low)
    grad_rows = mm(pick, grad[...])
    gate_part = mm(x, gate_w[0])
    up_part = mm(x, up_w[0])
    sigma = jax.nn.sigmoid(gate_part)
    hidden = (gate_part * sigma * up_part).astype(low)
    each = mm(hidden, down_w[0])
    dot = jnp.sum(grad_rows * each, axis=1, keepdims=True)
    dots[pl.ds(e, 1), :] = jnp.sum(jnp.where(hit, dot, 0.0), axis=0, keepdims=True)
    mixed[...] += mm(pick, (each * gate).astype(low), TN)
    grad_each = (grad_rows * gate).astype(low)
    grad_hidden = mm(grad_each, down_w[0], NT)
    grad_gate = (grad_hidden * up_part * sigma * (1.0 + gate_part * (1.0 - sigma))).astype(low)
    grad_up = (grad_hidden * gate_part * sigma).astype(low)
    down_out[0] = mm(hidden, grad_each, TN).astype(low)
    gate_out[0] = mm(x, grad_gate, TN).astype(low)
    up_out[0] = mm(x, grad_up, TN).astype(low)
    back_rows = mm(grad_gate, gate_w[0], NT) + mm(grad_up, up_w[0], NT)
    back[...] += mm(pick, back_rows.astype(low), TN)


def expert_kernel(counts, code, router, second, grad, gate_w, up_w, down_w,
                  mixed_out, back_out, gate_out, up_out, down_out, router_out,
                  rank, gates, dots, mixed, back):
    e = pl.program_id(0)
    rows = second.shape[0]
    low = jnp.bfloat16
    expert = lax.broadcasted_iota(jnp.int32, (E, rows), 0)
    first_id = code[...] // E
    second_id = code[...] % E
    picks = [jnp.where(expert == ids, 1.0, 0.0) for ids in (first_id, second_id)]

    @pl.when(e == 0)
    def _():
        logits = mm(router[...], second[...], NT)
        chosen = [jnp.sum(pick * logits, axis=0, keepdims=True) for pick in picks]
        top = jnp.maximum(chosen[0], chosen[1])
        raised = [jnp.exp(value - top) for value in chosen]
        total = raised[0] + raised[1]
        gates[...] = picks[0] * (raised[0] / total) + picks[1] * (raised[1] / total)
        hits = picks[0] + picks[1]
        earlier = lax.broadcasted_iota(jnp.int32, (rows, rows), 0) < lax.broadcasted_iota(
            jnp.int32, (rows, rows), 1
        )
        before = mm(hits.astype(low), jnp.where(earlier, 1.0, 0.0).astype(low))
        rank[...] = jnp.where(hits > 0.0, before, -1.0)
        mixed[...] = jnp.zeros_like(mixed)
        back[...] = jnp.zeros_like(back)

    refs = (second, grad, gate_w, up_w, down_w, gate_out, up_out, down_out, rank, gates, dots, mixed, back)
    count = counts[e]

    @pl.when(count <= CAP // 2)
    def _():
        expert_step(CAP // 2, e, refs)

    @pl.when(count > CAP // 2)
    def _():
        expert_step(CAP, e, refs)

    @pl.when(e == E - 1)
    def _():
        grad_gates = [jnp.sum(pick * dots[...], axis=0, keepdims=True) for pick in picks]
        own = [jnp.sum(pick * gates[...], axis=0, keepdims=True) for pick in picks]
        inner = own[0] * grad_gates[0] + own[1] * grad_gates[1]
        grad_logits = picks[0] * (own[0] * (grad_gates[0] - inner)) + picks[1] * (
            own[1] * (grad_gates[1] - inner)
        )
        grad_logits = grad_logits.astype(low)
        router_out[...] = mm(grad_logits, second[...])
        mixed_out[...] = mixed[...].astype(low)
        back_out[...] = (back[...] + mm(grad_logits, router[...], TN)).astype(low)


def experts(second, grad, code, counts, router, gate_w, up_w, down_w):
    rows = second.shape[0]
    hidden = gate_w.shape[2]
    low = jnp.bfloat16
    whole = lambda e, *_: (0, 0)
    by_expert = lambda e, *_: (e, 0, 0)
    wide = pl.BlockSpec((1, D, hidden), by_expert)
    tall = pl.BlockSpec((1, hidden, D), by_expert)
    block = pl.BlockSpec((rows, D), whole)
    return pl.pallas_call(
        expert_kernel,
        grid_spec=pltpu.PrefetchScalarGridSpec(
            num_scalar_prefetch=1,
            grid=(E,),
            in_specs=[
                pl.BlockSpec((1, rows), whole),
                pl.BlockSpec((E, D), whole),
                block,
                block,
                wide,
                wide,
                tall,
            ],
            out_specs=[block, block, wide, wide, tall, pl.BlockSpec((E, D), whole)],
            scratch_shapes=[
                pltpu.VMEM((E, rows), jnp.float32),
                pltpu.VMEM((E, rows), jnp.float32),
                pltpu.VMEM((E, rows), jnp.float32),
                pltpu.VMEM((rows, D), jnp.float32),
                pltpu.VMEM((rows, D), jnp.float32),
            ],
        ),
        out_shape=[
            jax.ShapeDtypeStruct((rows, D), low),
            jax.ShapeDtypeStruct((rows, D), low),
            jax.ShapeDtypeStruct((E, D, hidden), low),
            jax.ShapeDtypeStruct((E, D, hidden), low),
            jax.ShapeDtypeStruct((E, hidden, D), low),
            jax.ShapeDtypeStruct((E, D), jnp.float32),
        ],
        compiler_params=pltpu.CompilerParams(
            dimension_semantics=("arbitrary",), vmem_limit_bytes=58 * 2**20
        ),
        cost_estimate=pl.CostEstimate(
            flops=E * CAP * D * (18 * hidden + 8 * rows),
            bytes_accessed=12 * E * D * hidden + 8 * rows * D,
            transcendentals=E * CAP * hidden,
        ),
    )(counts, code, router, second, grad, gate_w, up_w, down_w)


class CubeGather:
    def __init__(self, groups, chunks, block, place, sems):
        self.bits = groups.bit_length() - 2
        self.chunks, self.block, self.place = chunks, block, place
        self.out_sem, self.in_sem, self.pair_out, self.pair_in, self.own_sem = sems
        self.me = lax.axis_index("dp")
        self.waits = []

    def flip(self, index, mask):
        for bit in range(self.bits + 1):
            if mask >> bit & 1:
                index = index + (1 << bit) * (1 - 2 * ((index // (1 << bit)) % 2))
        return index

    def send(self, chunk, have, bit, source):
        slot = have * self.bits + bit
        copy = pltpu.make_async_remote_copy(
            src_ref=source,
            dst_ref=self.place(chunk, self.flip(self.me, have << 1)),
            send_sem=self.out_sem.at[chunk, slot],
            recv_sem=self.in_sem.at[chunk, have ^ (1 << bit)],
            device_id={"dp": self.flip(self.me, 2 << bit)},
            device_id_type=MESH,
        )
        copy.start()
        self.waits.append(copy.wait_send)

    def pair(self, chunk, have, source):
        copy = pltpu.make_async_remote_copy(
            src_ref=source,
            dst_ref=self.place(chunk, self.flip(self.me, have << 1)),
            send_sem=self.pair_out.at[chunk, have],
            recv_sem=self.pair_in.at[chunk, have],
            device_id={"dp": self.flip(self.me, 1)},
            device_id_type=MESH,
        )
        copy.start()
        self.waits.append(copy.wait_send)

    def arrived(self, chunk, have, sem):
        ref = self.place(chunk, self.flip(self.me, have))
        pltpu.make_async_copy(ref, ref, sem).wait()

    def begin(self):
        for chunk in range(self.chunks):
            for step in range(self.bits):
                self.send(chunk, 0, (chunk + step) % self.bits, self.block(chunk))
        for chunk in range(self.chunks):
            self.pair(chunk, 0, self.block(chunk))
            copy = pltpu.make_async_copy(self.block(chunk), self.place(chunk, self.me), self.own_sem.at[chunk])
            copy.start()
            self.waits.append(copy.wait)

    def events(self):
        found = []
        for have in range(1, 1 << self.bits):
            for chunk in range(self.chunks):
                order = [(chunk + step) % self.bits for step in range(self.bits)]
                last = max(step for step, bit in enumerate(order) if have >> bit & 1)
                found.append((bin(have).count("1"), chunk, have, order[last + 1 :]))

        def event(chunk, have, later):
            self.arrived(chunk, have << 1, self.in_sem.at[chunk, have])
            source = self.place(chunk, self.flip(self.me, have << 1))
            for bit in later:
                self.send(chunk, have, bit, source)
            self.pair(chunk, have, source)

        return [functools.partial(event, *item[1:]) for item in sorted(found)]

    def finish(self):
        for chunk in range(self.chunks):
            for have in range(1 << self.bits):
                self.arrived(chunk, (have << 1) + 1, self.pair_in.at[chunk, have])
        for wait in self.waits:
            wait()


def cube_sems(groups, chunks):
    bits = groups.bit_length() - 2
    dma = pltpu.SemaphoreType.DMA
    return [
        dma((chunks, bits << bits)),
        dma((chunks, 1 << bits)),
        dma((chunks, 1 << bits)),
        dma((chunks, 1 << bits)),
        dma((chunks,)),
    ]


class LineGather:
    def __init__(self, parts, chunks, held, out_sem, in_sem):
        self.parts, self.chunks, self.held = parts, chunks, held
        self.out_sem, self.in_sem = out_sem, in_sem
        self.me = lax.axis_index("mp")
        self.rows = held.shape[1] // chunks

    def copy(self, origin, chunk, way):
        piece = self.held.at[origin, pl.ds(chunk * self.rows, self.rows)]
        return pltpu.make_async_remote_copy(
            src_ref=piece,
            dst_ref=piece,
            send_sem=self.out_sem.at[way, origin, chunk],
            recv_sem=self.in_sem.at[origin, chunk],
            device_id={"mp": self.me + 2 * way - 1},
            device_id_type=MESH,
        )

    def on_way(self, way, do):
        pl.when(self.me > 0 if way == 0 else self.me < self.parts - 1)(do)

    def begin(self, chunk):
        for way in (0, 1):
            self.on_way(way, lambda way=way: self.copy(self.me, chunk, way).start())

    def step(self, distance, way, chunk):
        origin = self.me + distance * (1 - 2 * way)

        @pl.when((origin >= 0) & (origin < self.parts))
        def _():
            self.copy(origin, chunk, way).wait_recv()
            self.on_way(way, lambda: self.copy(origin, chunk, way).start())

    def from_side(self, distance, way, do):
        origin = self.me + distance * (1 - 2 * way)
        pl.when((origin >= 0) & (origin < self.parts))(lambda: do(origin))

    def finish(self):
        for way in (0, 1):
            for distance in range(self.parts):
                origin = self.me + distance * (1 - 2 * way)
                here = (origin >= 0) & (origin < self.parts)
                there = (self.me > 0) if way == 0 else (self.me < self.parts - 1)

                @pl.when(here & there)
                def _():
                    for chunk in range(self.chunks):
                        self.copy(origin, chunk, way).wait_send()


class LineSum:
    def __init__(self, parts, chunks, held, come, out_sem, in_sem):
        self.parts, self.chunks, self.held, self.come = parts, chunks, held, come
        self.out_sem, self.in_sem = out_sem, in_sem
        self.me = lax.axis_index("mp")
        self.rows = held.shape[1] // chunks

    def copy(self, target, chunk):
        way = (target > self.me).astype(jnp.int32)
        span = pl.ds(chunk * self.rows, self.rows)
        return pltpu.make_async_remote_copy(
            src_ref=self.held.at[target, span],
            dst_ref=self.come.at[way, target, span],
            send_sem=self.out_sem.at[target, chunk],
            recv_sem=self.in_sem.at[way, target, chunk],
            device_id={"mp": self.me + 2 * way - 1},
            device_id_type=MESH,
        )

    def come_in(self, way, target, chunk):
        piece = self.come.at[way, target, pl.ds(chunk * self.rows, self.rows)]
        pltpu.make_async_copy(piece, piece, self.in_sem.at[way, target, chunk]).wait()

    def begin(self, target):
        end = ((target < self.me) & (self.me == self.parts - 1)) | ((target > self.me) & (self.me == 0))

        @pl.when(end)
        def _():
            for chunk in range(self.chunks):
                self.copy(target, chunk).start()

    def relay(self, target, chunk):
        between = ((target < self.me) & (self.me < self.parts - 1)) | ((target > self.me) & (self.me > 0))

        @pl.when(between)
        def _():
            way = (target > self.me).astype(jnp.int32)
            span = pl.ds(chunk * self.rows, self.rows)
            self.come_in(way, target, chunk)
            self.held[target, span, :] = self.held[target, span, :] + self.come[way, target, span, :]
            self.copy(target, chunk).start()

    def total(self, chunk, out):
        span = pl.ds(chunk * self.rows, self.rows)
        out[span, :] = self.held[self.me, span, :].astype(jnp.float32)
        for way, there in ((0, self.me < self.parts - 1), (1, self.me > 0)):

            @pl.when(there)
            def _():
                self.come_in(way, self.me, chunk)
                out[span, :] = out[span, :] + self.come[way, self.me, span, :].astype(jnp.float32)

    def finish(self):
        for target in range(self.parts):

            @pl.when(self.me != target)
            def _():
                for chunk in range(self.chunks):
                    self.copy(target, chunk).wait_send()


class Exchange:
    def __init__(self, groups, source, held, out_sem, in_sem):
        self.groups, self.source, self.held = groups, source, held
        self.out_sem, self.in_sem = out_sem, in_sem
        self.me = lax.axis_index("dp")
        self.rows = source.shape[0] // groups

    def copy(self, turn):
        peer = lax.rem(self.me + turn, self.groups)
        return pltpu.make_async_remote_copy(
            src_ref=self.source.at[pl.ds(peer * self.rows, self.rows)],
            dst_ref=self.held.at[pl.ds(self.me * self.rows, self.rows)],
            send_sem=self.out_sem.at[turn],
            recv_sem=self.in_sem.at[turn],
            device_id={"dp": peer},
            device_id_type=MESH,
        )

    def begin(self):
        for turn in range(1, self.groups):
            self.copy(turn).start()
        span = pl.ds(pl.multiple_of(self.me * self.rows, self.rows), self.rows)
        self.held[span, :] = self.source[span, :]

    def arrive(self):
        for turn in range(1, self.groups):
            self.copy(turn).wait_recv()

    def finish(self):
        for turn in range(1, self.groups):
            self.copy(turn).wait_send()


def row_type(rows):
    return jnp.bfloat16 if rows % 16 == 0 else jnp.float32


def greet(groups, parts):
    barrier = pltpu.get_barrier_semaphore()
    me, part = lax.axis_index("dp"), lax.axis_index("mp")
    for turn in range(1, groups):
        pl.semaphore_signal(
            barrier, inc=1, device_id={"dp": lax.rem(me + turn, groups)}, device_id_type=MESH
        )
    for step, there in ((-1, part > 0), (1, part < parts - 1)):

        @pl.when(there)
        def _():
            pl.semaphore_signal(barrier, inc=1, device_id={"mp": part + step}, device_id_type=MESH)

    sides = (part > 0).astype(jnp.int32) + (part < parts - 1).astype(jnp.int32)
    pl.semaphore_wait(barrier, groups - 1 + sides)


def scale_of(values):
    return lax.rsqrt(jnp.mean(values * values, axis=1, keepdims=True) + EPS)


def sorting(home, rows):
    place = lax.broadcasted_iota(jnp.int32, (rows, rows), 0)
    return jnp.where(place == home, 1.0, 0.0).astype(jnp.bfloat16)


def bias_of(seg_row, seg_col, start, low, stop):
    span = stop - start
    query = lax.broadcasted_iota(jnp.int32, (span, stop - low), 0) + start
    key = lax.broadcasted_iota(jnp.int32, (span, stop - low), 1) + low
    same = seg_col[start:stop, :] == seg_row[:, low:stop]
    return jnp.where(same & (key <= query), 0.0, -1e30)


def forward_kernel(groups, parts, heads, heads_kv, home, seg_row, seg_col, attn_gain, moe_gain, tokens, out_grad, wpack,
                   middle, first_out, qkv_out, mix_out, weights_out, second_out, grad_out,
                   first, second, grad, weights, qkv, mix, part, come, bias, sorted_second, sorted_grad, dealt_second, dealt_grad,
                   gather_sems, line_out, line_in, sum_out, sum_in, deal_out, deal_in, save_sem):
    low = jnp.bfloat16
    shard, width = tokens.shape
    me, place = lax.axis_index("dp"), lax.axis_index("mp")
    share = heads // heads_kv
    block = wpack.shape[0]
    cut = block // 2
    saves = []

    def save(number, source, target):
        copy = pltpu.make_async_copy(source, target, save_sem.at[number])
        copy.start()
        saves.append(copy)

    greet(groups, parts)
    gather = CubeGather(
        groups,
        2,
        lambda chunk: wpack.at[pl.ds(chunk * cut, cut)],
        lambda chunk, owner: weights.at[pl.ds(owner * block + chunk * cut, cut)],
        gather_sems,
    )
    gather.begin()
    values = tokens[...]
    first[place] = (values * scale_of(values) * attn_gain[...]).astype(low)
    lines = [LineGather(parts, 2, held, line_out.at[n], line_in.at[n]) for n, held in enumerate((first, grad, second))]
    for chunk in range(2):
        lines[0].begin(chunk)
    sort = sorting(home[...], shard)
    sorted_grad[...] = mm(sort, out_grad[...].astype(low)).astype(sorted_grad.dtype)
    for event in gather.events():
        event()
    deal_grad = Exchange(groups, sorted_grad, dealt_grad, deal_out.at[0], deal_in.at[0])
    deal_grad.begin()
    gather.finish()
    save(0, weights, weights_out)

    def project(origin):
        result = mm(first[origin], weights[:, : (heads + 2 * heads_kv) * HD])
        span = pl.ds(pl.multiple_of(origin * shard, shard), shard)
        for head in range(heads + 2 * heads_kv):
            qkv[head, span, :] = result[:, head * HD : (head + 1) * HD].astype(low)

    project(place)
    for distance in range(1, parts):
        for chunk in range(2):
            for way in (0, 1):
                lines[0].step(distance, way, chunk)
        for way in (0, 1):
            lines[0].from_side(distance, way, project)
    deal_grad.arrive()
    grad[place] = dealt_grad[...].astype(low)
    for chunk in range(2):
        lines[1].begin(chunk)
    save(1, first, first_out)
    save(2, qkv, qkv_out)

    sums = LineSum(parts, 2, part, come, sum_out, sum_in)
    order = sorted(range(parts), key=lambda t: (-abs(2 * t - parts + 1), -t))
    reach = -(-512 // shard)
    for number, target in enumerate(order):
        start, stop = target * shard, (target + 1) * shard
        bottom = max(0, target - reach) * shard
        bias[:, : stop - bottom] = bias_of(seg_row, seg_col, start, bottom, stop)

        def attend(head, _):
            group = head // share
            keys = qkv[heads + group, bottom:stop, :]
            scores = mm(qkv[head, start:stop, :], keys, NT) * HD**-0.5 + bias[:, : stop - bottom]
            raised = jnp.exp(scores - jnp.max(scores, axis=1, keepdims=True))
            probs = (raised * (1.0 / jnp.sum(raised, axis=1, keepdims=True))).astype(low)
            mix[head, start:stop, :] = mm(probs, qkv[heads + heads_kv + group, bottom:stop, :]).astype(low)
            return 0

        lax.fori_loop(0, heads, attend, 0)
        flat = jnp.concatenate([mix[head, start:stop, :] for head in range(heads)], axis=1)
        part[target] = mm(flat, weights[:, (heads + 2 * heads_kv) * HD :], NT).astype(low)
        sums.begin(target)
        if number < parts - 1:
            for chunk in range(2):
                for way in (0, 1):
                    lines[1].step(number + 1, way, chunk)
    save(3, mix, mix_out)
    for target in order:
        for chunk in range(2):
            sums.relay(target, chunk)
    for chunk in range(2):
        sums.total(chunk, middle)
    values = tokens[...] + middle[...]
    middle[...] = values
    normed = (values * scale_of(values) * moe_gain[...]).astype(low)
    sorted_second[...] = mm(sort, normed).astype(sorted_second.dtype)
    deal = Exchange(groups, sorted_second, dealt_second, deal_out.at[1], deal_in.at[1])
    deal.begin()
    save(4, grad, grad_out)
    deal.arrive()
    second[place] = dealt_second[...].astype(low)
    for chunk in range(2):
        lines[2].begin(chunk)
    for distance in range(1, parts):
        for chunk in range(2):
            for way in (0, 1):
                lines[2].step(distance, way, chunk)
    save(5, second, second_out)
    for line in lines:
        line.finish()
    sums.finish()
    deal_grad.finish()
    deal.finish()
    for copy in saves:
        copy.wait()


def forward(groups, parts, home, seg, attn_gain, moe_gain, tokens, out_grad, wpack, heads, heads_kv):
    shard, width = tokens.shape
    rows = shard * parts
    low = jnp.bfloat16
    slots = heads + 2 * heads_kv
    columns = wpack.shape[1]
    vmem = pl.BlockSpec(memory_space=pltpu.VMEM)
    hbm = pl.BlockSpec(memory_space=pl.ANY)
    dma = pltpu.SemaphoreType.DMA
    held = lambda: pltpu.VMEM((parts, shard, width), low)
    return pl.pallas_call(
        functools.partial(forward_kernel, groups, parts, heads, heads_kv),
        in_specs=[vmem] * 7 + [hbm],
        out_specs=[vmem] + [hbm] * 6,
        out_shape=[
            jax.ShapeDtypeStruct((shard, width), jnp.float32),
            jax.ShapeDtypeStruct((parts, shard, width), low),
            jax.ShapeDtypeStruct((slots, rows, HD), low),
            jax.ShapeDtypeStruct((heads, rows, HD), low),
            jax.ShapeDtypeStruct((width, columns), low),
            jax.ShapeDtypeStruct((parts, shard, width), low),
            jax.ShapeDtypeStruct((parts, shard, width), low),
        ],
        scratch_shapes=[
            held(),
            held(),
            held(),
            pltpu.VMEM((width, columns), low),
            pltpu.VMEM((slots, rows, HD), low),
            pltpu.VMEM((heads, rows, HD), low),
            held(),
            pltpu.VMEM((2, parts, shard, width), low),
            pltpu.VMEM((shard, shard * (1 - (-512 // shard))), jnp.float32),
            *[pltpu.VMEM((shard, width), row_type(shard // groups))] * 4,
            cube_sems(groups, 2),
            dma((3, 2, parts, 2)),
            dma((3, parts, 2)),
            dma((parts, 2)),
            dma((2, parts, 2)),
            dma((2, groups)),
            dma((2, groups)),
            dma((6,)),
        ],
        compiler_params=pltpu.CompilerParams(
            collective_id=0, has_side_effects=True, vmem_limit_bytes=56 * 2**20
        ),
        cost_estimate=pl.CostEstimate(
            flops=12 * rows * width * columns, bytes_accessed=60 * 2**20, transcendentals=rows * rows * heads
        ),
    )(home, seg[None, :], seg[:, None], attn_gain[None, :], moe_gain[None, :], tokens, out_grad, wpack)


def body(
    tokens,
    attn_gain,
    w_query,
    w_key,
    w_value,
    w_out,
    moe_gain,
    w_router,
    w_gate,
    w_up,
    w_down,
    seq_lengths,
    deal_order,
    expert_ids,
    out_grad,
):
    groups, parts = lax.axis_size("dp"), lax.axis_size("mp")
    rows = tokens.shape[0] * parts
    low_type = jnp.bfloat16
    heads, heads_kv = w_query.shape[1] // HD, w_key.shape[1] // HD
    wpack = jnp.concatenate([w_query, w_key, w_value, w_out.T], axis=1).astype(low_type)
    router_w, gate_w, up_w, down_w = (
        lax.all_gather(w_router.astype(low_type), "dp", axis=0, tiled=True),
        lax.all_gather(w_gate.astype(low_type), "dp", axis=1, tiled=True),
        lax.all_gather(w_up.astype(low_type), "dp", axis=1, tiled=True),
        lax.all_gather(w_down.astype(low_type), "dp", axis=0, tiled=True),
    )
    home, code, counts = deal_tables(deal_order, expert_ids, rows)
    segment = segment_of(seq_lengths[0], rows)
    middle, first_full, qkv, mix, weights, second_full, grad_full = forward(
        groups, parts, home[None, :], segment, attn_gain, moe_gain, tokens, out_grad, wpack, heads, heads_kv
    )
    second_full, grad_full = second_full.reshape(rows, D), grad_full.reshape(rows, D)
    mixed, back, grad_gate_all, grad_up_all, grad_down_all, grad_router = experts(
        second_full, grad_full, code, counts, router_w.T, gate_w, up_w, down_w
    )
    grad_normed_two = to_home(row_share(back), home)
    block_out = middle + to_home(row_share(mixed), home)
    columns = heads * HD
    first_full = first_full.reshape(rows, D)
    query_w, key_w, value_w, out_w = (
        weights[:, :columns],
        weights[:, columns : columns + heads_kv * HD],
        weights[:, columns + heads_kv * HD : columns + 2 * heads_kv * HD],
        weights[:, columns + 2 * heads_kv * HD :].T,
    )
    flat = lambda items: jnp.transpose(items, (1, 0, 2)).reshape(rows, -1)
    query, key, value = flat(qkv[:heads]), flat(qkv[heads : heads + heads_kv]), flat(qkv[heads + heads_kv :])
    mix = flat(mix)
    totals = attend_totals(query, key, segment)
    scale_one = lax.rsqrt(jnp.mean(tokens * tokens, axis=1) + EPS)
    scale_two = lax.rsqrt(jnp.mean(middle * middle, axis=1) + EPS)
    grad_middle_norm, grad_moe_gain = norm_back(middle, moe_gain, scale_two, grad_normed_two)
    grad_middle = out_grad + grad_middle_norm
    grad_attn_full = full_rows(grad_middle.astype(low_type))
    grad_mix = jnp.einsum(
        "td,hd->th", grad_attn_full, out_w, preferred_element_type=jnp.float32
    ).astype(low_type)
    grad_out_w = jnp.einsum("th,td->hd", mix, grad_attn_full, preferred_element_type=jnp.float32)
    grad_query, grad_key, grad_value = attend_back(query, key, value, segment, grad_mix, totals)
    grad_first = jnp.einsum("th,dh->td", grad_query, query_w, preferred_element_type=jnp.float32)
    grad_first = grad_first + jnp.einsum(
        "th,dh->td", grad_key, key_w, preferred_element_type=jnp.float32
    )
    grad_first = grad_first + jnp.einsum(
        "th,dh->td", grad_value, value_w, preferred_element_type=jnp.float32
    )
    grad_query_w = jnp.einsum(
        "td,th->dh", first_full, grad_query, preferred_element_type=jnp.float32
    )
    grad_key_w = jnp.einsum("td,th->dh", first_full, grad_key, preferred_element_type=jnp.float32)
    grad_value_w = jnp.einsum(
        "td,th->dh", first_full, grad_value, preferred_element_type=jnp.float32
    )
    grad_tokens_norm, grad_attn_gain = norm_back(
        tokens, attn_gain, scale_one, row_share(grad_first.astype(low_type)).astype(jnp.float32)
    )
    tokens_grad = grad_middle + grad_tokens_norm
    attn_gain_sum, moe_gain_sum, router_total = lax.psum(
        (grad_attn_gain, grad_moe_gain, grad_router), ("dp", "mp")
    )
    width = w_router.shape[0]
    router_sum = lax.dynamic_slice_in_dim(router_total, lax.axis_index("dp") * width, width, 1).T
    query_sum, key_sum, value_sum, out_sum, gate_sum, up_sum, down_sum = (
        lax.psum_scatter(
            grad_query_w.astype(jnp.bfloat16), "dp", scatter_dimension=0, tiled=True
        ).astype(jnp.float32),
        lax.psum_scatter(
            grad_key_w.astype(jnp.bfloat16), "dp", scatter_dimension=0, tiled=True
        ).astype(jnp.float32),
        lax.psum_scatter(
            grad_value_w.astype(jnp.bfloat16), "dp", scatter_dimension=0, tiled=True
        ).astype(jnp.float32),
        lax.psum_scatter(
            grad_out_w.astype(jnp.bfloat16), "dp", scatter_dimension=1, tiled=True
        ).astype(jnp.float32),
        lax.psum_scatter(
            grad_gate_all.astype(jnp.bfloat16), "dp", scatter_dimension=1, tiled=True
        ).astype(jnp.float32),
        lax.psum_scatter(
            grad_up_all.astype(jnp.bfloat16), "dp", scatter_dimension=1, tiled=True
        ).astype(jnp.float32),
        lax.psum_scatter(
            grad_down_all.astype(jnp.bfloat16), "dp", scatter_dimension=0, tiled=True
        ).astype(jnp.float32),
    )
    return (
        block_out,
        tokens_grad,
        attn_gain_sum,
        query_sum,
        key_sum,
        value_sum,
        out_sum,
        moe_gain_sum,
        router_sum,
        gate_sum,
        up_sum,
        down_sum,
    )


def solution(mesh):
    return jax.shard_map(
        body,
        mesh=mesh,
        in_specs=(
            P(("dp", "mp"), None),
            P(),
            P("dp", "mp"),
            P("dp", "mp"),
            P("dp", "mp"),
            P("mp", "dp"),
            P(),
            P("dp", None),
            P(None, "dp", "mp"),
            P(None, "dp", "mp"),
            P("dp", "mp", None),
            P("dp", None),
            P(),
            P("dp", None),
            P(("dp", "mp"), None),
        ),
        out_specs=(
            P(("dp", "mp"), None),
            P(("dp", "mp"), None),
            P(),
            P("dp", "mp"),
            P("dp", "mp"),
            P("dp", "mp"),
            P("mp", "dp"),
            P(),
            P("dp", None),
            P(None, "dp", "mp"),
            P(None, "dp", "mp"),
            P("dp", "mp", None),
        ),
        check_vma=False,
    )
```

```python
import functools

import jax
import jax.numpy as jnp
from jax import lax
from jax.experimental import pallas as pl
from jax.experimental.pallas import tpu as pltpu
from jax.sharding import PartitionSpec as P

D = 1536
HD = 64
E = 16
CAP = 256
MESH = pl.DeviceIdType.MESH


EPS = 1e-05


def deal_tables(deal_order, expert_ids, block):
    groups = lax.axis_size("dp")
    parts = lax.axis_size("mp")
    me_index = lax.axis_index("dp")
    part_index = lax.axis_index("mp")
    shard = block // parts
    own = (me_index * parts + part_index) * shard + jnp.arange(shard, dtype=jnp.int32)
    spots = jnp.arange(deal_order.shape[0], dtype=jnp.int32)
    dealt = jnp.sum(jnp.where(deal_order[:, None] == own[None, :], spots[:, None], 0), axis=0)
    home = jnp.sum((dealt[:, None] < dealt[None, :]).astype(jnp.int32), axis=0)
    mine = lax.dynamic_slice_in_dim(deal_order, me_index * block, block, 0)
    anchor = (mine % block) // shard * groups + mine // block
    key = anchor * block + jnp.arange(block, dtype=jnp.int32)
    arrival = jnp.sum((key[:, None] < key[None, :]).astype(jnp.int32), axis=0)
    pair = expert_ids[:, 0] * E + expert_ids[:, 1]
    hits = arrival[:, None] == jnp.arange(block, dtype=jnp.int32)[None, :]
    code = jnp.sum(jnp.where(hits, pair[:, None], 0), axis=0)
    counts = jnp.sum((expert_ids.reshape(-1)[:, None] == jnp.arange(E, dtype=jnp.int32)[None, :]).astype(jnp.int32), axis=0)
    return (home, code[None, :], counts)


def segment_of(lengths, rows):
    ends = jnp.cumsum(lengths)
    places = jnp.arange(rows, dtype=jnp.int32)
    return jnp.sum((places[:, None] >= ends[None, :]).astype(jnp.int32), axis=1)


def mm(a, b, dims=((1,), (0,))):
    return lax.dot_general(a, b, (dims, ((), ())), preferred_element_type=jnp.float32)


NT = ((1,), (1,))
TN = ((0,), (0,))


def expert_step(width, e, refs):
    (second, grad, gate_w, up_w, down_w, gate_out, up_out, down_out, rank, gates, dots, mixed, back) = refs
    rows = second.shape[0]
    low = jnp.bfloat16
    place = lax.broadcasted_iota(jnp.int32, (width, rows), 0).astype(jnp.float32)
    hit = place == rank[pl.ds(e, 1), :]
    pick = jnp.where(hit, 1.0, 0.0).astype(low)
    gate = jnp.sum(jnp.where(hit, gates[pl.ds(e, 1), :], 0.0), axis=1, keepdims=True)
    x = mm(pick, second[...]).astype(low)
    grad_rows = mm(pick, grad[...])
    gate_part = mm(x, gate_w[0])
    up_part = mm(x, up_w[0])
    sigma = jax.nn.sigmoid(gate_part)
    hidden = (gate_part * sigma * up_part).astype(low)
    each = mm(hidden, down_w[0])
    dot = jnp.sum(grad_rows * each, axis=1, keepdims=True)
    dots[pl.ds(e, 1), :] = jnp.sum(jnp.where(hit, dot, 0.0), axis=0, keepdims=True)
    mixed[...] += mm(pick, (each * gate).astype(low), TN)
    grad_each = (grad_rows * gate).astype(low)
    grad_hidden = mm(grad_each, down_w[0], NT)
    grad_gate = (grad_hidden * up_part * sigma * (1.0 + gate_part * (1.0 - sigma))).astype(low)
    grad_up = (grad_hidden * gate_part * sigma).astype(low)
    down_grad = mm(hidden, grad_each, TN).astype(low)
    high, wide = down_grad.shape
    subs, span = down_out.shape[2], high // 4 // down_out.shape[2]
    for chunk in range(4):
        for sub in range(subs):
            row = (chunk * subs + sub) * span
            for column in range(wide // high):
                down_out[0, chunk, sub, column * span : (column + 1) * span, :] = down_grad[
                    row : row + span, column * high : (column + 1) * high
                ]
    gate_out[0] = mm(x, grad_gate, TN).astype(low)
    up_out[0] = mm(x, grad_up, TN).astype(low)
    back_rows = mm(grad_gate, gate_w[0], NT) + mm(grad_up, up_w[0], NT)
    back[...] += mm(pick, back_rows.astype(low), TN)


def expert_kernel(counts, code, router, second, grad, gate_w, up_w, down_w,
                  mixed_out, back_out, gate_out, up_out, down_out, router_out,
                  rank, gates, dots, mixed, back):
    e = pl.program_id(0)
    rows = second.shape[0]
    low = jnp.bfloat16
    expert = lax.broadcasted_iota(jnp.int32, (E, rows), 0)
    first_id = code[...] // E
    second_id = code[...] % E
    picks = [jnp.where(expert == ids, 1.0, 0.0) for ids in (first_id, second_id)]

    @pl.when(e == 0)
    def _():
        logits = mm(router[...], second[...], NT)
        chosen = [jnp.sum(pick * logits, axis=0, keepdims=True) for pick in picks]
        top = jnp.maximum(chosen[0], chosen[1])
        raised = [jnp.exp(value - top) for value in chosen]
        total = raised[0] + raised[1]
        gates[...] = picks[0] * (raised[0] / total) + picks[1] * (raised[1] / total)
        hits = picks[0] + picks[1]
        earlier = lax.broadcasted_iota(jnp.int32, (rows, rows), 0) < lax.broadcasted_iota(
            jnp.int32, (rows, rows), 1
        )
        before = mm(hits.astype(low), jnp.where(earlier, 1.0, 0.0).astype(low))
        rank[...] = jnp.where(hits > 0.0, before, -1.0)
        mixed[...] = jnp.zeros_like(mixed)
        back[...] = jnp.zeros_like(back)

    refs = (second, grad, gate_w, up_w, down_w, gate_out, up_out, down_out, rank, gates, dots, mixed, back)
    count = counts[e]

    @pl.when(count <= CAP // 2)
    def _():
        expert_step(CAP // 2, e, refs)

    @pl.when(count > CAP // 2)
    def _():
        expert_step(CAP, e, refs)

    @pl.when(e == E - 1)
    def _():
        grad_gates = [jnp.sum(pick * dots[...], axis=0, keepdims=True) for pick in picks]
        own = [jnp.sum(pick * gates[...], axis=0, keepdims=True) for pick in picks]
        inner = own[0] * grad_gates[0] + own[1] * grad_gates[1]
        grad_logits = picks[0] * (own[0] * (grad_gates[0] - inner)) + picks[1] * (
            own[1] * (grad_gates[1] - inner)
        )
        grad_logits = grad_logits.astype(low)
        router_grad = mm(grad_logits, second[...])
        for owner in range(router_out.shape[0]):
            span = router_out.shape[2]
            router_out[owner] = router_grad[:, owner * span : (owner + 1) * span]
        mixed_out[...] = mixed[...].astype(low)
        back_out[...] = (back[...] + mm(grad_logits, router[...], TN)).astype(low)


def experts(groups, second, grad, code, counts, router, gate_w, up_w, down_w):
    per = E // groups
    rows = second.shape[0]
    hidden = gate_w.shape[2]
    low = jnp.bfloat16
    whole = lambda e, *_: (0, 0)
    by_expert = lambda e, *_: (e, 0, 0)
    wide = pl.BlockSpec((1, D, hidden), by_expert)
    tall = pl.BlockSpec((1, hidden, D), by_expert)
    block = pl.BlockSpec((rows, D), whole)
    return pl.pallas_call(
        expert_kernel,
        grid_spec=pltpu.PrefetchScalarGridSpec(
            num_scalar_prefetch=1,
            grid=(E,),
            in_specs=[
                pl.BlockSpec((1, rows), whole),
                pl.BlockSpec((E, D), whole),
                block,
                block,
                wide,
                wide,
                tall,
            ],
            out_specs=[
                block,
                block,
                wide,
                wide,
                pl.BlockSpec((1, 4, 4 // per, D // groups, hidden), lambda e, *_: (e // per, 0, e % per, 0, 0)),
                pl.BlockSpec((groups, E, D // groups), lambda e, *_: (0, 0, 0)),
            ],
            scratch_shapes=[
                pltpu.VMEM((E, rows), jnp.float32),
                pltpu.VMEM((E, rows), jnp.float32),
                pltpu.VMEM((E, rows), jnp.float32),
                pltpu.VMEM((rows, D), jnp.float32),
                pltpu.VMEM((rows, D), jnp.float32),
            ],
        ),
        out_shape=[
            jax.ShapeDtypeStruct((rows, D), low),
            jax.ShapeDtypeStruct((rows, D), low),
            jax.ShapeDtypeStruct((E, D, hidden), low),
            jax.ShapeDtypeStruct((E, D, hidden), low),
            jax.ShapeDtypeStruct((groups, 4, 4, D // groups, hidden), low),
            jax.ShapeDtypeStruct((groups, E, D // groups), jnp.float32),
        ],
        compiler_params=pltpu.CompilerParams(
            dimension_semantics=("arbitrary",), vmem_limit_bytes=58 * 2**20
        ),
        cost_estimate=pl.CostEstimate(
            flops=E * CAP * D * (18 * hidden + 8 * rows),
            bytes_accessed=12 * E * D * hidden + 8 * rows * D,
            transcendentals=E * CAP * hidden,
        ),
    )(counts, code, router, second, grad, gate_w, up_w, down_w)


class CubeGather:
    def __init__(self, groups, chunks, block, place, sems):
        self.bits = groups.bit_length() - 2
        self.chunks, self.block, self.place = chunks, block, place
        self.out_sem, self.in_sem, self.pair_out, self.pair_in, self.own_sem = sems
        self.me = lax.axis_index("dp")
        self.waits = []

    def flip(self, index, mask):
        for bit in range(self.bits + 1):
            if mask >> bit & 1:
                index = index + (1 << bit) * (1 - 2 * ((index // (1 << bit)) % 2))
        return index

    def send(self, chunk, have, bit, source):
        slot = have * self.bits + bit
        copy = pltpu.make_async_remote_copy(
            src_ref=source,
            dst_ref=self.place(chunk, self.flip(self.me, have << 1)),
            send_sem=self.out_sem.at[chunk, slot],
            recv_sem=self.in_sem.at[chunk, have ^ (1 << bit)],
            device_id={"dp": self.flip(self.me, 2 << bit)},
            device_id_type=MESH,
        )
        copy.start()
        self.waits.append(copy.wait_send)

    def pair(self, chunk, have, source):
        copy = pltpu.make_async_remote_copy(
            src_ref=source,
            dst_ref=self.place(chunk, self.flip(self.me, have << 1)),
            send_sem=self.pair_out.at[chunk, have],
            recv_sem=self.pair_in.at[chunk, have],
            device_id={"dp": self.flip(self.me, 1)},
            device_id_type=MESH,
        )
        copy.start()
        self.waits.append(copy.wait_send)

    def arrived(self, chunk, have, sem):
        ref = self.place(chunk, self.flip(self.me, have))
        pltpu.make_async_copy(ref, ref, sem).wait()

    def begin(self):
        for chunk in range(self.chunks):
            for step in range(self.bits):
                self.send(chunk, 0, (chunk + step) % self.bits, self.block(chunk))
        for chunk in range(self.chunks):
            self.pair(chunk, 0, self.block(chunk))
            copy = pltpu.make_async_copy(self.block(chunk), self.place(chunk, self.me), self.own_sem.at[chunk])
            copy.start()
            self.waits.append(copy.wait)

    def events(self):
        found = []
        for have in range(1, 1 << self.bits):
            for chunk in range(self.chunks):
                order = [(chunk + step) % self.bits for step in range(self.bits)]
                last = max(step for step, bit in enumerate(order) if have >> bit & 1)
                found.append((bin(have).count("1"), chunk, have, order[last + 1 :]))

        def event(chunk, have, later):
            self.arrived(chunk, have << 1, self.in_sem.at[chunk, have])
            source = self.place(chunk, self.flip(self.me, have << 1))
            for bit in later:
                self.send(chunk, have, bit, source)
            self.pair(chunk, have, source)

        return [functools.partial(event, *item[1:]) for item in sorted(found)]

    def finish(self):
        for chunk in range(self.chunks):
            for have in range(1 << self.bits):
                self.arrived(chunk, (have << 1) + 1, self.pair_in.at[chunk, have])
        for wait in self.waits:
            wait()


def cube_sems(groups, chunks):
    bits = groups.bit_length() - 2
    dma = pltpu.SemaphoreType.DMA
    return [
        dma((chunks, bits << bits)),
        dma((chunks, 1 << bits)),
        dma((chunks, 1 << bits)),
        dma((chunks, 1 << bits)),
        dma((chunks,)),
    ]


class LineGather:
    def __init__(self, parts, chunks, held, out_sem, in_sem):
        self.parts, self.chunks, self.held = parts, chunks, held
        self.out_sem, self.in_sem = out_sem, in_sem
        self.me = lax.axis_index("mp")
        self.rows = held.shape[1] // chunks

    def copy(self, origin, chunk, way):
        piece = self.held.at[origin, pl.ds(chunk * self.rows, self.rows)]
        return pltpu.make_async_remote_copy(
            src_ref=piece,
            dst_ref=piece,
            send_sem=self.out_sem.at[way, origin, chunk],
            recv_sem=self.in_sem.at[origin, chunk],
            device_id={"mp": self.me + 2 * way - 1},
            device_id_type=MESH,
        )

    def on_way(self, way, do):
        pl.when(self.me > 0 if way == 0 else self.me < self.parts - 1)(do)

    def begin(self, chunk):
        for way in (0, 1):
            self.on_way(way, lambda way=way: self.copy(self.me, chunk, way).start())

    def step(self, distance, way, chunk):
        origin = self.me + distance * (1 - 2 * way)

        @pl.when((origin >= 0) & (origin < self.parts))
        def _():
            self.copy(origin, chunk, way).wait_recv()
            self.on_way(way, lambda: self.copy(origin, chunk, way).start())

    def from_side(self, distance, way, do):
        origin = self.me + distance * (1 - 2 * way)
        pl.when((origin >= 0) & (origin < self.parts))(lambda: do(origin))

    def finish(self):
        for way in (0, 1):
            for distance in range(self.parts):
                origin = self.me + distance * (1 - 2 * way)
                here = (origin >= 0) & (origin < self.parts)
                there = (self.me > 0) if way == 0 else (self.me < self.parts - 1)

                @pl.when(here & there)
                def _():
                    for chunk in range(self.chunks):
                        self.copy(origin, chunk, way).wait_send()


class LineSum:
    def __init__(self, parts, chunks, held, come, out_sem, in_sem):
        self.parts, self.chunks, self.held, self.come = parts, chunks, held, come
        self.out_sem, self.in_sem = out_sem, in_sem
        self.me = lax.axis_index("mp")
        self.rows = held.shape[1] // chunks

    def slot(self, way, target, device):
        return target + (self.parts - target) * ((target == device) & (way == 0)).astype(jnp.int32)

    def copy(self, target, chunk):
        way = (target > self.me).astype(jnp.int32)
        slot = self.slot(way, target, self.me + 2 * way - 1)
        span = pl.ds(chunk * self.rows, self.rows)
        return pltpu.make_async_remote_copy(
            src_ref=self.held.at[target, span],
            dst_ref=self.come.at[slot, span],
            send_sem=self.out_sem.at[target, chunk],
            recv_sem=self.in_sem.at[slot, chunk],
            device_id={"mp": self.me + 2 * way - 1},
            device_id_type=MESH,
        )

    def come_in(self, slot, chunk):
        piece = self.come.at[slot, pl.ds(chunk * self.rows, self.rows)]
        pltpu.make_async_copy(piece, piece, self.in_sem.at[slot, chunk]).wait()

    def turned(self, target):
        right = (2 * self.me >= self.parts).astype(jnp.int32)
        return target + right * (self.parts - 1 - 2 * target)

    def begin(self, target):
        end = ((target < self.me) & (self.me == self.parts - 1)) | ((target > self.me) & (self.me == 0))

        @pl.when(end)
        def _():
            for chunk in range(self.chunks):
                self.copy(target, chunk).start()

    def relay(self, target, chunk):
        between = ((target < self.me) & (self.me < self.parts - 1)) | ((target > self.me) & (self.me > 0))

        @pl.when(between)
        def _():
            span = pl.ds(chunk * self.rows, self.rows)
            self.come_in(target, chunk)
            self.held[target, span, :] = self.held[target, span, :] + self.come[target, span, :]
            self.copy(target, chunk).start()

    def total(self, chunk, out):
        span = pl.ds(chunk * self.rows, self.rows)
        out[span, :] = self.held[self.me, span, :].astype(jnp.float32)
        for slot, there in ((self.parts, self.me < self.parts - 1), (self.me, self.me > 0)):

            @pl.when(there)
            def _():
                self.come_in(slot, chunk)
                out[span, :] = out[span, :] + self.come[slot, span, :].astype(jnp.float32)

    def finish(self):
        for target in range(self.parts):

            @pl.when(self.me != target)
            def _():
                for chunk in range(self.chunks):
                    self.copy(target, chunk).wait_send()


class Exchange:
    def __init__(self, groups, source, held, out_sem, in_sem):
        self.groups, self.source, self.held = groups, source, held
        self.out_sem, self.in_sem = out_sem, in_sem
        self.me = lax.axis_index("dp")
        self.rows = source.shape[0] // groups

    def copy(self, turn):
        peer = lax.rem(self.me + turn, self.groups)
        return pltpu.make_async_remote_copy(
            src_ref=self.source.at[pl.ds(peer * self.rows, self.rows)],
            dst_ref=self.held.at[pl.ds(self.me * self.rows, self.rows)],
            send_sem=self.out_sem.at[turn],
            recv_sem=self.in_sem.at[turn],
            device_id={"dp": peer},
            device_id_type=MESH,
        )

    def begin(self):
        for turn in range(1, self.groups):
            self.copy(turn).start()
        span = pl.ds(pl.multiple_of(self.me * self.rows, self.rows), self.rows)
        self.held[span, :] = self.source[span, :]

    def arrive(self):
        for turn in range(1, self.groups):
            self.copy(turn).wait_recv()

    def finish(self):
        for turn in range(1, self.groups):
            self.copy(turn).wait_send()


def row_type(rows):
    return jnp.bfloat16 if rows % 16 == 0 else jnp.float32


def greet(groups, parts):
    barrier = pltpu.get_barrier_semaphore()
    for axis, size in (("dp", groups), ("mp", parts)):
        for turn in range(1, size):
            peer = lax.rem(lax.axis_index(axis) + turn, size)
            pl.semaphore_signal(barrier, inc=1, device_id={axis: peer}, device_id_type=MESH)
    pl.semaphore_wait(barrier, groups + parts - 2)


def far_first(parts):
    return sorted(range(parts), key=lambda t: (-abs(2 * t - parts + 1), -t))


def scale_of(values):
    return lax.rsqrt(jnp.mean(values * values, axis=1, keepdims=True) + EPS)


def sorting(home, rows):
    place = lax.broadcasted_iota(jnp.int32, (rows, rows), 0)
    return jnp.where(place == home, 1.0, 0.0).astype(jnp.bfloat16)


def bias_of(seg_row, seg_col, start, low, stop):
    span = stop - start
    query = lax.broadcasted_iota(jnp.int32, (span, stop - low), 0) + start
    key = lax.broadcasted_iota(jnp.int32, (span, stop - low), 1) + low
    same = seg_col[start:stop, :] == seg_row[:, low:stop]
    return jnp.where(same & (key <= query), 0.0, -1e30)


def forward_kernel(groups, parts, heads, heads_kv, home, seg_row, seg_col, attn_gain, moe_gain, tokens, out_grad, wpack,
                   middle, first_out, qkv_out, mix_out, weights_out, second_out, grad_out,
                   first, second, grad, weights, qkv, mix, part, come, bias, sorted_second, sorted_grad, dealt_second, dealt_grad,
                   gather_sems, line_out, line_in, sum_out, sum_in, deal_out, deal_in, save_sem):
    low = jnp.bfloat16
    shard, width = tokens.shape
    me, place = lax.axis_index("dp"), lax.axis_index("mp")
    share = heads // heads_kv
    block = wpack.shape[0]
    cut = block // 2
    saves = []

    def save(number, source, target):
        copy = pltpu.make_async_copy(source, target, save_sem.at[number])
        copy.start()
        saves.append(copy)

    greet(groups, parts)
    gather = CubeGather(
        groups,
        2,
        lambda chunk: wpack.at[pl.ds(chunk * cut, cut)],
        lambda chunk, owner: weights.at[pl.ds(owner * block + chunk * cut, cut)],
        gather_sems,
    )
    gather.begin()
    values = tokens[...]
    first[place] = (values * scale_of(values) * attn_gain[...]).astype(low)
    lines = [LineGather(parts, 2, held, line_out.at[n], line_in.at[n]) for n, held in enumerate((first, grad, second))]
    for chunk in range(2):
        lines[0].begin(chunk)
    sort = sorting(home[...], shard)
    sorted_grad[...] = mm(sort, out_grad[...].astype(low)).astype(sorted_grad.dtype)
    for event in gather.events():
        event()
    deal_grad = Exchange(groups, sorted_grad, dealt_grad, deal_out.at[0], deal_in.at[0])
    deal_grad.begin()
    gather.finish()
    save(0, weights, weights_out)

    def project(origin):
        result = mm(first[origin], weights[:, : (heads + 2 * heads_kv) * HD])
        span = pl.ds(pl.multiple_of(origin * shard, shard), shard)
        for head in range(heads + 2 * heads_kv):
            qkv[head, span, :] = result[:, head * HD : (head + 1) * HD].astype(low)

    project(place)
    for distance in range(1, parts):
        for chunk in range(2):
            for way in (0, 1):
                lines[0].step(distance, way, chunk)
        for way in (0, 1):
            lines[0].from_side(distance, way, project)
    deal_grad.arrive()
    grad[place] = dealt_grad[...].astype(low)
    for chunk in range(2):
        lines[1].begin(chunk)
    save(1, first, first_out)
    save(2, qkv, qkv_out)

    sums = LineSum(parts, 2, part, come, sum_out, sum_in)
    order = far_first(parts)
    reach = -(-512 // shard)
    for number, target in enumerate(order):
        start, stop = target * shard, (target + 1) * shard
        bottom = max(0, target - reach) * shard
        bias[:, : stop - bottom] = bias_of(seg_row, seg_col, start, bottom, stop)

        def attend(head, _):
            group = head // share
            keys = qkv[heads + group, bottom:stop, :]
            scores = mm(qkv[head, start:stop, :], keys, NT) * HD**-0.5 + bias[:, : stop - bottom]
            raised = jnp.exp(scores - jnp.max(scores, axis=1, keepdims=True))
            probs = (raised * (1.0 / jnp.sum(raised, axis=1, keepdims=True))).astype(low)
            mix[head, start:stop, :] = mm(probs, qkv[heads + heads_kv + group, bottom:stop, :]).astype(low)
            return 0

        lax.fori_loop(0, heads, attend, 0)
        flat = jnp.concatenate([mix[head, start:stop, :] for head in range(heads)], axis=1)
        part[target] = mm(flat, weights[:, (heads + 2 * heads_kv) * HD :], NT).astype(low)
        sums.begin(target)
        if number < parts - 1:
            for chunk in range(2):
                for way in (0, 1):
                    lines[1].step(number + 1, way, chunk)
    save(3, mix, mix_out)
    for target in order:
        for chunk in range(2):
            sums.relay(sums.turned(target), chunk)
    for chunk in range(2):
        sums.total(chunk, middle)
    values = tokens[...] + middle[...]
    middle[...] = values
    normed = (values * scale_of(values) * moe_gain[...]).astype(low)
    sorted_second[...] = mm(sort, normed).astype(sorted_second.dtype)
    deal = Exchange(groups, sorted_second, dealt_second, deal_out.at[1], deal_in.at[1])
    deal.begin()
    save(4, grad, grad_out)
    deal.arrive()
    second[place] = dealt_second[...].astype(low)
    for chunk in range(2):
        lines[2].begin(chunk)
    for distance in range(1, parts):
        for chunk in range(2):
            for way in (0, 1):
                lines[2].step(distance, way, chunk)
    save(5, second, second_out)
    for line in lines:
        line.finish()
    sums.finish()
    deal_grad.finish()
    deal.finish()
    for copy in saves:
        copy.wait()


def forward(groups, parts, home, seg, attn_gain, moe_gain, tokens, out_grad, wpack, heads, heads_kv):
    shard, width = tokens.shape
    rows = shard * parts
    low = jnp.bfloat16
    slots = heads + 2 * heads_kv
    columns = wpack.shape[1]
    vmem = pl.BlockSpec(memory_space=pltpu.VMEM)
    hbm = pl.BlockSpec(memory_space=pl.ANY)
    dma = pltpu.SemaphoreType.DMA
    held = lambda: pltpu.VMEM((parts, shard, width), low)
    return pl.pallas_call(
        functools.partial(forward_kernel, groups, parts, heads, heads_kv),
        in_specs=[vmem] * 7 + [hbm],
        out_specs=[vmem] + [hbm] * 6,
        out_shape=[
            jax.ShapeDtypeStruct((shard, width), jnp.float32),
            jax.ShapeDtypeStruct((parts, shard, width), low),
            jax.ShapeDtypeStruct((slots, rows, HD), low),
            jax.ShapeDtypeStruct((heads, rows, HD), low),
            jax.ShapeDtypeStruct((width, columns), low),
            jax.ShapeDtypeStruct((parts, shard, width), low),
            jax.ShapeDtypeStruct((parts, shard, width), low),
        ],
        scratch_shapes=[
            held(),
            held(),
            held(),
            pltpu.VMEM((width, columns), low),
            pltpu.VMEM((slots, rows, HD), low),
            pltpu.VMEM((heads, rows, HD), low),
            held(),
            pltpu.VMEM((parts + 1, shard, width), low),
            pltpu.VMEM((shard, shard * (1 - (-512 // shard))), jnp.float32),
            *[pltpu.VMEM((shard, width), row_type(shard // groups))] * 4,
            cube_sems(groups, 2),
            dma((3, 2, parts, 2)),
            dma((3, parts, 2)),
            dma((parts, 2)),
            dma((parts + 1, 2)),
            dma((2, groups)),
            dma((2, groups)),
            dma((6,)),
        ],
        compiler_params=pltpu.CompilerParams(
            collective_id=0, has_side_effects=True, vmem_limit_bytes=56 * 2**20
        ),
        cost_estimate=pl.CostEstimate(
            flops=12 * rows * width * columns, bytes_accessed=60 * 2**20, transcendentals=rows * rows * heads
        ),
    )(home, seg[None, :], seg[:, None], attn_gain[None, :], moe_gain[None, :], tokens, out_grad, wpack)


class CubeSum:
    def __init__(self, groups, chunks, own, pair_held, step_held, sems):
        self.bits = groups.bit_length() - 2
        self.chunks, self.own, self.pair_held, self.step_held = chunks, own, pair_held, step_held
        self.out_sem, self.in_sem, self.pair_out, self.pair_in = sems
        self.me = lax.axis_index("dp")
        self.waits = []

    def flip(self, index, mask):
        for bit in range(self.bits + 1):
            if mask >> bit & 1:
                index = index + (1 << bit) * (1 - 2 * ((index // (1 << bit)) % 2))
        return index

    def step_of(self, chunk, want):
        for step in range(self.bits):
            bit = (chunk + step) % self.bits
            if want >> bit & 1:
                return step, bit
        return self.bits, None

    def pair(self, chunk):
        for want in range(1 << self.bits):
            copy = pltpu.make_async_remote_copy(
                src_ref=self.own(chunk, self.flip(self.me, 2 * want + 1)),
                dst_ref=self.pair_held(chunk, want),
                send_sem=self.pair_out.at[chunk, want],
                recv_sem=self.pair_in.at[chunk, want],
                device_id={"dp": self.flip(self.me, 1)},
                device_id_type=MESH,
            )
            copy.start()
            self.waits.append(copy.wait_send)

    def send(self, chunk, want, source):
        step, bit = self.step_of(chunk, want)
        rest = want ^ (1 << bit)
        copy = pltpu.make_async_remote_copy(
            src_ref=source,
            dst_ref=self.step_held(chunk, step, rest),
            send_sem=self.out_sem.at[chunk, want],
            recv_sem=self.in_sem.at[chunk, step, rest],
            device_id={"dp": self.flip(self.me, 2 << bit)},
            device_id_type=MESH,
        )
        copy.start()
        return copy.wait_send

    def terms(self, chunk, want):
        found = [self.own(chunk, self.flip(self.me, 2 * want)), self.pair_held(chunk, want)]
        pltpu.make_async_copy(found[1], found[1], self.pair_in.at[chunk, want]).wait()
        for step in range(self.step_of(chunk, want)[0]):
            held = self.step_held(chunk, step, want)
            pltpu.make_async_copy(held, held, self.in_sem.at[chunk, step, want]).wait()
            found.append(held)
        return found

    def items(self, lag):
        found = []
        for chunk in range(self.chunks):
            for want in range(1 << self.bits):
                step = self.step_of(chunk, want)[0]
                found.append((chunk + lag * step, step, chunk, want))
        return [item[2:] for item in sorted(found)]

    def finish(self):
        for wait in self.waits:
            wait()


def sum_sems(groups, chunks):
    bits = groups.bit_length() - 2
    dma = pltpu.SemaphoreType.DMA
    return [
        dma((chunks, 1 << bits)),
        dma((chunks, bits, 1 << bits)),
        dma((chunks, 1 << bits)),
        dma((chunks, 1 << bits)),
    ]


class Stream:
    def __init__(self, cube, lag, terms, sums, totals, out, load_sem, save_sem):
        self.cube, self.terms, self.sums, self.totals, self.out = cube, terms, sums, totals, out
        self.load_sem, self.save_sem = load_sem, save_sem
        self.list = cube.items(lag)
        self.at, self.sent, self.saved, self.loads = 0, [], [], None

    def tick(self, times=1):
        for _ in range(times):
            if self.at <= len(self.list):
                loads = self.fetch(self.at) if self.at < len(self.list) else None
                if self.loads is not None:
                    self.add(self.at - 1)
                self.loads = loads
                self.at += 1

    def fetch(self, number):
        slot = number % 2
        loads = []
        for term, ref in enumerate(self.cube.terms(*self.list[number])):
            copy = pltpu.make_async_copy(ref, self.terms.at[slot, term], self.load_sem.at[slot, term])
            copy.start()
            loads.append(copy)
        return loads

    def add(self, number):
        slot = number % 2
        chunk, want = self.list[number]
        for copy in self.loads:
            copy.wait()
        count = len(self.loads)
        if want:
            place = len(self.sent) % self.sums.shape[0]
            if len(self.sent) >= self.sums.shape[0]:
                self.sent[len(self.sent) - self.sums.shape[0]]()
            target = self.sums.at[place]
        else:
            place = len(self.saved) % self.totals.shape[0]
            if len(self.saved) >= self.totals.shape[0]:
                self.saved[len(self.saved) - self.totals.shape[0]]()
            target = self.totals.at[place]

        def row(index, _):
            total = self.terms[slot, 0, index].astype(jnp.float32)
            for term in range(1, count):
                total = total + self.terms[slot, term, index].astype(jnp.float32)
            target[index] = total.astype(target.dtype)
            return 0

        lax.fori_loop(0, target.shape[0], row, 0)
        if want:
            self.sent.append(self.cube.send(chunk, want, target))
        else:
            copy = pltpu.make_async_copy(target, self.out(chunk), self.save_sem.at[place])
            copy.start()
            self.saved.append(copy.wait)

    def finish(self):
        self.tick(len(self.list) + 1 - self.at)
        for wait in self.sent[-self.sums.shape[0] :] + self.saved[-self.totals.shape[0] :]:
            wait()


class Share:
    def __init__(self, axis, size, held, out_sem, in_sem, source):
        self.axis, self.size, self.held = axis, size, held
        self.out_sem, self.in_sem, self.source = out_sem, in_sem, source
        self.me = lax.axis_index(axis)

    def copy(self, turn):
        peer = lax.rem(self.me + turn, self.size)
        return pltpu.make_async_remote_copy(
            src_ref=self.source(peer),
            dst_ref=self.held.at[self.me],
            send_sem=self.out_sem.at[turn],
            recv_sem=self.in_sem.at[turn],
            device_id={self.axis: peer},
            device_id_type=MESH,
        )

    def begin(self):
        for turn in range(1, self.size):
            self.copy(turn).start()
        self.held[self.me] = self.source(self.me)[...]

    def total(self):
        for turn in range(1, self.size):
            self.copy(turn).wait()
        total = self.held[0]
        for index in range(1, self.size):
            total = total + self.held[index]
        return total


def backward_kernel(groups, parts, heads, heads_kv, home, seg_row, seg_col, attn_gain, moe_gain, tokens, out_grad, middle,
                    router_part, back_in, mixed_in, first_in, qkv_in, mix_in, weights_in, gate_in, up_in, down_in,
                    block_out, tokens_grad, gains_out, router_out, pack_out, gate_out, up_out, down_out, pair_held, step_held,
                    held, come, mixed, mixed_come, grad, qkv, mix, weights, grad_mix, grad_query, grad_key, grad_value,
                    flat, bias, pack, pack_pair, pack_step, stage, land_back, land_mixed, terms, sums, totals,
                    router_all, router_line, gains, gains_line, gains_all,
                    load_sem, cube_sems, pack_sems, term_sem, save_sem, line_out, line_in, sum_out, sum_in, deal_out, deal_in,
                    share_out, share_in):
    low = jnp.bfloat16
    shard, width = tokens.shape
    me, place = lax.axis_index("dp"), lax.axis_index("mp")
    share = heads // heads_kv
    slots = heads + 2 * heads_kv
    bits = groups.bit_length() - 2
    arrays = ((back_in, held), (weights_in, weights), (mix_in, mix), (qkv_in, qkv), (mixed_in, mixed))
    loads = []
    for number, (source, target) in enumerate(arrays):
        loads.append(pltpu.make_async_copy(source, target, load_sem.at[number]))
        loads[-1].start()
    greet(groups, parts)

    gains[...] = jnp.zeros_like(gains)
    count = gate_in.shape[0] // 4
    owner_rows = width // groups

    def own(chunk, owner):
        if chunk < 2 * count:
            ref = (gate_in, up_in)[chunk // count]
            return ref.at[pl.ds(chunk % count * 4, 4), pl.ds(owner * owner_rows, owner_rows)]
        return down_in.at[owner, chunk - 2 * count]

    places = {}

    def step_place(chunk, step, want):
        return step_held.at[chunk, places.setdefault((chunk, step, want), len([k for k in places if k[0] == chunk]))]

    cube = CubeSum(groups, 3 * count, own, lambda chunk, want: pair_held.at[chunk, want], step_place, cube_sems)
    out = lambda chunk: (gate_out, up_out, down_out)[chunk // count].at[chunk % count]
    stream = Stream(cube, 3, terms, sums, totals, out, term_sem, save_sem)

    back = LineSum(parts, 2, held, come, sum_out.at[0], sum_in.at[0])
    loads[0].wait()
    order = far_first(parts)
    for target in order:
        back.begin(back.turned(target))
    for chunk in range(3 * count):
        cube.pair(chunk)
    routers = Share("dp", groups, router_all, share_out.at[0], share_in.at[0], lambda peer: router_part.at[peer])
    routers.begin()
    stream.tick(3)
    for target in order:
        for chunk in range(2):
            back.relay(back.turned(target), chunk)
            stream.tick(2 if target != order[-1] else 0)
    for chunk in range(2):
        back.total(chunk, block_out)
    stage[...] = block_out[...].astype(stage.dtype)
    deal = Exchange(groups, stage, land_back, deal_out.at[0], deal_in.at[0])
    deal.begin()
    back.finish()
    loads[4].wait()
    extra = LineSum(parts, 2, mixed, mixed_come, sum_out.at[1], sum_in.at[1])
    for target in order:
        extra.begin(extra.turned(target))
    router_line[place] = routers.total()
    router_sums = Share("mp", parts, router_line, share_out.at[1], share_in.at[1], lambda peer: router_line.at[place])
    for turn in range(1, parts):
        router_sums.copy(turn).start()
    sort = sorting(home[...], shard)
    values = middle[...]
    scale = scale_of(values)
    deal.arrive()
    grad_second = mm(sort, land_back[...].astype(low), TN)
    weighted = grad_second * moe_gain[...]
    inner = jnp.mean(weighted * values, axis=1, keepdims=True)
    gains[0:1, :] = jnp.sum(grad_second * values * scale, axis=0, keepdims=True)
    grad_middle = out_grad[...] + (scale * weighted - values * (scale * scale * scale * inner))
    tokens_grad[...] = grad_middle
    grad[place] = grad_middle.astype(low)
    line = LineGather(parts, 2, grad, line_out, line_in)
    for chunk in range(2):
        line.begin(chunk)
    loads[1].wait()
    loads[2].wait()

    def mix_back(origin):
        result = mm(grad[origin], weights[:, slots * HD :])
        span = pl.ds(pl.multiple_of(origin * shard, shard), shard)
        for head in range(heads):
            grad_mix[head, span, :] = result[:, head * HD : (head + 1) * HD].astype(low)

    mix_back(place)
    stream.tick(2)
    for distance in range(1, parts):
        for chunk in range(2):
            for way in (0, 1):
                line.step(distance, way, chunk)
            extra.relay(extra.turned(order[distance - 1]), chunk)
            stream.tick(3)
        for way in (0, 1):
            line.from_side(distance, way, mix_back)
    for chunk in range(2):
        extra.relay(extra.turned(order[parts - 1]), chunk)
    mix_flat = jnp.concatenate([mix[head] for head in range(heads)], axis=1)
    pack[:, slots * HD :] = mm(grad[...].reshape(parts * shard, width), mix_flat, TN).astype(low)
    deal.finish()
    for chunk in range(2):
        extra.total(chunk, block_out)
    stage[...] = block_out[...].astype(stage.dtype)
    deal_mixed = Exchange(groups, stage, land_mixed, deal_out.at[1], deal_in.at[1])
    deal_mixed.begin()
    loads[3].wait()
    extra.finish()
    first_load = pltpu.make_async_copy(first_in, mixed, load_sem.at[5])
    first_load.start()
    stream.tick(2)

    first_sum = LineSum(parts, 2, held, come, sum_out.at[2], sum_in.at[2])
    grad_key[...] = jnp.zeros_like(grad_key)
    grad_value[...] = jnp.zeros_like(grad_value)
    reach = -(-512 // shard)
    for target in reversed(range(parts)):
        start, stop = target * shard, (target + 1) * shard
        bottom = max(0, target - reach) * shard
        bias[:, : stop - bottom] = bias_of(seg_row, seg_col, start, bottom, stop)

        def attend(head, _):
            group = head // share
            query = qkv[head, start:stop, :]
            keys = qkv[heads + group, bottom:stop, :]
            scores = mm(query, keys, NT) * HD**-0.5 + bias[:, : stop - bottom]
            raised = jnp.exp(scores - jnp.max(scores, axis=1, keepdims=True))
            probs = raised * (1.0 / jnp.sum(raised, axis=1, keepdims=True))
            grad_rows = grad_mix[head, start:stop, :]
            grad_probs = mm(grad_rows, qkv[heads + heads_kv + group, bottom:stop, :], NT)
            inner = jnp.sum(probs * grad_probs, axis=1, keepdims=True)
            grad_scores = (probs * (grad_probs - inner)).astype(low)
            grad_query[head, start:stop, :] = (mm(grad_scores, keys) * HD**-0.5).astype(low)
            grad_key[group, bottom:stop, :] += mm(grad_scores, query, TN)
            grad_value[group, bottom:stop, :] += mm(probs.astype(low), grad_rows, TN)
            return 0

        lax.fori_loop(0, heads, attend, 0)
        pieces = [grad_query[head, start:stop, :] for head in range(heads)]
        pieces += [(grad_key[group, start:stop, :] * HD**-0.5).astype(low) for group in range(heads_kv)]
        pieces += [grad_value[group, start:stop, :].astype(low) for group in range(heads_kv)]
        flat[start:stop, :] = jnp.concatenate(pieces, axis=1)
        held[target] = mm(flat[start:stop, :], weights[:, : slots * HD], NT).astype(low)
        first_sum.begin(target)
        stream.tick(2)
    first_load.wait()
    pack[:, : slots * HD] = mm(mixed[...].reshape(parts * shard, width), flat[...], TN).astype(low)
    cut = owner_rows // 2
    pack_places = {}

    def pack_place(chunk, step, want):
        return pack_step.at[chunk, pack_places.setdefault((chunk, step, want), len([k for k in pack_places if k[0] == chunk]))]

    pack_cube = CubeSum(
        groups,
        2,
        lambda chunk, owner: pack.at[pl.ds(owner * owner_rows + chunk * cut, cut)],
        lambda chunk, want: pack_pair.at[chunk, want],
        pack_place,
        pack_sems,
    )
    for chunk in range(2):
        pack_cube.pair(chunk)
    for target in reversed(range(parts)):
        for chunk in range(2):
            first_sum.relay(target, chunk)
        stream.tick(2)
    pack_sent = []
    for chunk, want in pack_cube.items(1):
        refs = pack_cube.terms(chunk, want)
        total = refs[0][...].astype(jnp.float32)
        for ref in refs[1:]:
            total = total + ref[...].astype(jnp.float32)
        if want:
            refs[0][...] = total.astype(low)
            pack_sent.append(pack_cube.send(chunk, want, refs[0]))
        else:
            pack_out[chunk * cut : (chunk + 1) * cut, :] = total
    for chunk in range(2):
        first_sum.total(chunk, block_out)
    grad_first = block_out[...]
    values = tokens[...]
    scale = scale_of(values)
    weighted = grad_first * attn_gain[...]
    inner = jnp.mean(weighted * values, axis=1, keepdims=True)
    gains[1:2, :] = jnp.sum(grad_first * values * scale, axis=0, keepdims=True)
    gains_lines = Share("mp", parts, gains_line, share_out.at[2], share_in.at[2], lambda peer: gains)
    gains_lines.begin()
    tokens_grad[...] += scale * weighted - values * (scale * scale * scale * inner)
    deal_mixed.arrive()
    block_out[...] = middle[...] + mm(sort, land_mixed[...].astype(low), TN)
    router_out[...] = router_sums.total()
    gains[...] = gains_lines.total()
    gains_rest = Share("dp", groups, gains_all, share_out.at[3], share_in.at[3], lambda peer: gains)
    gains_rest.begin()
    stream.finish()
    gains_out[...] = gains_rest.total()
    line.finish()
    first_sum.finish()
    deal_mixed.finish()
    cube.finish()
    pack_cube.finish()
    for wait in pack_sent:
        wait()


def backward(groups, parts, heads, heads_kv, home, seg, attn_gain, moe_gain, tokens, out_grad, middle, router_part,
             back, mixed, first, qkv, mix, weights, gate_grad, up_grad, down_grad):
    shard, width = tokens.shape
    rows = shard * parts
    low = jnp.bfloat16
    slots = heads + 2 * heads_kv
    columns = weights.shape[1]
    owner_rows, hidden = width // groups, gate_grad.shape[2]
    bits = groups.bit_length() - 2
    chunks = 3 * (E // 4)
    cut = owner_rows // 2
    vmem = pl.BlockSpec(memory_space=pltpu.VMEM)
    hbm = pl.BlockSpec(memory_space=pl.ANY)
    dma = pltpu.SemaphoreType.DMA
    f32 = lambda *shape: jax.ShapeDtypeStruct(shape, jnp.float32)
    unit = (4, owner_rows, hidden)
    held = pltpu.VMEM((parts, shard, width), low)
    come = pltpu.VMEM((parts + 1, shard, width), low)
    line = row_type(shard // groups)
    return pl.pallas_call(
        functools.partial(backward_kernel, groups, parts, heads, heads_kv),
        in_specs=[vmem] * 9 + [hbm] * 9,
        out_specs=[vmem] * 5 + [hbm] * 5,
        out_shape=[
            f32(shard, width),
            f32(shard, width),
            f32(8, width),
            f32(E, owner_rows),
            f32(owner_rows, columns),
            f32(E // 4, *unit),
            f32(E // 4, *unit),
            f32(E // 4, *unit),
            jax.ShapeDtypeStruct((chunks, 1 << bits, *unit), low),
            jax.ShapeDtypeStruct((chunks, (1 << bits) - 1, *unit), low),
        ],
        scratch_shapes=[
            held,
            come,
            held,
            come,
            held,
            pltpu.VMEM((slots, rows, HD), low),
            pltpu.VMEM((heads, rows, HD), low),
            pltpu.VMEM((width, columns), low),
            pltpu.VMEM((heads, rows, HD), low),
            pltpu.VMEM((heads, rows, HD), low),
            pltpu.VMEM((heads_kv, rows, HD), jnp.float32),
            pltpu.VMEM((heads_kv, rows, HD), jnp.float32),
            pltpu.VMEM((rows, slots * HD), low),
            pltpu.VMEM((shard, shard * (1 - (-512 // shard))), jnp.float32),
            pltpu.VMEM((width, columns), low),
            pltpu.VMEM((2, 1 << bits, cut, columns), low),
            pltpu.VMEM((2, (1 << bits) - 1, cut, columns), low),
            pltpu.VMEM((shard, width), line),
            pltpu.VMEM((shard, width), line),
            pltpu.VMEM((shard, width), line),
            pltpu.VMEM((2, 2 + bits, *unit), low),
            pltpu.VMEM((4, *unit), low),
            pltpu.VMEM((2, *unit), jnp.float32),
            pltpu.VMEM((groups, E, owner_rows), jnp.float32),
            pltpu.VMEM((parts, E, owner_rows), jnp.float32),
            pltpu.VMEM((8, width), jnp.float32),
            pltpu.VMEM((parts, 8, width), jnp.float32),
            pltpu.VMEM((groups, 8, width), jnp.float32),
            dma((6,)),
            sum_sems(groups, chunks),
            sum_sems(groups, 2),
            dma((2, 2 + bits)),
            dma((2,)),
            dma((2, parts, 2)),
            dma((parts, 2)),
            dma((3, parts, 2)),
            dma((3, parts + 1, 2)),
            dma((2, groups)),
            dma((2, groups)),
            dma((4, max(groups, parts))),
            dma((4, max(groups, parts))),
        ],
        compiler_params=pltpu.CompilerParams(
            collective_id=1, has_side_effects=True, vmem_limit_bytes=63 * 2**20
        ),
        cost_estimate=pl.CostEstimate(
            flops=24 * rows * width * columns, bytes_accessed=200 * 2**20, transcendentals=rows * rows * heads
        ),
    )(home, seg[None, :], seg[:, None], attn_gain[None, :], moe_gain[None, :], tokens, out_grad, middle, router_part,
      back, mixed, first, qkv, mix, weights, gate_grad, up_grad, down_grad)


def body(
    tokens,
    attn_gain,
    w_query,
    w_key,
    w_value,
    w_out,
    moe_gain,
    w_router,
    w_gate,
    w_up,
    w_down,
    seq_lengths,
    deal_order,
    expert_ids,
    out_grad,
):
    groups, parts = lax.axis_size("dp"), lax.axis_size("mp")
    rows = tokens.shape[0] * parts
    low_type = jnp.bfloat16
    heads, heads_kv = w_query.shape[1] // HD, w_key.shape[1] // HD
    wpack = jnp.concatenate([w_query, w_key, w_value, w_out.T], axis=1).astype(low_type)
    router_w, gate_w, up_w, down_w = (
        lax.all_gather(w_router.astype(low_type), "dp", axis=0, tiled=True),
        lax.all_gather(w_gate.astype(low_type), "dp", axis=1, tiled=True),
        lax.all_gather(w_up.astype(low_type), "dp", axis=1, tiled=True),
        lax.all_gather(w_down.astype(low_type), "dp", axis=0, tiled=True),
    )
    home, code, counts = deal_tables(deal_order, expert_ids, rows)
    segment = segment_of(seq_lengths[0], rows)
    middle, first_full, qkv, mix, weights, second_full, grad_full = forward(
        groups, parts, home[None, :], segment, attn_gain, moe_gain, tokens, out_grad, wpack, heads, heads_kv
    )
    mixed, back, gate_grad, up_grad, down_grad, router_part = experts(
        groups,
        second_full.reshape(rows, D),
        grad_full.reshape(rows, D),
        code,
        counts,
        router_w.T,
        gate_w,
        up_w,
        down_w,
    )
    block_out, tokens_grad, gains, router_sum, pack_sum, gate_sum, up_sum, down_sum, _, _ = backward(
        groups,
        parts,
        heads,
        heads_kv,
        home[None, :],
        segment,
        attn_gain,
        moe_gain,
        tokens,
        out_grad,
        middle,
        router_part,
        back.reshape(second_full.shape),
        mixed.reshape(second_full.shape),
        first_full,
        qkv,
        mix,
        weights,
        gate_grad,
        up_grad,
        down_grad,
    )
    per, hidden = w_down.shape[:2]
    subs = 4 // per
    down_sum = down_sum.reshape(4, per, subs, D // hidden, hidden // 4 // subs, hidden)
    down_sum = jnp.transpose(down_sum, (1, 0, 2, 4, 3, 5))
    columns, columns_kv = heads * HD, heads_kv * HD
    return (
        block_out,
        tokens_grad,
        gains[1],
        pack_sum[:, :columns],
        pack_sum[:, columns : columns + columns_kv],
        pack_sum[:, columns + columns_kv : columns + 2 * columns_kv],
        pack_sum[:, columns + 2 * columns_kv :].T,
        gains[0],
        router_sum.T,
        gate_sum.reshape(w_gate.shape),
        up_sum.reshape(w_up.shape),
        down_sum.reshape(w_down.shape),
    )


def solution(mesh):
    return jax.shard_map(
        body,
        mesh=mesh,
        in_specs=(
            P(("dp", "mp"), None),
            P(),
            P("dp", "mp"),
            P("dp", "mp"),
            P("dp", "mp"),
            P("mp", "dp"),
            P(),
            P("dp", None),
            P(None, "dp", "mp"),
            P(None, "dp", "mp"),
            P("dp", "mp", None),
            P("dp", None),
            P(),
            P("dp", None),
            P(("dp", "mp"), None),
        ),
        out_specs=(
            P(("dp", "mp"), None),
            P(("dp", "mp"), None),
            P(),
            P("dp", "mp"),
            P("dp", "mp"),
            P("dp", "mp"),
            P("mp", "dp"),
            P(),
            P("dp", None),
            P(None, "dp", "mp"),
            P(None, "dp", "mp"),
            P("dp", "mp", None),
        ),
        check_vma=False,
    )
```

```python
import functools

import jax
import jax.numpy as jnp
from jax import lax
from jax.experimental import pallas as pl
from jax.experimental.pallas import tpu as pltpu
from jax.sharding import PartitionSpec as P

D = 1536
HD = 64
E = 16
CAP = 256
CUTS = 4
MESH = pl.DeviceIdType.MESH


EPS = 1e-05


def deal_tables(deal_order, expert_ids, block):
    groups = lax.axis_size("dp")
    parts = lax.axis_size("mp")
    me_index = lax.axis_index("dp")
    part_index = lax.axis_index("mp")
    shard = block // parts
    own = (me_index * parts + part_index) * shard + jnp.arange(shard, dtype=jnp.int32)
    spots = jnp.arange(deal_order.shape[0], dtype=jnp.int32)
    dealt = jnp.sum(jnp.where(deal_order[:, None] == own[None, :], spots[:, None], 0), axis=0)
    home = jnp.sum((dealt[:, None] < dealt[None, :]).astype(jnp.int32), axis=0)
    mine = lax.dynamic_slice_in_dim(deal_order, me_index * block, block, 0)
    anchor = (mine % block) // shard * groups + mine // block
    key = anchor * block + jnp.arange(block, dtype=jnp.int32)
    arrival = jnp.sum((key[:, None] < key[None, :]).astype(jnp.int32), axis=0)
    pair = expert_ids[:, 0] * E + expert_ids[:, 1]
    hits = arrival[:, None] == jnp.arange(block, dtype=jnp.int32)[None, :]
    code = jnp.sum(jnp.where(hits, pair[:, None], 0), axis=0)
    counts = jnp.sum((expert_ids.reshape(-1)[:, None] == jnp.arange(E, dtype=jnp.int32)[None, :]).astype(jnp.int32), axis=0)
    return (home, code[None, :], counts)


def segment_of(lengths, rows):
    ends = jnp.cumsum(lengths)
    places = jnp.arange(rows, dtype=jnp.int32)
    return jnp.sum((places[:, None] >= ends[None, :]).astype(jnp.int32), axis=1)


def mm(a, b, dims=((1,), (0,))):
    return lax.dot_general(a, b, (dims, ((), ())), preferred_element_type=jnp.float32)


NT = ((1,), (1,))
TN = ((0,), (0,))


def expert_step(width, start, count, refs):
    (x_all, grad_all, gate_all, dots, gate_w, up_w, down_w, gate_out, up_out, down_out) = refs
    low = jnp.bfloat16
    span = pl.ds(start, width)
    valid = lax.broadcasted_iota(jnp.int32, (width, 1), 0) < count
    gate = jnp.where(valid, gate_all[span, :], 0.0)
    x = x_all[span, :]
    grad_rows = grad_all[span, :]
    gate_part = mm(x, gate_w[0])
    up_part = mm(x, up_w[0])
    sigma = jax.nn.sigmoid(gate_part)
    hidden = (gate_part * sigma * up_part).astype(low)
    each = mm(hidden, down_w[0])
    grad_rows_wide = grad_rows.astype(jnp.float32)
    dots[span, :] = jnp.sum(grad_rows_wide * each, axis=1, keepdims=True)
    grad_each = (grad_rows_wide * gate).astype(low)
    grad_all[span, :] = jnp.where(valid, (each * gate).astype(low), grad_rows)
    grad_hidden = mm(grad_each, down_w[0], NT)
    grad_gate = (grad_hidden * up_part * sigma * (1.0 + gate_part * (1.0 - sigma))).astype(low)
    grad_up = (grad_hidden * gate_part * sigma).astype(low)
    down_grad = mm(hidden, grad_each, TN).astype(low)
    high, wide = down_grad.shape
    subs, rows = down_out.shape[2], high // 4 // down_out.shape[2]
    for chunk in range(4):
        for sub in range(subs):
            row = (chunk * subs + sub) * rows
            for column in range(wide // high):
                down_out[0, chunk, sub, column * rows : (column + 1) * rows, :] = down_grad[
                    row : row + rows, column * high : (column + 1) * high
                ]
    gate_out[0] = mm(x, grad_gate, TN).astype(low)
    up_out[0] = mm(x, grad_up, TN).astype(low)
    back_rows = mm(grad_gate, gate_w[0], NT) + mm(grad_up, up_w[0], NT)
    x_all[span, :] = jnp.where(valid, back_rows.astype(low), x)


def expert_kernel(counts, starts, code, base, router, second, grad, gate_w, up_w, down_w,
                  mixed_out, back_out, gate_out, up_out, down_out, router_out,
                  slot, gates, x_all, grad_all, gate_all, dots):
    e = pl.program_id(0)
    rows = second.shape[0]
    low = jnp.bfloat16
    tile = CAP
    tiles = x_all.shape[0] // tile - 1
    expert = lax.broadcasted_iota(jnp.int32, (E, rows), 0)
    picks = [jnp.where(expert == ids, 1.0, 0.0) for ids in (code[...] // E, code[...] % E)]
    own = lambda pick, values: jnp.sum(pick * values, axis=0, keepdims=True)

    @pl.when(e == 0)
    def _():
        logits = mm(router[...], second[...], NT)
        chosen = [own(pick, logits) for pick in picks]
        top = jnp.maximum(chosen[0], chosen[1])
        raised = [jnp.exp(value - top) for value in chosen]
        total = raised[0] + raised[1]
        earlier = lax.broadcasted_iota(jnp.int32, (rows, rows), 0) < lax.broadcasted_iota(
            jnp.int32, (rows, rows), 1
        )
        before = mm((picks[0] + picks[1]).astype(low), jnp.where(earlier, 1.0, 0.0).astype(low)) + base[...]
        for k in (0, 1):
            gates[k : k + 1, :] = raised[k] / total
            slot[k : k + 1, :] = own(picks[k], before)

        def pick_tile(number, _):
            span = pl.ds(pl.multiple_of(number * tile, tile), tile)
            place = (lax.broadcasted_iota(jnp.int32, (tile, rows), 0) + number * tile).astype(jnp.float32)
            hits = [place == slot[k : k + 1, :] for k in (0, 1)]
            pick = jnp.where(hits[0] | hits[1], 1.0, 0.0).astype(low)
            scaled = jnp.where(hits[0], gates[0:1, :], 0.0) + jnp.where(hits[1], gates[1:2, :], 0.0)
            gate_all[span, :] = jnp.sum(scaled, axis=1, keepdims=True)
            x_all[span, :] = mm(pick, second[...]).astype(low)
            grad_all[span, :] = mm(pick, grad[...]).astype(low)
            return 0

        lax.fori_loop(0, tiles, pick_tile, 0)
        x_all[tiles * tile :, :] = jnp.zeros((tile, D), low)
        grad_all[tiles * tile :, :] = jnp.zeros((tile, D), low)
        gate_all[tiles * tile :, :] = jnp.zeros((tile, 1), jnp.float32)

    refs = (x_all, grad_all, gate_all, dots, gate_w, up_w, down_w, gate_out, up_out, down_out)
    count = counts[e]
    start = pl.multiple_of(starts[e], 16)
    widths = (CAP // 2, CAP)
    for less, width in zip((-1,) + widths, widths):

        @pl.when((count > less) & (count <= width))
        def _(width=width):
            expert_step(width, start, count, refs)

    @pl.when(e == E - 1)
    def _():
        def dots_tile(number, totals):
            span = pl.ds(pl.multiple_of(number * tile, tile), tile)
            place = (lax.broadcasted_iota(jnp.int32, (tile, rows), 0) + number * tile).astype(jnp.float32)
            return tuple(
                totals[k] + jnp.sum(jnp.where(place == slot[k : k + 1, :], dots[span, :], 0.0), axis=0, keepdims=True)
                for k in (0, 1)
            )

        zero = jnp.zeros((1, rows), jnp.float32)
        grad_gates = lax.fori_loop(0, tiles, dots_tile, (zero, zero))
        shares = [gates[k : k + 1, :] for k in (0, 1)]
        inner = shares[0] * grad_gates[0] + shares[1] * grad_gates[1]
        grad_logits = picks[0] * (shares[0] * (grad_gates[0] - inner)) + picks[1] * (
            shares[1] * (grad_gates[1] - inner)
        )
        router_grad = mm(grad_logits.astype(low), second[...])
        for owner in range(router_out.shape[0]):
            span = router_out.shape[2]
            router_out[owner] = router_grad[:, owner * span : (owner + 1) * span]
        columns = jnp.transpose(jnp.concatenate([slot[...], grad_logits], axis=0))
        block = rows // 4
        place = lax.broadcasted_iota(jnp.int32, (block, tiles * tile), 1).astype(jnp.float32)
        for number in range(4):
            part = columns[number * block : (number + 1) * block, :]
            hit = (place == part[:, 0:1]) | (place == part[:, 1:2])
            put = jnp.where(hit, 1.0, 0.0).astype(low)
            span = pl.ds(number * block, block)
            mixed_out[span, :] = mm(put, grad_all[: tiles * tile, :]).astype(low)
            routed = mm(part[:, 8:].astype(low), router[...])
            back_out[span, :] = (mm(put, x_all[: tiles * tile, :]) + routed).astype(low)


def experts(groups, second, grad, code, counts, router, gate_w, up_w, down_w):
    per = E // groups
    rows = second.shape[0]
    hidden = gate_w.shape[2]
    low = jnp.bfloat16
    taken = (counts + 15) // 16 * 16
    starts = jnp.cumsum(taken) - taken
    packed = -(-(2 * rows + 16 * E) // CAP) * CAP + CAP
    whole = lambda e, *_: (0, 0)
    by_expert = lambda e, *_: (e, 0, 0)
    wide = pl.BlockSpec((1, D, hidden), by_expert)
    tall = pl.BlockSpec((1, hidden, D), by_expert)
    block = pl.BlockSpec((rows, D), whole, pipeline_mode=pl.Buffered(1))
    out = pl.BlockSpec((rows, D), whole)
    return pl.pallas_call(
        expert_kernel,
        grid_spec=pltpu.PrefetchScalarGridSpec(
            num_scalar_prefetch=2,
            grid=(E,),
            in_specs=[
                pl.BlockSpec((1, rows), whole),
                pl.BlockSpec((E, 1), whole),
                pl.BlockSpec((E, D), whole),
                block,
                block,
                wide,
                wide,
                tall,
            ],
            out_specs=[
                out,
                out,
                wide,
                wide,
                pl.BlockSpec((1, 4, 4 // per, D // groups, hidden), lambda e, *_: (e // per, 0, e % per, 0, 0)),
                pl.BlockSpec((groups, E, D // groups), lambda e, *_: (0, 0, 0)),
            ],
            scratch_shapes=[
                pltpu.VMEM((8, rows), jnp.float32),
                pltpu.VMEM((8, rows), jnp.float32),
                pltpu.VMEM((packed, D), low),
                pltpu.VMEM((packed, D), low),
                pltpu.VMEM((packed, 1), jnp.float32),
                pltpu.VMEM((packed, 1), jnp.float32),
            ],
        ),
        out_shape=[
            jax.ShapeDtypeStruct((rows, D), low),
            jax.ShapeDtypeStruct((rows, D), low),
            jax.ShapeDtypeStruct((E, D, hidden), low),
            jax.ShapeDtypeStruct((E, D, hidden), low),
            jax.ShapeDtypeStruct((groups, 4, 4, D // groups, hidden), low),
            jax.ShapeDtypeStruct((groups, E, D // groups), jnp.float32),
        ],
        compiler_params=pltpu.CompilerParams(
            dimension_semantics=("arbitrary",), vmem_limit_bytes=58 * 2**20
        ),
        cost_estimate=pl.CostEstimate(
            flops=2 * rows * D * (18 * hidden + 8 * rows),
            bytes_accessed=12 * E * D * hidden + 8 * rows * D,
            transcendentals=2 * rows * hidden,
        ),
    )(counts, starts, code, starts.astype(jnp.float32)[:, None], router, second, grad, gate_w, up_w, down_w)


class CubeGather:
    def __init__(self, groups, chunks, block, place, sems):
        self.bits = groups.bit_length() - 2
        self.chunks, self.block, self.place = chunks, block, place
        self.out_sem, self.in_sem, self.pair_out, self.pair_in, self.own_sem = sems
        self.me = lax.axis_index("dp")
        self.waits = []

    def flip(self, index, mask):
        for bit in range(self.bits + 1):
            if mask >> bit & 1:
                index = index + (1 << bit) * (1 - 2 * ((index // (1 << bit)) % 2))
        return index

    def send(self, chunk, have, bit, source):
        slot = have * self.bits + bit
        copy = pltpu.make_async_remote_copy(
            src_ref=source,
            dst_ref=self.place(chunk, self.flip(self.me, have << 1)),
            send_sem=self.out_sem.at[chunk, slot],
            recv_sem=self.in_sem.at[chunk, have ^ (1 << bit)],
            device_id={"dp": self.flip(self.me, 2 << bit)},
            device_id_type=MESH,
        )
        copy.start()
        self.waits.append(copy.wait_send)

    def pair(self, chunk, have, source):
        copy = pltpu.make_async_remote_copy(
            src_ref=source,
            dst_ref=self.place(chunk, self.flip(self.me, have << 1)),
            send_sem=self.pair_out.at[chunk, have],
            recv_sem=self.pair_in.at[chunk, have],
            device_id={"dp": self.flip(self.me, 1)},
            device_id_type=MESH,
        )
        copy.start()
        self.waits.append(copy.wait_send)

    def arrived(self, chunk, have, sem):
        ref = self.place(chunk, self.flip(self.me, have))
        pltpu.make_async_copy(ref, ref, sem).wait()

    def begin(self, chunk):
        for step in range(self.bits):
            self.send(chunk, 0, (chunk + step) % self.bits, self.block(chunk))
        self.pair(chunk, 0, self.block(chunk))
        copy = pltpu.make_async_copy(self.block(chunk), self.place(chunk, self.me), self.own_sem.at[chunk])
        copy.start()
        self.waits.append(copy.wait)

    def events(self):
        found = []
        for have in range(1, 1 << self.bits):
            for chunk in range(self.chunks):
                order = [(chunk + step) % self.bits for step in range(self.bits)]
                last = max(step for step, bit in enumerate(order) if have >> bit & 1)
                found.append((bin(have).count("1"), chunk, have, order[last + 1 :]))

        def event(chunk, have, later):
            self.arrived(chunk, have << 1, self.in_sem.at[chunk, have])
            source = self.place(chunk, self.flip(self.me, have << 1))
            for bit in later:
                self.send(chunk, have, bit, source)
            self.pair(chunk, have, source)

        return [functools.partial(event, *item[1:]) for item in sorted(found)]

    def finish(self):
        for chunk in range(self.chunks):
            for have in range(1 << self.bits):
                self.arrived(chunk, (have << 1) + 1, self.pair_in.at[chunk, have])
        for wait in self.waits:
            wait()


def cube_sems(groups, chunks):
    bits = groups.bit_length() - 2
    dma = pltpu.SemaphoreType.DMA
    return [
        dma((chunks, bits << bits)),
        dma((chunks, 1 << bits)),
        dma((chunks, 1 << bits)),
        dma((chunks, 1 << bits)),
        dma((chunks,)),
    ]


class LineGather:
    def __init__(self, parts, chunks, held, out_sem, in_sem):
        self.parts, self.chunks, self.held = parts, chunks, held
        self.out_sem, self.in_sem = out_sem, in_sem
        self.me = lax.axis_index("mp")
        self.rows = held.shape[1] // chunks

    def copy(self, origin, chunk, way):
        piece = self.held.at[origin, pl.ds(chunk * self.rows, self.rows)]
        return pltpu.make_async_remote_copy(
            src_ref=piece,
            dst_ref=piece,
            send_sem=self.out_sem.at[way, origin, chunk],
            recv_sem=self.in_sem.at[origin, chunk],
            device_id={"mp": self.me + 2 * way - 1},
            device_id_type=MESH,
        )

    def on_way(self, way, do):
        pl.when(self.me > 0 if way == 0 else self.me < self.parts - 1)(do)

    def begin(self, chunk):
        for way in (0, 1):
            self.on_way(way, lambda way=way: self.copy(self.me, chunk, way).start())

    def step(self, distance, way, chunk):
        origin = self.me + distance * (1 - 2 * way)

        @pl.when((origin >= 0) & (origin < self.parts))
        def _():
            self.copy(origin, chunk, way).wait_recv()
            self.on_way(way, lambda: self.copy(origin, chunk, way).start())

    def from_side(self, distance, way, do):
        origin = self.me + distance * (1 - 2 * way)
        pl.when((origin >= 0) & (origin < self.parts))(lambda: do(origin))

    def finish(self):
        for way in (0, 1):
            for distance in range(self.parts):
                origin = self.me + distance * (1 - 2 * way)
                here = (origin >= 0) & (origin < self.parts)
                there = (self.me > 0) if way == 0 else (self.me < self.parts - 1)

                @pl.when(here & there)
                def _():
                    for chunk in range(self.chunks):
                        self.copy(origin, chunk, way).wait_send()


class LineSum:
    def __init__(self, parts, chunks, held, come, out_sem, in_sem):
        self.parts, self.chunks, self.held, self.come = parts, chunks, held, come
        self.out_sem, self.in_sem = out_sem, in_sem
        self.me = lax.axis_index("mp")
        self.rows = held.shape[1] // chunks

    def slot(self, way, target, device):
        return target + (self.parts - target) * ((target == device) & (way == 0)).astype(jnp.int32)

    def copy(self, target, chunk):
        way = (target > self.me).astype(jnp.int32)
        slot = self.slot(way, target, self.me + 2 * way - 1)
        span = pl.ds(chunk * self.rows, self.rows)
        return pltpu.make_async_remote_copy(
            src_ref=self.held.at[target, span],
            dst_ref=self.come.at[slot, span],
            send_sem=self.out_sem.at[target, chunk],
            recv_sem=self.in_sem.at[slot, chunk],
            device_id={"mp": self.me + 2 * way - 1},
            device_id_type=MESH,
        )

    def come_in(self, slot, chunk):
        piece = self.come.at[slot, pl.ds(chunk * self.rows, self.rows)]
        pltpu.make_async_copy(piece, piece, self.in_sem.at[slot, chunk]).wait()

    def turned(self, target):
        right = (2 * self.me >= self.parts).astype(jnp.int32)
        return target + right * (self.parts - 1 - 2 * target)

    def begin(self, target):
        end = ((target < self.me) & (self.me == self.parts - 1)) | ((target > self.me) & (self.me == 0))

        @pl.when(end)
        def _():
            for chunk in range(self.chunks):
                self.copy(target, chunk).start()

    def relay(self, target, chunk):
        between = ((target < self.me) & (self.me < self.parts - 1)) | ((target > self.me) & (self.me > 0))

        @pl.when(between)
        def _():
            span = pl.ds(chunk * self.rows, self.rows)
            self.come_in(target, chunk)
            self.held[target, span, :] = self.held[target, span, :] + self.come[target, span, :]
            self.copy(target, chunk).start()

    def total(self, chunk, out):
        span = pl.ds(chunk * self.rows, self.rows)
        out[span, :] = self.held[self.me, span, :].astype(jnp.float32)
        for slot, there in ((self.parts, self.me < self.parts - 1), (self.me, self.me > 0)):

            @pl.when(there)
            def _():
                self.come_in(slot, chunk)
                out[span, :] = out[span, :] + self.come[slot, span, :].astype(jnp.float32)

    def finish(self):
        for target in range(self.parts):

            @pl.when(self.me != target)
            def _():
                for chunk in range(self.chunks):
                    self.copy(target, chunk).wait_send()


class Exchange:
    def __init__(self, groups, source, held, out_sem, in_sem):
        self.groups, self.source, self.held = groups, source, held
        self.out_sem, self.in_sem = out_sem, in_sem
        self.me = lax.axis_index("dp")
        self.rows = source.shape[0] // groups

    def copy(self, turn):
        peer = lax.rem(self.me + turn, self.groups)
        return pltpu.make_async_remote_copy(
            src_ref=self.source.at[pl.ds(peer * self.rows, self.rows)],
            dst_ref=self.held.at[pl.ds(self.me * self.rows, self.rows)],
            send_sem=self.out_sem.at[turn],
            recv_sem=self.in_sem.at[turn],
            device_id={"dp": peer},
            device_id_type=MESH,
        )

    def begin(self):
        for turn in range(1, self.groups):
            self.copy(turn).start()
        span = pl.ds(pl.multiple_of(self.me * self.rows, self.rows), self.rows)
        self.held[span, :] = self.source[span, :]

    def arrive(self):
        for turn in range(1, self.groups):
            self.copy(turn).wait_recv()

    def finish(self):
        for turn in range(1, self.groups):
            self.copy(turn).wait_send()


def row_type(rows):
    return jnp.bfloat16 if rows % 16 == 0 else jnp.float32


def greet(groups, parts):
    barrier = pltpu.get_barrier_semaphore()
    for axis, size in (("dp", groups), ("mp", parts)):
        for turn in range(1, size):
            peer = lax.rem(lax.axis_index(axis) + turn, size)
            pl.semaphore_signal(barrier, inc=1, device_id={axis: peer}, device_id_type=MESH)
    pl.semaphore_wait(barrier, groups + parts - 2)


def far_first(parts):
    return sorted(range(parts), key=lambda t: (-abs(2 * t - parts + 1), -t))


def scale_of(values):
    return lax.rsqrt(jnp.mean(values * values, axis=1, keepdims=True) + EPS)


def sorting(home, rows):
    place = lax.broadcasted_iota(jnp.int32, (rows, rows), 0)
    return jnp.where(place == home, 1.0, 0.0).astype(jnp.bfloat16)


def bias_of(seg_row, seg_col, start, low, stop):
    span = stop - start
    query = lax.broadcasted_iota(jnp.int32, (span, stop - low), 0) + start
    key = lax.broadcasted_iota(jnp.int32, (span, stop - low), 1) + low
    same = seg_col[start:stop, :] == seg_row[:, low:stop]
    return jnp.where(same & (key <= query), 0.0, -1e30)


def forward_kernel(groups, parts, heads, heads_kv, home, seg_row, seg_col, attn_gain, moe_gain, tokens, out_grad, wpack,
                   gate_in, up_in, down_in,
                   middle, router_out, first_out, qkv_out, mix_out, weights_out, second_out, grad_out, gate_full, up_full, down_full,
                   first, second, grad, weights, qkv, mix, part, come, bias, sorted_second, sorted_grad, dealt_second, dealt_grad,
                   wide_load, tall_load, gate_low, up_low, down_low,
                   gather_sems, moe_sems, line_out, line_in, sum_out, sum_in, deal_out, deal_in, save_sem, load_sem):
    low = jnp.bfloat16
    shard, width = tokens.shape
    me, place = lax.axis_index("dp"), lax.axis_index("mp")
    share = heads // heads_kv
    block = wpack.shape[0]
    cut = block // 2
    saves = []

    def save(number, source, target):
        copy = pltpu.make_async_copy(source, target, save_sem.at[number])
        copy.start()
        saves.append(copy)

    greet(groups, parts)
    gather = CubeGather(
        groups,
        2,
        lambda chunk: wpack.at[pl.ds(chunk * cut, cut)],
        lambda chunk, owner: weights.at[pl.ds(owner * block + chunk * cut, cut)],
        gather_sems,
    )
    for chunk in range(2):
        gather.begin(chunk)
    values = tokens[...]
    first[place] = (values * scale_of(values) * attn_gain[...]).astype(low)
    lines = [LineGather(parts, CUTS, held, line_out.at[n], line_in.at[n]) for n, held in enumerate((first, grad, second))]
    for chunk in range(CUTS):
        lines[0].begin(chunk)
    sort = sorting(home[...], shard)
    sorted_grad[...] = mm(sort, out_grad[...].astype(low)).astype(sorted_grad.dtype)
    for event in gather.events():
        event()
    deal_grad = Exchange(groups, sorted_grad, dealt_grad, deal_out.at[0], deal_in.at[0])
    deal_grad.begin()
    gather.finish()

    count = gate_in.shape[0] // 4
    per, hidden, _ = down_in.shape
    high = hidden // 4

    def place_of(chunk, owner):
        if chunk < 2 * count:
            full = (gate_full, up_full)[chunk // count]
            return full.at[pl.ds(chunk % count * 4, 4), pl.ds(owner * block, block)]
        return down_full.at[pl.ds(owner * per, per), pl.ds((chunk - 2 * count) * high, high)]

    def block_of(chunk, arrays):
        if chunk < 2 * count:
            return arrays[chunk // count].at[pl.ds(chunk % count * 4, 4)]
        return arrays[2].at[:, pl.ds((chunk - 2 * count) * high, high)]

    moe = CubeGather(groups, 2 * count + 4, lambda chunk: block_of(chunk, (gate_low, up_low, down_low)), place_of, moe_sems)

    def load(chunk):
        held = (wide_load if chunk < 2 * count else tall_load).at[chunk % 2]
        copy = pltpu.make_async_copy(block_of(chunk, (gate_in, up_in, down_in)), held, load_sem.at[chunk % 2])
        copy.start()
        return copy, held

    loaded = [load(0)]
    for chunk in range(moe.chunks):
        if chunk + 1 < moe.chunks:
            loaded.append(load(chunk + 1))
        copy, held = loaded[chunk]
        copy.wait()
        target = block_of(chunk, (gate_low, up_low, down_low))

        def row(index, _):
            target[index] = held[index].astype(low)
            return 0

        lax.fori_loop(0, held.shape[0], row, 0)
        moe.begin(chunk)
    events = moe.events()
    save(0, weights.at[:, : weights_out.shape[1]], weights_out)
    router = weights[:, weights_out.shape[1] :].astype(jnp.float32)
    router_out[...] = jnp.transpose(router)[:E, :].astype(low)

    def project(origin):
        result = mm(first[origin], weights[:, : (heads + 2 * heads_kv) * HD])
        span = pl.ds(pl.multiple_of(origin * shard, shard), shard)
        for head in range(heads + 2 * heads_kv):
            qkv[head, span, :] = result[:, head * HD : (head + 1) * HD].astype(low)

    project(place)
    for distance in range(1, parts):
        if distance == parts - 1:
            deal_grad.arrive()
            grad[place] = dealt_grad[...].astype(low)
            for chunk in range(CUTS):
                lines[1].begin(chunk)
        for chunk in range(CUTS):
            for way in (0, 1):
                lines[0].step(distance, way, chunk)
        for way in (0, 1):
            lines[0].from_side(distance, way, project)
    save(1, first, first_out)
    save(2, qkv, qkv_out)

    sums = LineSum(parts, CUTS, part, come, sum_out, sum_in)
    order = far_first(parts)
    reach = -(-512 // shard)
    for number, target in enumerate(order):
        start, stop = target * shard, (target + 1) * shard
        bottom = max(0, target - reach) * shard
        bias[:, : stop - bottom] = bias_of(seg_row, seg_col, start, bottom, stop)

        def attend(head, _):
            group = head // share
            keys = qkv[heads + group, bottom:stop, :]
            scores = mm(qkv[head, start:stop, :], keys, NT) * HD**-0.5 + bias[:, : stop - bottom]
            raised = jnp.exp(scores - jnp.max(scores, axis=1, keepdims=True))
            probs = (raised * (1.0 / jnp.sum(raised, axis=1, keepdims=True))).astype(low)
            mix[head, start:stop, :] = mm(probs, qkv[heads + heads_kv + group, bottom:stop, :]).astype(low)
            return 0

        lax.fori_loop(0, heads, attend, 0)
        flat = jnp.concatenate([mix[head, start:stop, :] for head in range(heads)], axis=1)
        part[target] = mm(flat, weights[:, (heads + 2 * heads_kv) * HD : weights_out.shape[1]], NT).astype(low)
        sums.begin(target)
    save(3, mix, mix_out)
    for number, target in enumerate(order):
        for chunk in range(CUTS):
            if number < parts - 1:
                for way in (0, 1):
                    lines[1].step(number + 1, way, chunk)
            sums.relay(sums.turned(target), chunk)
    for chunk in range(CUTS):
        sums.total(chunk, middle)
    values = tokens[...] + middle[...]
    middle[...] = values
    normed = (values * scale_of(values) * moe_gain[...]).astype(low)
    sorted_second[...] = mm(sort, normed).astype(sorted_second.dtype)
    deal = Exchange(groups, sorted_second, dealt_second, deal_out.at[1], deal_in.at[1])
    for event in events[:4]:
        event()
    deal.begin()
    save(4, grad, grad_out)
    singles = moe.bits * moe.chunks
    for event in events[4:singles]:
        event()
    deal.arrive()
    second[place] = dealt_second[...].astype(low)
    for chunk in range(CUTS):
        lines[2].begin(chunk)
    rest = events[singles:]
    turns = (parts - 1) * CUTS
    for turn in range(turns):
        for way in (0, 1):
            lines[2].step(1 + turn // CUTS, way, turn % CUTS)
        for event in rest[turn * len(rest) // turns : (turn + 1) * len(rest) // turns]:
            event()
    save(5, second, second_out)
    moe.finish()
    for line in lines:
        line.finish()
    sums.finish()
    deal_grad.finish()
    deal.finish()
    for copy in saves:
        copy.wait()


def forward(groups, parts, home, seg, attn_gain, moe_gain, tokens, out_grad, wpack, w_gate, w_up, w_down, heads, heads_kv):
    shard, width = tokens.shape
    rows = shard * parts
    low = jnp.bfloat16
    slots = heads + 2 * heads_kv
    columns = wpack.shape[1]
    block, hidden = w_gate.shape[1:]
    per = w_down.shape[0]
    chunks = 2 * (E // 4) + 4
    vmem = pl.BlockSpec(memory_space=pltpu.VMEM)
    hbm = pl.BlockSpec(memory_space=pl.ANY)
    dma = pltpu.SemaphoreType.DMA
    held = lambda: pltpu.VMEM((parts, shard, width), low)
    return pl.pallas_call(
        functools.partial(forward_kernel, groups, parts, heads, heads_kv),
        in_specs=[vmem] * 7 + [hbm] * 4,
        out_specs=[vmem] * 2 + [hbm] * 9,
        out_shape=[
            jax.ShapeDtypeStruct((shard, width), jnp.float32),
            jax.ShapeDtypeStruct((E, width), low),
            jax.ShapeDtypeStruct((parts, shard, width), low),
            jax.ShapeDtypeStruct((slots, rows, HD), low),
            jax.ShapeDtypeStruct((heads, rows, HD), low),
            jax.ShapeDtypeStruct((width, columns - 128), low),
            jax.ShapeDtypeStruct((parts, shard, width), low),
            jax.ShapeDtypeStruct((parts, shard, width), low),
            jax.ShapeDtypeStruct((E, width, hidden), low),
            jax.ShapeDtypeStruct((E, width, hidden), low),
            jax.ShapeDtypeStruct((E, hidden, width), low),
        ],
        scratch_shapes=[
            held(),
            held(),
            held(),
            pltpu.VMEM((width, columns), low),
            pltpu.VMEM((slots, rows, HD), low),
            pltpu.VMEM((heads, rows, HD), low),
            held(),
            pltpu.VMEM((parts + 1, shard, width), low),
            pltpu.VMEM((shard, shard * (1 - (-512 // shard))), jnp.float32),
            *[pltpu.VMEM((shard, width), row_type(shard // groups))] * 4,
            pltpu.VMEM((2, 4, block, hidden), jnp.float32),
            pltpu.VMEM((2, per, hidden // 4, width), jnp.float32),
            pltpu.VMEM((E, block, hidden), low),
            pltpu.VMEM((E, block, hidden), low),
            pltpu.VMEM((per, hidden, width), low),
            cube_sems(groups, 2),
            cube_sems(groups, chunks),
            dma((3, 2, parts, CUTS)),
            dma((3, parts, CUTS)),
            dma((parts, CUTS)),
            dma((parts + 1, CUTS)),
            dma((2, groups)),
            dma((2, groups)),
            dma((6,)),
            dma((2,)),
        ],
        compiler_params=pltpu.CompilerParams(
            collective_id=0, has_side_effects=True, vmem_limit_bytes=56 * 2**20
        ),
        cost_estimate=pl.CostEstimate(
            flops=12 * rows * width * columns, bytes_accessed=60 * 2**20, transcendentals=rows * rows * heads
        ),
    )(home, seg[None, :], seg[:, None], attn_gain[None, :], moe_gain[None, :], tokens, out_grad, wpack,
      w_gate, w_up, w_down)


class CubeSum:
    def __init__(self, groups, chunks, own, pair_held, step_held, sems):
        self.bits = groups.bit_length() - 2
        self.chunks, self.own, self.pair_held, self.step_held = chunks, own, pair_held, step_held
        self.out_sem, self.in_sem, self.pair_out, self.pair_in = sems
        self.me = lax.axis_index("dp")
        self.waits = []

    def flip(self, index, mask):
        for bit in range(self.bits + 1):
            if mask >> bit & 1:
                index = index + (1 << bit) * (1 - 2 * ((index // (1 << bit)) % 2))
        return index

    def step_of(self, chunk, want):
        for step in range(self.bits):
            bit = (chunk + step) % self.bits
            if want >> bit & 1:
                return step, bit
        return self.bits, None

    def pair(self, chunk):
        for want in range(1 << self.bits):
            copy = pltpu.make_async_remote_copy(
                src_ref=self.own(chunk, self.flip(self.me, 2 * want + 1)),
                dst_ref=self.pair_held(chunk, want),
                send_sem=self.pair_out.at[chunk, want],
                recv_sem=self.pair_in.at[chunk, want],
                device_id={"dp": self.flip(self.me, 1)},
                device_id_type=MESH,
            )
            copy.start()
            self.waits.append(copy.wait_send)

    def send(self, chunk, want, source):
        step, bit = self.step_of(chunk, want)
        rest = want ^ (1 << bit)
        copy = pltpu.make_async_remote_copy(
            src_ref=source,
            dst_ref=self.step_held(chunk, step, rest),
            send_sem=self.out_sem.at[chunk, want],
            recv_sem=self.in_sem.at[chunk, step, rest],
            device_id={"dp": self.flip(self.me, 2 << bit)},
            device_id_type=MESH,
        )
        copy.start()
        return copy.wait_send

    def terms(self, chunk, want):
        found = [self.own(chunk, self.flip(self.me, 2 * want)), self.pair_held(chunk, want)]
        pltpu.make_async_copy(found[1], found[1], self.pair_in.at[chunk, want]).wait()
        for step in range(self.step_of(chunk, want)[0]):
            held = self.step_held(chunk, step, want)
            pltpu.make_async_copy(held, held, self.in_sem.at[chunk, step, want]).wait()
            found.append(held)
        return found

    def items(self, lag):
        found = []
        for chunk in range(self.chunks):
            for want in range(1 << self.bits):
                step = self.step_of(chunk, want)[0]
                found.append((chunk + lag * step, step, chunk, want))
        return [item[2:] for item in sorted(found)]

    def finish(self):
        for wait in self.waits:
            wait()


def sum_sems(groups, chunks):
    bits = groups.bit_length() - 2
    dma = pltpu.SemaphoreType.DMA
    return [
        dma((chunks, 1 << bits)),
        dma((chunks, bits, 1 << bits)),
        dma((chunks, 1 << bits)),
        dma((chunks, 1 << bits)),
    ]


class Stream:
    def __init__(self, cube, lag, terms, sums, totals, out, load_sem, save_sem):
        self.cube, self.terms, self.sums, self.totals, self.out = cube, terms, sums, totals, out
        self.load_sem, self.save_sem = load_sem, save_sem
        self.list = cube.items(lag)
        self.at, self.sent, self.saved, self.loads = 0, [], [], None

    def tick(self, times=1):
        for _ in range(times):
            if self.at <= len(self.list):
                loads = self.fetch(self.at) if self.at < len(self.list) else None
                if self.loads is not None:
                    self.add(self.at - 1)
                self.loads = loads
                self.at += 1

    def fetch(self, number):
        slot = number % 2
        loads = []
        for term, ref in enumerate(self.cube.terms(*self.list[number])):
            copy = pltpu.make_async_copy(ref, self.terms.at[slot, term], self.load_sem.at[slot, term])
            copy.start()
            loads.append(copy)
        return loads

    def add(self, number):
        slot = number % 2
        chunk, want = self.list[number]
        for copy in self.loads:
            copy.wait()
        count = len(self.loads)
        if want:
            place = len(self.sent) % self.sums.shape[0]
            if len(self.sent) >= self.sums.shape[0]:
                self.sent[len(self.sent) - self.sums.shape[0]]()
            target = self.sums.at[place]
        else:
            place = len(self.saved) % self.totals.shape[0]
            if len(self.saved) >= self.totals.shape[0]:
                self.saved[len(self.saved) - self.totals.shape[0]]()
            target = self.totals.at[place]

        def row(index, _):
            total = self.terms[slot, 0, index].astype(jnp.float32)
            for term in range(1, count):
                total = total + self.terms[slot, term, index].astype(jnp.float32)
            target[index] = total.astype(target.dtype)
            return 0

        lax.fori_loop(0, target.shape[0], row, 0)
        if want:
            self.sent.append(self.cube.send(chunk, want, target))
        else:
            for source, result in self.out(chunk, target):
                pltpu.make_async_copy(source, result, self.save_sem.at[place]).start()
            self.saved.append(pltpu.make_async_copy(target, target, self.save_sem.at[place]).wait)

    def finish(self):
        self.tick(len(self.list) + 1 - self.at)
        for wait in self.sent[-self.sums.shape[0] :] + self.saved[-self.totals.shape[0] :]:
            wait()


class Share:
    def __init__(self, axis, size, held, out_sem, in_sem, source):
        self.axis, self.size, self.held = axis, size, held
        self.out_sem, self.in_sem, self.source = out_sem, in_sem, source
        self.me = lax.axis_index(axis)

    def copy(self, turn):
        peer = lax.rem(self.me + turn, self.size)
        return pltpu.make_async_remote_copy(
            src_ref=self.source(peer),
            dst_ref=self.held.at[self.me],
            send_sem=self.out_sem.at[turn],
            recv_sem=self.in_sem.at[turn],
            device_id={self.axis: peer},
            device_id_type=MESH,
        )

    def begin(self):
        for turn in range(1, self.size):
            self.copy(turn).start()
        self.held[self.me] = self.source(self.me)[...]

    def total(self):
        for turn in range(1, self.size):
            self.copy(turn).wait()
        total = self.held[0]
        for index in range(1, self.size):
            total = total + self.held[index]
        return total


def backward_kernel(groups, parts, heads, heads_kv, home, seg_row, seg_col, attn_gain, moe_gain, tokens, out_grad, middle,
                    router_part, back_in, mixed_in, first_in, qkv_in, mix_in, weights_in, gate_in, up_in, down_in,
                    block_out, tokens_grad, gains_out, router_out, pack_out, gate_out, up_out, down_out, pair_held, step_held,
                    held, come, mixed, mixed_come, grad, qkv, mix, weights, grad_mix, grad_query, grad_key, grad_value,
                    flat, bias, pack, pack_pair, pack_step, stage, land_back, land_mixed, terms, sums, totals,
                    router_all, router_line, gains, gains_line, gains_all,
                    load_sem, cube_sems, pack_sems, term_sem, save_sem, line_out, line_in, sum_out, sum_in, deal_out, deal_in,
                    share_out, share_in):
    low = jnp.bfloat16
    shard, width = tokens.shape
    me, place = lax.axis_index("dp"), lax.axis_index("mp")
    share = heads // heads_kv
    slots = heads + 2 * heads_kv
    bits = groups.bit_length() - 2
    arrays = ((back_in, held), (weights_in, weights), (mix_in, mix), (qkv_in, qkv), (mixed_in, mixed))
    loads = []
    for number, (source, target) in enumerate(arrays):
        loads.append(pltpu.make_async_copy(source, target, load_sem.at[number]))
        loads[-1].start()
    greet(groups, parts)

    gains[...] = jnp.zeros_like(gains)
    count = gate_in.shape[0] // 4
    owner_rows = width // groups

    def own(chunk, owner):
        if chunk < 2 * count:
            ref = (gate_in, up_in)[chunk // count]
            return ref.at[pl.ds(chunk % count * 4, 4), pl.ds(owner * owner_rows, owner_rows)]
        return down_in.at[owner, chunk - 2 * count]

    places = {}

    def step_place(chunk, step, want):
        return step_held.at[chunk, places.setdefault((chunk, step, want), len([k for k in places if k[0] == chunk]))]

    cube = CubeSum(groups, 3 * count, own, lambda chunk, want: pair_held.at[chunk, want], step_place, cube_sems)
    per, hidden, _ = down_out.shape
    subs = 4 // per
    span = hidden // 4 // subs

    def out(chunk, total):
        if chunk < 2 * count:
            return [(total, (gate_out, up_out)[chunk // count].at[pl.ds(chunk % count * 4, 4)])]
        found = []
        for index in range(4):
            row = (chunk - 2 * count) * (hidden // 4) + index % subs * span
            for column in range(width // hidden):
                source = total.at[index, pl.ds(column * span, span)]
                target = down_out.at[index // subs, pl.ds(row, span), pl.ds(column * hidden, hidden)]
                found.append((source, target))
        return found

    stream = Stream(cube, 3, terms, sums, totals, out, term_sem, save_sem)

    back = LineSum(parts, CUTS, held, come, sum_out.at[0], sum_in.at[0])
    loads[0].wait()
    order = far_first(parts)
    for target in order:
        back.begin(back.turned(target))
    for chunk in range(3 * count):
        cube.pair(chunk)
    routers = Share("dp", groups, router_all, share_out.at[0], share_in.at[0], lambda peer: router_part.at[peer])
    routers.begin()
    stream.tick(1)
    for target in order:
        for chunk in range(CUTS):
            back.relay(back.turned(target), chunk)
            stream.tick(1 if target in order[:2] else 0)
    for chunk in range(CUTS):
        back.total(chunk, block_out)
    stage[...] = block_out[...].astype(stage.dtype)
    deal = Exchange(groups, stage, land_back, deal_out.at[0], deal_in.at[0])
    deal.begin()
    back.finish()
    router_line[place] = routers.total()
    router_sums = Share("mp", parts, router_line, share_out.at[1], share_in.at[1], lambda peer: router_line.at[place])
    for turn in range(1, parts):
        router_sums.copy(turn).start()
    sort = sorting(home[...], shard)
    values = middle[...]
    scale = scale_of(values)
    deal.arrive()
    grad_second = mm(sort, land_back[...].astype(low), TN)
    weighted = grad_second * moe_gain[...]
    inner = jnp.mean(weighted * values, axis=1, keepdims=True)
    gains[0:1, :] = jnp.sum(grad_second * values * scale, axis=0, keepdims=True)
    grad_middle = out_grad[...] + (scale * weighted - values * (scale * scale * scale * inner))
    tokens_grad[...] = grad_middle
    grad[place] = grad_middle.astype(low)
    line = LineGather(parts, CUTS, grad, line_out, line_in)
    for chunk in range(CUTS):
        line.begin(chunk)
    loads[4].wait()
    extra = LineSum(parts, CUTS, mixed, mixed_come, sum_out.at[1], sum_in.at[1])
    for target in order:
        extra.begin(extra.turned(target))
    loads[1].wait()

    def mix_back(origin):
        result = mm(grad[origin], weights[:, slots * HD :])
        span = pl.ds(pl.multiple_of(origin * shard, shard), shard)
        for head in range(heads):
            grad_mix[head, span, :] = result[:, head * HD : (head + 1) * HD].astype(low)

    mix_back(place)
    stream.tick(2)
    for distance in range(1, parts):
        for chunk in range(CUTS):
            for way in (0, 1):
                line.step(distance, way, chunk)
            stream.tick()
        for way in (0, 1):
            line.from_side(distance, way, mix_back)
    loads[3].wait()

    first_sum = LineSum(parts, CUTS, held, come, sum_out.at[2], sum_in.at[2])
    grad_key[...] = jnp.zeros_like(grad_key)
    grad_value[...] = jnp.zeros_like(grad_value)
    reach = -(-512 // shard)
    for number, target in enumerate(reversed(range(parts))):
        start, stop = target * shard, (target + 1) * shard
        bottom = max(0, target - reach) * shard
        bias[:, : stop - bottom] = bias_of(seg_row, seg_col, start, bottom, stop)

        def attend(head, _):
            group = head // share
            query = qkv[head, start:stop, :]
            keys = qkv[heads + group, bottom:stop, :]
            scores = mm(query, keys, NT) * HD**-0.5 + bias[:, : stop - bottom]
            raised = jnp.exp(scores - jnp.max(scores, axis=1, keepdims=True))
            probs = raised * (1.0 / jnp.sum(raised, axis=1, keepdims=True))
            grad_rows = grad_mix[head, start:stop, :]
            grad_probs = mm(grad_rows, qkv[heads + heads_kv + group, bottom:stop, :], NT)
            inner = jnp.sum(probs * grad_probs, axis=1, keepdims=True)
            grad_scores = (probs * (grad_probs - inner)).astype(low)
            grad_query[head, start:stop, :] = (mm(grad_scores, keys) * HD**-0.5).astype(low)
            grad_key[group, bottom:stop, :] += mm(grad_scores, query, TN)
            grad_value[group, bottom:stop, :] += mm(probs.astype(low), grad_rows, TN)
            return 0

        lax.fori_loop(0, heads, attend, 0)
        pieces = [grad_query[head, start:stop, :] for head in range(heads)]
        pieces += [(grad_key[group, start:stop, :] * HD**-0.5).astype(low) for group in range(heads_kv)]
        pieces += [grad_value[group, start:stop, :].astype(low) for group in range(heads_kv)]
        flat[start:stop, :] = jnp.concatenate(pieces, axis=1)
        held[target] = mm(flat[start:stop, :], weights[:, : slots * HD], NT).astype(low)
        first_sum.begin(target)
        for chunk in range(CUTS):
            extra.relay(extra.turned(order[number]), chunk)
            if number > 0:
                first_sum.relay(target + 1, chunk)
            stream.tick(1)
    loads[2].wait()
    mix_flat = jnp.concatenate([mix[head] for head in range(heads)], axis=1)
    pack[:, slots * HD :] = mm(grad[...].reshape(parts * shard, width), mix_flat, TN).astype(low)
    for chunk in range(CUTS):
        first_sum.relay(0, chunk)
        extra.total(chunk, block_out)
        stream.tick()
    deal.finish()
    stage[...] = block_out[...].astype(stage.dtype)
    deal_mixed = Exchange(groups, stage, land_mixed, deal_out.at[1], deal_in.at[1])
    deal_mixed.begin()
    extra.finish()
    first_load = pltpu.make_async_copy(first_in, mixed, load_sem.at[5])
    first_load.start()
    stream.tick(2)
    first_load.wait()
    pack[:, : slots * HD] = mm(mixed[...].reshape(parts * shard, width), flat[...], TN).astype(low)
    cut = owner_rows // 2
    pack_places = {}

    def pack_place(chunk, step, want):
        return pack_step.at[chunk, pack_places.setdefault((chunk, step, want), len([k for k in pack_places if k[0] == chunk]))]

    pack_cube = CubeSum(
        groups,
        2,
        lambda chunk, owner: pack.at[pl.ds(owner * owner_rows + chunk * cut, cut)],
        lambda chunk, want: pack_pair.at[chunk, want],
        pack_place,
        pack_sems,
    )
    for chunk in range(2):
        pack_cube.pair(chunk)
    deal_mixed.arrive()
    home_rows = mm(sort, land_mixed[...].astype(low), TN)
    pack_sent = []
    for chunk, want in pack_cube.items(1):
        stream.tick(1)
        refs = pack_cube.terms(chunk, want)
        total = refs[0][...].astype(jnp.float32)
        for ref in refs[1:]:
            total = total + ref[...].astype(jnp.float32)
        if want:
            refs[0][...] = total.astype(low)
            pack_sent.append(pack_cube.send(chunk, want, refs[0]))
        else:
            pack_out[chunk * cut : (chunk + 1) * cut, :] = total
    for chunk in range(CUTS):
        first_sum.total(chunk, block_out)
    grad_first = block_out[...]
    values = tokens[...]
    scale = scale_of(values)
    weighted = grad_first * attn_gain[...]
    inner = jnp.mean(weighted * values, axis=1, keepdims=True)
    gains[1:2, :] = jnp.sum(grad_first * values * scale, axis=0, keepdims=True)
    gains_lines = Share("mp", parts, gains_line, share_out.at[2], share_in.at[2], lambda peer: gains)
    gains_lines.begin()
    tokens_grad[...] += scale * weighted - values * (scale * scale * scale * inner)
    block_out[...] = middle[...] + home_rows
    router_out[...] = router_sums.total()
    gains[...] = gains_lines.total()
    gains_rest = Share("dp", groups, gains_all, share_out.at[3], share_in.at[3], lambda peer: gains)
    gains_rest.begin()
    stream.finish()
    gains_out[...] = gains_rest.total()
    line.finish()
    first_sum.finish()
    deal_mixed.finish()
    cube.finish()
    pack_cube.finish()
    for wait in pack_sent:
        wait()


def backward(groups, parts, heads, heads_kv, home, seg, attn_gain, moe_gain, tokens, out_grad, middle, router_part,
             back, mixed, first, qkv, mix, weights, gate_grad, up_grad, down_grad):
    shard, width = tokens.shape
    rows = shard * parts
    low = jnp.bfloat16
    slots = heads + 2 * heads_kv
    columns = weights.shape[1]
    owner_rows, hidden = width // groups, gate_grad.shape[2]
    bits = groups.bit_length() - 2
    chunks = 3 * (E // 4)
    cut = owner_rows // 2
    vmem = pl.BlockSpec(memory_space=pltpu.VMEM)
    hbm = pl.BlockSpec(memory_space=pl.ANY)
    dma = pltpu.SemaphoreType.DMA
    f32 = lambda *shape: jax.ShapeDtypeStruct(shape, jnp.float32)
    unit = (4, owner_rows, hidden)
    held = pltpu.VMEM((parts, shard, width), low)
    come = pltpu.VMEM((parts + 1, shard, width), low)
    line = row_type(shard // groups)
    return pl.pallas_call(
        functools.partial(backward_kernel, groups, parts, heads, heads_kv),
        in_specs=[vmem] * 9 + [hbm] * 9,
        out_specs=[vmem] * 5 + [hbm] * 5,
        out_shape=[
            f32(shard, width),
            f32(shard, width),
            f32(8, width),
            f32(E, owner_rows),
            f32(owner_rows, columns),
            f32(E, owner_rows, hidden),
            f32(E, owner_rows, hidden),
            f32(E // groups, hidden, width),
            jax.ShapeDtypeStruct((chunks, 1 << bits, *unit), low),
            jax.ShapeDtypeStruct((chunks, (1 << bits) - 1, *unit), low),
        ],
        scratch_shapes=[
            held,
            come,
            held,
            come,
            held,
            pltpu.VMEM((slots, rows, HD), low),
            pltpu.VMEM((heads, rows, HD), low),
            pltpu.VMEM((width, columns), low),
            pltpu.VMEM((heads, rows, HD), low),
            pltpu.VMEM((heads, rows, HD), low),
            pltpu.VMEM((heads_kv, rows, HD), jnp.float32),
            pltpu.VMEM((heads_kv, rows, HD), jnp.float32),
            pltpu.VMEM((rows, slots * HD), low),
            pltpu.VMEM((shard, shard * (1 - (-512 // shard))), jnp.float32),
            pltpu.VMEM((width, columns), low),
            pltpu.VMEM((2, 1 << bits, cut, columns), low),
            pltpu.VMEM((2, (1 << bits) - 1, cut, columns), low),
            pltpu.VMEM((shard, width), line),
            pltpu.VMEM((shard, width), line),
            pltpu.VMEM((shard, width), line),
            pltpu.VMEM((2, 2 + bits, *unit), low),
            pltpu.VMEM((4, *unit), low),
            pltpu.VMEM((2, *unit), jnp.float32),
            pltpu.VMEM((groups, E, owner_rows), jnp.float32),
            pltpu.VMEM((parts, E, owner_rows), jnp.float32),
            pltpu.VMEM((8, width), jnp.float32),
            pltpu.VMEM((parts, 8, width), jnp.float32),
            pltpu.VMEM((groups, 8, width), jnp.float32),
            dma((6,)),
            sum_sems(groups, chunks),
            sum_sems(groups, 2),
            dma((2, 2 + bits)),
            dma((2,)),
            dma((2, parts, CUTS)),
            dma((parts, CUTS)),
            dma((3, parts, CUTS)),
            dma((3, parts + 1, CUTS)),
            dma((2, groups)),
            dma((2, groups)),
            dma((4, max(groups, parts))),
            dma((4, max(groups, parts))),
        ],
        compiler_params=pltpu.CompilerParams(
            collective_id=1, has_side_effects=True, vmem_limit_bytes=63 * 2**20
        ),
        cost_estimate=pl.CostEstimate(
            flops=24 * rows * width * columns, bytes_accessed=200 * 2**20, transcendentals=rows * rows * heads
        ),
    )(home, seg[None, :], seg[:, None], attn_gain[None, :], moe_gain[None, :], tokens, out_grad, middle, router_part,
      back, mixed, first, qkv, mix, weights, gate_grad, up_grad, down_grad)


def body(
    tokens,
    attn_gain,
    w_query,
    w_key,
    w_value,
    w_out,
    moe_gain,
    w_router,
    w_gate,
    w_up,
    w_down,
    seq_lengths,
    deal_order,
    expert_ids,
    out_grad,
):
    groups, parts = lax.axis_size("dp"), lax.axis_size("mp")
    rows = tokens.shape[0] * parts
    low_type = jnp.bfloat16
    heads, heads_kv = w_query.shape[1] // HD, w_key.shape[1] // HD
    wpack = jnp.concatenate(
        [w_query, w_key, w_value, w_out.T, jnp.pad(w_router, ((0, 0), (0, 128 - E)))], axis=1
    ).astype(low_type)
    home, code, counts = deal_tables(deal_order, expert_ids, rows)
    segment = segment_of(seq_lengths[0], rows)
    middle, router_w, first_full, qkv, mix, weights, second_full, grad_full, gate_w, up_w, down_w = forward(
        groups, parts, home[None, :], segment, attn_gain, moe_gain, tokens, out_grad, wpack, w_gate, w_up, w_down, heads, heads_kv
    )
    mixed, back, gate_grad, up_grad, down_grad, router_part = experts(
        groups,
        second_full.reshape(rows, D),
        grad_full.reshape(rows, D),
        code,
        counts,
        router_w,
        gate_w,
        up_w,
        down_w,
    )
    block_out, tokens_grad, gains, router_sum, pack_sum, gate_sum, up_sum, down_sum, _, _ = backward(
        groups,
        parts,
        heads,
        heads_kv,
        home[None, :],
        segment,
        attn_gain,
        moe_gain,
        tokens,
        out_grad,
        middle,
        router_part,
        back.reshape(second_full.shape),
        mixed.reshape(second_full.shape),
        first_full,
        qkv,
        mix,
        weights,
        gate_grad,
        up_grad,
        down_grad,
    )
    columns, columns_kv = heads * HD, heads_kv * HD
    return (
        block_out,
        tokens_grad,
        gains[1],
        pack_sum[:, :columns],
        pack_sum[:, columns : columns + columns_kv],
        pack_sum[:, columns + columns_kv : columns + 2 * columns_kv],
        pack_sum[:, columns + 2 * columns_kv :].T,
        gains[0],
        router_sum.T,
        gate_sum,
        up_sum,
        down_sum,
    )


def solution(mesh):
    return jax.shard_map(
        body,
        mesh=mesh,
        in_specs=(
            P(("dp", "mp"), None),
            P(),
            P("dp", "mp"),
            P("dp", "mp"),
            P("dp", "mp"),
            P("mp", "dp"),
            P(),
            P("dp", None),
            P(None, "dp", "mp"),
            P(None, "dp", "mp"),
            P("dp", "mp", None),
            P("dp", None),
            P(),
            P("dp", None),
            P(("dp", "mp"), None),
        ),
        out_specs=(
            P(("dp", "mp"), None),
            P(("dp", "mp"), None),
            P(),
            P("dp", "mp"),
            P("dp", "mp"),
            P("dp", "mp"),
            P("mp", "dp"),
            P(),
            P("dp", None),
            P(None, "dp", "mp"),
            P(None, "dp", "mp"),
            P("dp", "mp", None),
        ),
        check_vma=False,
    )
```

```python
import functools

import jax
import jax.numpy as jnp
from jax import lax
from jax.experimental import pallas as pl
from jax.experimental.pallas import tpu as pltpu
from jax.sharding import PartitionSpec as P

D = 1536
HD = 64
E = 16
CAP = 256
CUTS = 4
MESH = pl.DeviceIdType.MESH


EPS = 1e-05


def deal_tables(deal_order, expert_ids, block):
    groups = lax.axis_size("dp")
    parts = lax.axis_size("mp")
    me_index = lax.axis_index("dp")
    part_index = lax.axis_index("mp")
    shard = block // parts
    own = (me_index * parts + part_index) * shard + jnp.arange(shard, dtype=jnp.int32)
    spots = jnp.arange(deal_order.shape[0], dtype=jnp.int32)
    dealt = jnp.sum(jnp.where(deal_order[:, None] == own[None, :], spots[:, None], 0), axis=0)
    home = jnp.sum((dealt[:, None] < dealt[None, :]).astype(jnp.int32), axis=0)
    mine = lax.dynamic_slice_in_dim(deal_order, me_index * block, block, 0)
    anchor = (mine % block) // shard * groups + mine // block
    key = anchor * block + jnp.arange(block, dtype=jnp.int32)
    arrival = jnp.sum((key[:, None] < key[None, :]).astype(jnp.int32), axis=0)
    pair = expert_ids[:, 0] * E + expert_ids[:, 1]
    hits = arrival[:, None] == jnp.arange(block, dtype=jnp.int32)[None, :]
    code = jnp.sum(jnp.where(hits, pair[:, None], 0), axis=0)
    counts = jnp.sum((expert_ids.reshape(-1)[:, None] == jnp.arange(E, dtype=jnp.int32)[None, :]).astype(jnp.int32), axis=0)
    return (home, code[None, :], counts)


def segment_of(lengths, rows):
    ends = jnp.cumsum(lengths)
    places = jnp.arange(rows, dtype=jnp.int32)
    return jnp.sum((places[:, None] >= ends[None, :]).astype(jnp.int32), axis=1)


def mm(a, b, dims=((1,), (0,))):
    return lax.dot_general(a, b, (dims, ((), ())), preferred_element_type=jnp.float32)


NT = ((1,), (1,))
TN = ((0,), (0,))


def expert_step(width, start, count, refs):
    (x_all, grad_all, gate_all, dots, gate_w, up_w, down_w, gate_out, up_out, down_out) = refs
    low = jnp.bfloat16
    span = pl.ds(start, width)
    valid = lax.broadcasted_iota(jnp.int32, (width, 1), 0) < count
    gate = jnp.where(valid, gate_all[span, :], 0.0)
    x = x_all[span, :]
    grad_rows = grad_all[span, :]
    gate_part = mm(x, gate_w[...])
    up_part = mm(x, up_w[...])
    sigma = jax.nn.sigmoid(gate_part)
    hidden = (gate_part * sigma * up_part).astype(low)
    each = mm(hidden, down_w[...])
    grad_rows_wide = grad_rows.astype(jnp.float32)
    dots[span, :] = jnp.sum(grad_rows_wide * each, axis=1, keepdims=True)
    grad_each = (grad_rows_wide * gate).astype(low)
    grad_all[span, :] = jnp.where(valid, (each * gate).astype(low), grad_rows)
    grad_hidden = mm(grad_each, down_w[...], NT)
    grad_gate = (grad_hidden * up_part * sigma * (1.0 + gate_part * (1.0 - sigma))).astype(low)
    grad_up = (grad_hidden * gate_part * sigma).astype(low)
    down_grad = mm(hidden, grad_each, TN).astype(low)
    high, wide = down_grad.shape
    subs, rows = down_out.shape[2], high // 4 // down_out.shape[2]
    for chunk in range(4):
        for sub in range(subs):
            row = (chunk * subs + sub) * rows
            for column in range(wide // high):
                down_out[0, chunk, sub, column * rows : (column + 1) * rows, :] = down_grad[
                    row : row + rows, column * high : (column + 1) * high
                ]
    gate_out[0] = mm(x, grad_gate, TN).astype(low)
    up_out[0] = mm(x, grad_up, TN).astype(low)
    back_rows = mm(grad_gate, gate_w[...], NT) + mm(grad_up, up_w[...], NT)
    x_all[span, :] = jnp.where(valid, back_rows.astype(low), x)


def expert_kernel(counts, starts, code, base, router, second, grad, gate_w, up_w, down_w,
                  mixed_out, back_out, gate_out, up_out, down_out, router_out,
                  slot, gates, x_all, grad_all, gate_all, dots, gate_held, up_held, down_held, load_sem):
    e = pl.program_id(0)
    depth = gate_held.shape[0]

    def load(expert):
        place = lax.rem(expert, depth)
        return [
            pltpu.make_async_copy(source.at[expert], held.at[place], load_sem.at[place, number])
            for number, (source, held) in enumerate(((gate_w, gate_held), (up_w, up_held), (down_w, down_held)))
        ]

    @pl.when(e == 0)
    def _():
        for expert in range(depth):
            for copy in load(expert):
                copy.start()

    rows = second.shape[0]
    low = jnp.bfloat16
    tile = CAP
    tiles = x_all.shape[0] // tile - 1
    expert = lax.broadcasted_iota(jnp.int32, (E, rows), 0)
    picks = [jnp.where(expert == ids, 1.0, 0.0) for ids in (code[...] // E, code[...] % E)]
    own = lambda pick, values: jnp.sum(pick * values, axis=0, keepdims=True)

    @pl.when(e == 0)
    def _():
        logits = mm(router[...], second[...], NT)
        chosen = [own(pick, logits) for pick in picks]
        top = jnp.maximum(chosen[0], chosen[1])
        raised = [jnp.exp(value - top) for value in chosen]
        total = raised[0] + raised[1]
        earlier = lax.broadcasted_iota(jnp.int32, (rows, rows), 0) < lax.broadcasted_iota(
            jnp.int32, (rows, rows), 1
        )
        before = mm((picks[0] + picks[1]).astype(low), jnp.where(earlier, 1.0, 0.0).astype(low)) + base[...]
        for k in (0, 1):
            gates[k : k + 1, :] = raised[k] / total
            slot[k : k + 1, :] = own(picks[k], before)

        def pick_tile(number, _):
            span = pl.ds(pl.multiple_of(number * tile, tile), tile)
            place = (lax.broadcasted_iota(jnp.int32, (tile, rows), 0) + number * tile).astype(jnp.float32)
            hits = [place == slot[k : k + 1, :] for k in (0, 1)]
            pick = jnp.where(hits[0] | hits[1], 1.0, 0.0).astype(low)
            scaled = jnp.where(hits[0], gates[0:1, :], 0.0) + jnp.where(hits[1], gates[1:2, :], 0.0)
            gate_all[span, :] = jnp.sum(scaled, axis=1, keepdims=True)
            x_all[span, :] = mm(pick, second[...]).astype(low)
            grad_all[span, :] = mm(pick, grad[...]).astype(low)
            return 0

        lax.fori_loop(0, tiles, pick_tile, 0)
        x_all[tiles * tile :, :] = jnp.zeros((tile, D), low)
        grad_all[tiles * tile :, :] = jnp.zeros((tile, D), low)
        gate_all[tiles * tile :, :] = jnp.zeros((tile, 1), jnp.float32)

    held = [ref.at[lax.rem(e, depth)] for ref in (gate_held, up_held, down_held)]
    refs = (x_all, grad_all, gate_all, dots, *held, gate_out, up_out, down_out)
    for copy in load(e):
        copy.wait()
    count = counts[e]
    start = pl.multiple_of(starts[e], 16)
    widths = (CAP // 2, CAP)
    for less, width in zip((-1,) + widths, widths):

        @pl.when((count > less) & (count <= width))
        def _(width=width):
            expert_step(width, start, count, refs)

    @pl.when(e + depth < E)
    def _():
        for copy in load(e + depth):
            copy.start()

    @pl.when(e == E - 1)
    def _():
        def dots_tile(number, totals):
            span = pl.ds(pl.multiple_of(number * tile, tile), tile)
            place = (lax.broadcasted_iota(jnp.int32, (tile, rows), 0) + number * tile).astype(jnp.float32)
            return tuple(
                totals[k] + jnp.sum(jnp.where(place == slot[k : k + 1, :], dots[span, :], 0.0), axis=0, keepdims=True)
                for k in (0, 1)
            )

        zero = jnp.zeros((1, rows), jnp.float32)
        grad_gates = lax.fori_loop(0, tiles, dots_tile, (zero, zero))
        shares = [gates[k : k + 1, :] for k in (0, 1)]
        inner = shares[0] * grad_gates[0] + shares[1] * grad_gates[1]
        grad_logits = picks[0] * (shares[0] * (grad_gates[0] - inner)) + picks[1] * (
            shares[1] * (grad_gates[1] - inner)
        )
        router_grad = mm(grad_logits.astype(low), second[...])
        for owner in range(router_out.shape[0]):
            span = router_out.shape[2]
            router_out[owner] = router_grad[:, owner * span : (owner + 1) * span]
        columns = jnp.transpose(jnp.concatenate([slot[...], grad_logits], axis=0))
        block = rows // 4
        place = lax.broadcasted_iota(jnp.int32, (block, tiles * tile), 1).astype(jnp.float32)
        for number in range(4):
            part = columns[number * block : (number + 1) * block, :]
            hit = (place == part[:, 0:1]) | (place == part[:, 1:2])
            put = jnp.where(hit, 1.0, 0.0).astype(low)
            span = pl.ds(number * block, block)
            mixed_out[span, :] = mm(put, grad_all[: tiles * tile, :]).astype(low)
            routed = mm(part[:, 8:].astype(low), router[...])
            back_out[span, :] = (mm(put, x_all[: tiles * tile, :]) + routed).astype(low)


def experts(groups, second, grad, code, counts, router, gate_w, up_w, down_w):
    per = E // groups
    rows = second.shape[0]
    hidden = gate_w.shape[2]
    low = jnp.bfloat16
    taken = (counts + 15) // 16 * 16
    starts = jnp.cumsum(taken) - taken
    packed = -(-(2 * rows + 16 * E) // CAP) * CAP + CAP
    whole = lambda e, *_: (0, 0)
    by_expert = lambda e, *_: (e, 0, 0)
    wide = pl.BlockSpec((1, D, hidden), by_expert)
    depth = 4
    block = pl.BlockSpec((rows, D), whole, pipeline_mode=pl.Buffered(1))
    out = pl.BlockSpec((rows, D), whole, pipeline_mode=pl.Buffered(1))
    return pl.pallas_call(
        expert_kernel,
        grid_spec=pltpu.PrefetchScalarGridSpec(
            num_scalar_prefetch=2,
            grid=(E,),
            in_specs=[
                pl.BlockSpec((1, rows), whole),
                pl.BlockSpec((E, 1), whole),
                pl.BlockSpec((E, D), whole),
                block,
                block,
                *[pl.BlockSpec(memory_space=pl.ANY)] * 3,
            ],
            out_specs=[
                out,
                out,
                wide,
                wide,
                pl.BlockSpec((1, 4, 4 // per, D // groups, hidden), lambda e, *_: (e // per, 0, e % per, 0, 0)),
                pl.BlockSpec((groups, E, D // groups), lambda e, *_: (0, 0, 0)),
            ],
            scratch_shapes=[
                pltpu.VMEM((8, rows), jnp.float32),
                pltpu.VMEM((8, rows), jnp.float32),
                pltpu.VMEM((packed, D), low),
                pltpu.VMEM((packed, D), low),
                pltpu.VMEM((packed, 1), jnp.float32),
                pltpu.VMEM((packed, 1), jnp.float32),
                pltpu.VMEM((depth, D, hidden), low),
                pltpu.VMEM((depth, D, hidden), low),
                pltpu.VMEM((depth, hidden, D), low),
                pltpu.SemaphoreType.DMA((depth, 3)),
            ],
        ),
        out_shape=[
            jax.ShapeDtypeStruct((rows, D), low),
            jax.ShapeDtypeStruct((rows, D), low),
            jax.ShapeDtypeStruct((E, D, hidden), low),
            jax.ShapeDtypeStruct((E, D, hidden), low),
            jax.ShapeDtypeStruct((groups, 4, 4, D // groups, hidden), low),
            jax.ShapeDtypeStruct((groups, E, D // groups), jnp.float32),
        ],
        compiler_params=pltpu.CompilerParams(
            dimension_semantics=("arbitrary",), vmem_limit_bytes=58 * 2**20
        ),
        cost_estimate=pl.CostEstimate(
            flops=2 * rows * D * (18 * hidden + 8 * rows),
            bytes_accessed=12 * E * D * hidden + 8 * rows * D,
            transcendentals=2 * rows * hidden,
        ),
    )(counts, starts, code, starts.astype(jnp.float32)[:, None], router, second, grad, gate_w, up_w, down_w)


class CubeGather:
    def __init__(self, groups, chunks, block, place, sems):
        self.bits = groups.bit_length() - 2
        self.chunks, self.block, self.place = chunks, block, place
        self.out_sem, self.in_sem, self.pair_out, self.pair_in, self.own_sem = sems
        self.me = lax.axis_index("dp")
        self.waits = []

    def flip(self, index, mask):
        for bit in range(self.bits + 1):
            if mask >> bit & 1:
                index = index + (1 << bit) * (1 - 2 * ((index // (1 << bit)) % 2))
        return index

    def send(self, chunk, have, bit, source):
        slot = have * self.bits + bit
        copy = pltpu.make_async_remote_copy(
            src_ref=source,
            dst_ref=self.place(chunk, self.flip(self.me, have << 1)),
            send_sem=self.out_sem.at[chunk, slot],
            recv_sem=self.in_sem.at[chunk, have ^ (1 << bit)],
            device_id={"dp": self.flip(self.me, 2 << bit)},
            device_id_type=MESH,
        )
        copy.start()
        self.waits.append(copy.wait_send)

    def pair(self, chunk, have, source):
        copy = pltpu.make_async_remote_copy(
            src_ref=source,
            dst_ref=self.place(chunk, self.flip(self.me, have << 1)),
            send_sem=self.pair_out.at[chunk, have],
            recv_sem=self.pair_in.at[chunk, have],
            device_id={"dp": self.flip(self.me, 1)},
            device_id_type=MESH,
        )
        copy.start()
        self.waits.append(copy.wait_send)

    def arrived(self, chunk, have, sem):
        ref = self.place(chunk, self.flip(self.me, have))
        pltpu.make_async_copy(ref, ref, sem).wait()

    def begin(self, chunk):
        for step in range(self.bits):
            self.send(chunk, 0, (chunk + step) % self.bits, self.block(chunk))
        self.pair(chunk, 0, self.block(chunk))
        copy = pltpu.make_async_copy(self.block(chunk), self.place(chunk, self.me), self.own_sem.at[chunk])
        copy.start()
        self.waits.append(copy.wait)

    def events(self):
        found = []
        for have in range(1, 1 << self.bits):
            for chunk in range(self.chunks):
                order = [(chunk + step) % self.bits for step in range(self.bits)]
                last = max(step for step, bit in enumerate(order) if have >> bit & 1)
                found.append((bin(have).count("1"), chunk, have, order[last + 1 :]))

        def event(chunk, have, later):
            self.arrived(chunk, have << 1, self.in_sem.at[chunk, have])
            source = self.place(chunk, self.flip(self.me, have << 1))
            for bit in later:
                self.send(chunk, have, bit, source)
            self.pair(chunk, have, source)

        return [functools.partial(event, *item[1:]) for item in sorted(found)]

    def finish(self):
        for chunk in range(self.chunks):
            for have in range(1 << self.bits):
                self.arrived(chunk, (have << 1) + 1, self.pair_in.at[chunk, have])
        for wait in self.waits:
            wait()


def cube_sems(groups, chunks):
    bits = groups.bit_length() - 2
    dma = pltpu.SemaphoreType.DMA
    return [
        dma((chunks, bits << bits)),
        dma((chunks, 1 << bits)),
        dma((chunks, 1 << bits)),
        dma((chunks, 1 << bits)),
        dma((chunks,)),
    ]


class LineGather:
    def __init__(self, parts, chunks, held, out_sem, in_sem):
        self.parts, self.chunks, self.held = parts, chunks, held
        self.out_sem, self.in_sem = out_sem, in_sem
        self.me = lax.axis_index("mp")
        self.rows = held.shape[1] // chunks

    def copy(self, origin, chunk, way):
        piece = self.held.at[origin, pl.ds(chunk * self.rows, self.rows)]
        return pltpu.make_async_remote_copy(
            src_ref=piece,
            dst_ref=piece,
            send_sem=self.out_sem.at[way, origin, chunk],
            recv_sem=self.in_sem.at[origin, chunk],
            device_id={"mp": self.me + 2 * way - 1},
            device_id_type=MESH,
        )

    def on_way(self, way, do):
        pl.when(self.me > 0 if way == 0 else self.me < self.parts - 1)(do)

    def begin(self, chunk):
        for way in (0, 1):
            self.on_way(way, lambda way=way: self.copy(self.me, chunk, way).start())

    def step(self, distance, way, chunk):
        origin = self.me + distance * (1 - 2 * way)

        @pl.when((origin >= 0) & (origin < self.parts))
        def _():
            self.copy(origin, chunk, way).wait_recv()
            self.on_way(way, lambda: self.copy(origin, chunk, way).start())

    def from_side(self, distance, way, do):
        origin = self.me + distance * (1 - 2 * way)
        pl.when((origin >= 0) & (origin < self.parts))(lambda: do(origin))

    def finish(self):
        for way in (0, 1):
            for distance in range(self.parts):
                origin = self.me + distance * (1 - 2 * way)
                here = (origin >= 0) & (origin < self.parts)
                there = (self.me > 0) if way == 0 else (self.me < self.parts - 1)

                @pl.when(here & there)
                def _():
                    for chunk in range(self.chunks):
                        self.copy(origin, chunk, way).wait_send()


class LineSum:
    def __init__(self, parts, chunks, held, come, out_sem, in_sem):
        self.parts, self.chunks, self.held, self.come = parts, chunks, held, come
        self.out_sem, self.in_sem = out_sem, in_sem
        self.me = lax.axis_index("mp")
        self.rows = held.shape[1] // chunks

    def slot(self, way, target, device):
        return target + (self.parts - target) * ((target == device) & (way == 0)).astype(jnp.int32)

    def copy(self, target, chunk):
        way = (target > self.me).astype(jnp.int32)
        slot = self.slot(way, target, self.me + 2 * way - 1)
        span = pl.ds(chunk * self.rows, self.rows)
        return pltpu.make_async_remote_copy(
            src_ref=self.held.at[target, span],
            dst_ref=self.come.at[slot, span],
            send_sem=self.out_sem.at[target, chunk],
            recv_sem=self.in_sem.at[slot, chunk],
            device_id={"mp": self.me + 2 * way - 1},
            device_id_type=MESH,
        )

    def come_in(self, slot, chunk):
        piece = self.come.at[slot, pl.ds(chunk * self.rows, self.rows)]
        pltpu.make_async_copy(piece, piece, self.in_sem.at[slot, chunk]).wait()

    def turned(self, target):
        right = (2 * self.me >= self.parts).astype(jnp.int32)
        return target + right * (self.parts - 1 - 2 * target)

    def begin(self, target):
        end = ((target < self.me) & (self.me == self.parts - 1)) | ((target > self.me) & (self.me == 0))

        @pl.when(end)
        def _():
            for chunk in range(self.chunks):
                self.copy(target, chunk).start()

    def relay(self, target, chunk):
        between = ((target < self.me) & (self.me < self.parts - 1)) | ((target > self.me) & (self.me > 0))

        @pl.when(between)
        def _():
            span = pl.ds(chunk * self.rows, self.rows)
            self.come_in(target, chunk)
            self.held[target, span, :] = self.held[target, span, :] + self.come[target, span, :]
            self.copy(target, chunk).start()

    def total(self, chunk, out):
        span = pl.ds(chunk * self.rows, self.rows)
        out[span, :] = self.held[self.me, span, :].astype(jnp.float32)
        for slot, there in ((self.parts, self.me < self.parts - 1), (self.me, self.me > 0)):

            @pl.when(there)
            def _():
                self.come_in(slot, chunk)
                out[span, :] = out[span, :] + self.come[slot, span, :].astype(jnp.float32)

    def finish(self):
        for target in range(self.parts):

            @pl.when(self.me != target)
            def _():
                for chunk in range(self.chunks):
                    self.copy(target, chunk).wait_send()


class Exchange:
    def __init__(self, groups, source, held, out_sem, in_sem):
        self.groups, self.source, self.held = groups, source, held
        self.out_sem, self.in_sem = out_sem, in_sem
        self.me = lax.axis_index("dp")
        self.rows = source.shape[0] // groups

    def copy(self, turn):
        peer = lax.rem(self.me + turn, self.groups)
        return pltpu.make_async_remote_copy(
            src_ref=self.source.at[pl.ds(peer * self.rows, self.rows)],
            dst_ref=self.held.at[pl.ds(self.me * self.rows, self.rows)],
            send_sem=self.out_sem.at[turn],
            recv_sem=self.in_sem.at[turn],
            device_id={"dp": peer},
            device_id_type=MESH,
        )

    def begin(self):
        for turn in range(1, self.groups):
            self.copy(turn).start()
        span = pl.ds(pl.multiple_of(self.me * self.rows, self.rows), self.rows)
        self.held[span, :] = self.source[span, :]

    def arrive(self):
        for turn in range(1, self.groups):
            self.copy(turn).wait_recv()

    def finish(self):
        for turn in range(1, self.groups):
            self.copy(turn).wait_send()


def row_type(rows):
    return jnp.bfloat16 if rows % 16 == 0 else jnp.float32


def greet(groups, parts):
    barrier = pltpu.get_barrier_semaphore()
    for axis, size in (("dp", groups), ("mp", parts)):
        for turn in range(1, size):
            peer = lax.rem(lax.axis_index(axis) + turn, size)
            pl.semaphore_signal(barrier, inc=1, device_id={axis: peer}, device_id_type=MESH)
    pl.semaphore_wait(barrier, groups + parts - 2)


def far_first(parts):
    return sorted(range(parts), key=lambda t: (-abs(2 * t - parts + 1), -t))


def scale_of(values):
    return lax.rsqrt(jnp.mean(values * values, axis=1, keepdims=True) + EPS)


def sorting(home, rows):
    place = lax.broadcasted_iota(jnp.int32, (rows, rows), 0)
    return jnp.where(place == home, 1.0, 0.0).astype(jnp.bfloat16)


def bias_of(seg_row, seg_col, start, low, stop):
    span = stop - start
    query = lax.broadcasted_iota(jnp.int32, (span, stop - low), 0) + start
    key = lax.broadcasted_iota(jnp.int32, (span, stop - low), 1) + low
    same = seg_col[start:stop, :] == seg_row[:, low:stop]
    return jnp.where(same & (key <= query), 0.0, -1e30)


def forward_kernel(groups, parts, heads, heads_kv, home, seg_row, seg_col, attn_gain, moe_gain, tokens, out_grad, wpack,
                   gate_in, up_in, down_in,
                   middle, router_out, first_out, qkv_out, mix_out, weights_out, second_out, grad_out, gate_full, up_full, down_full,
                   first, second, grad, weights, qkv, mix, part, come, bias, sorted_second, sorted_grad, dealt_second, dealt_grad,
                   wide_load, tall_load, gate_low, up_low, down_low,
                   gather_sems, moe_sems, line_out, line_in, sum_out, sum_in, deal_out, deal_in, save_sem, load_sem):
    low = jnp.bfloat16
    shard, width = tokens.shape
    me, place = lax.axis_index("dp"), lax.axis_index("mp")
    share = heads // heads_kv
    block = wpack.shape[0]
    cut = block // 2
    saves = []

    def save(number, source, target):
        copy = pltpu.make_async_copy(source, target, save_sem.at[number])
        copy.start()
        saves.append(copy)

    greet(groups, parts)
    gather = CubeGather(
        groups,
        2,
        lambda chunk: wpack.at[pl.ds(chunk * cut, cut)],
        lambda chunk, owner: weights.at[pl.ds(owner * block + chunk * cut, cut)],
        gather_sems,
    )
    for chunk in range(2):
        gather.begin(chunk)
    values = tokens[...]
    first[place] = (values * scale_of(values) * attn_gain[...][None, :]).astype(low)
    lines = [LineGather(parts, CUTS, held, line_out.at[n], line_in.at[n]) for n, held in enumerate((first, grad, second))]
    for chunk in range(CUTS):
        lines[0].begin(chunk)
    sort = sorting(home[...], shard)
    sorted_grad[...] = mm(sort, out_grad[...].astype(low)).astype(sorted_grad.dtype)
    deal_grad = Exchange(groups, sorted_grad, dealt_grad, deal_out.at[0], deal_in.at[0])
    deal_grad.begin()
    events = gather.events()
    for event in events[: 2 * gather.bits]:
        event()
    for chunk in range(CUTS):
        for way in (0, 1):
            lines[0].step(1, way, chunk)
    for event in events[2 * gather.bits :]:
        event()
    gather.finish()

    count = gate_in.shape[0] // 4
    per, hidden, _ = down_in.shape
    high = hidden // 4

    def place_of(chunk, owner):
        if chunk < 2 * count:
            full = (gate_full, up_full)[chunk // count]
            return full.at[pl.ds(chunk % count * 4, 4), pl.ds(owner * block, block)]
        return down_full.at[pl.ds(owner * per, per), pl.ds((chunk - 2 * count) * high, high)]

    def block_of(chunk, arrays):
        if chunk < 2 * count:
            return arrays[chunk // count].at[pl.ds(chunk % count * 4, 4)]
        return arrays[2].at[:, pl.ds((chunk - 2 * count) * high, high)]

    moe = CubeGather(groups, 2 * count + 4, lambda chunk: block_of(chunk, (gate_low, up_low, down_low)), place_of, moe_sems)

    def load(chunk):
        held = (wide_load if chunk < 2 * count else tall_load).at[chunk % 2]
        copy = pltpu.make_async_copy(block_of(chunk, (gate_in, up_in, down_in)), held, load_sem.at[chunk % 2])
        copy.start()
        return copy, held

    loaded = [load(0)]

    def cast(chunk):
        if chunk + 1 < moe.chunks:
            loaded.append(load(chunk + 1))
        copy, held = loaded[chunk]
        copy.wait()
        target = block_of(chunk, (gate_low, up_low, down_low))

        def row(index, _):
            target[index] = held[index].astype(low)
            return 0

        lax.fori_loop(0, held.shape[0], row, 0)
        moe.begin(chunk)

    events = moe.events()
    cast(0)
    save(0, weights.at[:, : weights_out.shape[1]], weights_out)
    router = weights[:, weights_out.shape[1] :].astype(jnp.float32)
    router_out[...] = jnp.transpose(router)[:E, :].astype(low)

    def project(origin):
        result = mm(first[origin], weights[:, : (heads + 2 * heads_kv) * HD])
        span = pl.ds(pl.multiple_of(origin * shard, shard), shard)
        for head in range(heads + 2 * heads_kv):
            qkv[head, span, :] = result[:, head * HD : (head + 1) * HD].astype(low)

    turns = [(distance, chunk) for distance in range(2, parts) for chunk in range(CUTS)]
    done = 1
    for number, (distance, chunk) in enumerate(turns):
        if distance == parts - 1 and chunk == 0:
            deal_grad.arrive()
            grad[place] = dealt_grad[...].astype(low)
            for piece in range(CUTS):
                lines[1].begin(piece)
        for way in (0, 1):
            lines[0].step(distance, way, chunk)
        while done < moe.chunks and done * len(turns) <= (number + 1) * moe.chunks:
            cast(done)
            done += 1
        if number == 0:
            project(place)
        if chunk == CUTS - 1:
            for way in (0, 1):
                lines[0].from_side(distance - 1, way, project)
    for way in (0, 1):
        lines[0].from_side(parts - 1, way, project)
    save(1, first, first_out)
    save(2, qkv, qkv_out)

    sums = LineSum(parts, CUTS, part, come, sum_out, sum_in)
    order = far_first(parts)
    reach = -(-512 // shard)
    for number, target in enumerate(order):
        start, stop = target * shard, (target + 1) * shard
        bottom = max(0, target - reach) * shard
        bias[:, : stop - bottom] = bias_of(seg_row, seg_col, start, bottom, stop)

        def attend(head, _):
            group = head // share
            keys = qkv[heads + group, bottom:stop, :]
            scores = mm(qkv[head, start:stop, :], keys, NT) * HD**-0.5 + bias[:, : stop - bottom]
            raised = jnp.exp(scores - jnp.max(scores, axis=1, keepdims=True))
            probs = (raised * (1.0 / jnp.sum(raised, axis=1, keepdims=True))).astype(low)
            mix[head, start:stop, :] = mm(probs, qkv[heads + heads_kv + group, bottom:stop, :]).astype(low)
            return 0

        lax.fori_loop(0, heads, attend, 0)
        flat = jnp.concatenate([mix[head, start:stop, :] for head in range(heads)], axis=1)
        part[target] = mm(flat, weights[:, (heads + 2 * heads_kv) * HD : weights_out.shape[1]], NT).astype(low)
        sums.begin(target)
    save(3, mix, mix_out)
    for number, target in enumerate(order):
        for chunk in range(CUTS):
            if number < parts - 1:
                for way in (0, 1):
                    lines[1].step(number + 1, way, chunk)
            sums.relay(sums.turned(target), chunk)
    for chunk in range(CUTS):
        sums.total(chunk, middle)
    values = tokens[...] + middle[...]
    middle[...] = values
    normed = (values * scale_of(values) * moe_gain[...][None, :]).astype(low)
    sorted_second[...] = mm(sort, normed).astype(sorted_second.dtype)
    deal = Exchange(groups, sorted_second, dealt_second, deal_out.at[1], deal_in.at[1])
    deal.begin()
    save(4, grad, grad_out)
    singles = moe.bits * moe.chunks
    for event in events[:singles]:
        event()
    deal.arrive()
    second[place] = dealt_second[...].astype(low)
    for chunk in range(CUTS):
        lines[2].begin(chunk)
    rest = events[singles:]
    turns = (parts - 1) * CUTS
    for turn in range(turns):
        for way in (0, 1):
            lines[2].step(1 + turn // CUTS, way, turn % CUTS)
        for event in rest[turn * len(rest) // turns : (turn + 1) * len(rest) // turns]:
            event()
    save(5, second, second_out)
    moe.finish()
    for line in lines:
        line.finish()
    sums.finish()
    deal_grad.finish()
    deal.finish()
    for copy in saves:
        copy.wait()


def forward(groups, parts, home, seg, attn_gain, moe_gain, tokens, out_grad, wpack, w_gate, w_up, w_down, heads, heads_kv):
    shard, width = tokens.shape
    rows = shard * parts
    low = jnp.bfloat16
    slots = heads + 2 * heads_kv
    columns = wpack.shape[1]
    block, hidden = w_gate.shape[1:]
    per = w_down.shape[0]
    chunks = 2 * (E // 4) + 4
    vmem = pl.BlockSpec(memory_space=pltpu.VMEM)
    hbm = pl.BlockSpec(memory_space=pl.ANY)
    dma = pltpu.SemaphoreType.DMA
    held = lambda: pltpu.VMEM((parts, shard, width), low)
    return pl.pallas_call(
        functools.partial(forward_kernel, groups, parts, heads, heads_kv),
        in_specs=[vmem] * 7 + [hbm] * 4,
        out_specs=[vmem] * 2 + [hbm] * 9,
        out_shape=[
            jax.ShapeDtypeStruct((shard, width), jnp.float32),
            jax.ShapeDtypeStruct((E, width), low),
            jax.ShapeDtypeStruct((parts, shard, width), low),
            jax.ShapeDtypeStruct((slots, rows, HD), low),
            jax.ShapeDtypeStruct((heads, rows, HD), low),
            jax.ShapeDtypeStruct((width, columns - 128), low),
            jax.ShapeDtypeStruct((parts, shard, width), low),
            jax.ShapeDtypeStruct((parts, shard, width), low),
            jax.ShapeDtypeStruct((E, width, hidden), low),
            jax.ShapeDtypeStruct((E, width, hidden), low),
            jax.ShapeDtypeStruct((E, hidden, width), low),
        ],
        scratch_shapes=[
            held(),
            held(),
            held(),
            pltpu.VMEM((width, columns), low),
            pltpu.VMEM((slots, rows, HD), low),
            pltpu.VMEM((heads, rows, HD), low),
            held(),
            pltpu.VMEM((parts + 1, shard, width), low),
            pltpu.VMEM((shard, shard * (1 - (-512 // shard))), jnp.float32),
            *[pltpu.VMEM((shard, width), row_type(shard // groups))] * 4,
            pltpu.VMEM((2, 4, block, hidden), jnp.float32),
            pltpu.VMEM((2, per, hidden // 4, width), jnp.float32),
            pltpu.VMEM((E, block, hidden), low),
            pltpu.VMEM((E, block, hidden), low),
            pltpu.VMEM((per, hidden, width), low),
            cube_sems(groups, 2),
            cube_sems(groups, chunks),
            dma((3, 2, parts, CUTS)),
            dma((3, parts, CUTS)),
            dma((parts, CUTS)),
            dma((parts + 1, CUTS)),
            dma((2, groups)),
            dma((2, groups)),
            dma((6,)),
            dma((2,)),
        ],
        compiler_params=pltpu.CompilerParams(
            collective_id=0, has_side_effects=True, vmem_limit_bytes=56 * 2**20
        ),
        cost_estimate=pl.CostEstimate(
            flops=12 * rows * width * columns, bytes_accessed=60 * 2**20, transcendentals=rows * rows * heads
        ),
    )(home, seg[None, :], seg[:, None], attn_gain, moe_gain, tokens, out_grad, wpack,
      w_gate, w_up, w_down)


class CubeSum:
    def __init__(self, groups, chunks, own, pair_held, step_held, sems):
        self.bits = groups.bit_length() - 2
        self.chunks, self.own, self.pair_held, self.step_held = chunks, own, pair_held, step_held
        self.out_sem, self.in_sem, self.pair_out, self.pair_in = sems
        self.me = lax.axis_index("dp")
        self.waits = []

    def flip(self, index, mask):
        for bit in range(self.bits + 1):
            if mask >> bit & 1:
                index = index + (1 << bit) * (1 - 2 * ((index // (1 << bit)) % 2))
        return index

    def step_of(self, chunk, want):
        for step in range(self.bits):
            bit = (chunk + step) % self.bits
            if want >> bit & 1:
                return step, bit
        return self.bits, None

    def pair(self, chunk):
        for want in range(1 << self.bits):
            copy = pltpu.make_async_remote_copy(
                src_ref=self.own(chunk, self.flip(self.me, 2 * want + 1)),
                dst_ref=self.pair_held(chunk, want),
                send_sem=self.pair_out.at[chunk, want],
                recv_sem=self.pair_in.at[chunk, want],
                device_id={"dp": self.flip(self.me, 1)},
                device_id_type=MESH,
            )
            copy.start()
            self.waits.append(copy.wait_send)

    def send(self, chunk, want, source):
        step, bit = self.step_of(chunk, want)
        rest = want ^ (1 << bit)
        copy = pltpu.make_async_remote_copy(
            src_ref=source,
            dst_ref=self.step_held(chunk, step, rest),
            send_sem=self.out_sem.at[chunk, want],
            recv_sem=self.in_sem.at[chunk, step, rest],
            device_id={"dp": self.flip(self.me, 2 << bit)},
            device_id_type=MESH,
        )
        copy.start()
        return copy.wait_send

    def terms(self, chunk, want):
        found = [self.own(chunk, self.flip(self.me, 2 * want)), self.pair_held(chunk, want)]
        pltpu.make_async_copy(found[1], found[1], self.pair_in.at[chunk, want]).wait()
        for step in range(self.step_of(chunk, want)[0]):
            held = self.step_held(chunk, step, want)
            pltpu.make_async_copy(held, held, self.in_sem.at[chunk, step, want]).wait()
            found.append(held)
        return found

    def items(self, lag):
        found = []
        for chunk in range(self.chunks):
            for want in range(1 << self.bits):
                step = self.step_of(chunk, want)[0]
                found.append((chunk + lag * step, step, chunk, want))
        return [item[2:] for item in sorted(found)]

    def finish(self):
        for wait in self.waits:
            wait()


def sum_sems(groups, chunks):
    bits = groups.bit_length() - 2
    dma = pltpu.SemaphoreType.DMA
    return [
        dma((chunks, 1 << bits)),
        dma((chunks, bits, 1 << bits)),
        dma((chunks, 1 << bits)),
        dma((chunks, 1 << bits)),
    ]


class Stream:
    def __init__(self, cube, lag, terms, sums, totals, out, load_sem, save_sem):
        self.cube, self.terms, self.sums, self.totals, self.out = cube, terms, sums, totals, out
        self.load_sem, self.save_sem = load_sem, save_sem
        self.list = cube.items(lag)
        self.at, self.sent, self.saved, self.loads = 0, [], [], None

    def tick(self, times=1):
        for _ in range(times):
            if self.at <= len(self.list):
                loads = self.fetch(self.at) if self.at < len(self.list) else None
                if self.loads is not None:
                    self.add(self.at - 1)
                self.loads = loads
                self.at += 1

    def fetch(self, number):
        slot = number % 2
        loads = []
        for term, ref in enumerate(self.cube.terms(*self.list[number])):
            copy = pltpu.make_async_copy(ref, self.terms.at[slot, term], self.load_sem.at[slot, term])
            copy.start()
            loads.append(copy)
        return loads

    def add(self, number):
        slot = number % 2
        chunk, want = self.list[number]
        for copy in self.loads:
            copy.wait()
        count = len(self.loads)
        if want:
            place = len(self.sent) % self.sums.shape[0]
            if len(self.sent) >= self.sums.shape[0]:
                self.sent[len(self.sent) - self.sums.shape[0]]()
            target = self.sums.at[place]
        else:
            place = len(self.saved) % self.totals.shape[0]
            if len(self.saved) >= self.totals.shape[0]:
                self.saved[len(self.saved) - self.totals.shape[0]]()
            target = self.totals.at[place]

        def row(index, _):
            if count == 2:
                target[index] = self.terms[slot, 0, index] + self.terms[slot, 1, index]
                return 0
            total = self.terms[slot, 0, index].astype(jnp.float32)
            for term in range(1, count):
                total = total + self.terms[slot, term, index].astype(jnp.float32)
            target[index] = total.astype(target.dtype)
            return 0

        lax.fori_loop(0, target.shape[0], row, 0)
        if want:
            self.sent.append(self.cube.send(chunk, want, target))
        else:
            for source, result in self.out(chunk, target):
                pltpu.make_async_copy(source, result, self.save_sem.at[place]).start()
            self.saved.append(pltpu.make_async_copy(target, target, self.save_sem.at[place]).wait)

    def finish(self):
        self.tick(len(self.list) + 1 - self.at)
        for wait in self.sent[-self.sums.shape[0] :] + self.saved[-self.totals.shape[0] :]:
            wait()


class Share:
    def __init__(self, axis, size, held, out_sem, in_sem, source):
        self.axis, self.size, self.held = axis, size, held
        self.out_sem, self.in_sem, self.source = out_sem, in_sem, source
        self.me = lax.axis_index(axis)

    def copy(self, turn):
        peer = lax.rem(self.me + turn, self.size)
        return pltpu.make_async_remote_copy(
            src_ref=self.source(peer),
            dst_ref=self.held.at[self.me],
            send_sem=self.out_sem.at[turn],
            recv_sem=self.in_sem.at[turn],
            device_id={self.axis: peer},
            device_id_type=MESH,
        )

    def begin(self):
        for turn in range(1, self.size):
            self.copy(turn).start()
        self.held[self.me] = self.source(self.me)[...]

    def total(self):
        for turn in range(1, self.size):
            self.copy(turn).wait()
        total = self.held[0]
        for index in range(1, self.size):
            total = total + self.held[index]
        return total


def backward_kernel(groups, parts, heads, heads_kv, home, seg_row, seg_col, attn_gain, moe_gain, tokens, out_grad, middle,
                    router_part, back_in, mixed_in, first_in, qkv_in, mix_in, weights_in, gate_in, up_in, down_in,
                    block_out, tokens_grad, gains_out, router_out, pack_out, gate_out, up_out, down_out, pair_held, step_held,
                    held, come, mixed, mixed_come, grad, qkv, mix, weights, grad_mix, grad_query, grad_key, grad_value,
                    flat, bias, pack, pack_pair, pack_step, stage, land_back, land_mixed, terms, sums, totals,
                    router_all, router_line, gains, gains_line, gains_all,
                    load_sem, cube_sems, pack_sems, term_sem, save_sem, line_out, line_in, sum_out, sum_in, deal_out, deal_in,
                    share_out, share_in):
    low = jnp.bfloat16
    shard, width = tokens.shape
    me, place = lax.axis_index("dp"), lax.axis_index("mp")
    share = heads // heads_kv
    slots = heads + 2 * heads_kv
    bits = groups.bit_length() - 2
    arrays = ((back_in, held), (weights_in, weights), (mix_in, mix), (qkv_in, qkv), (mixed_in, mixed))
    loads = []
    for number, (source, target) in enumerate(arrays):
        loads.append(pltpu.make_async_copy(source, target, load_sem.at[number]))
        loads[-1].start()
    greet(groups, parts)

    gains[...] = jnp.zeros_like(gains)
    count = gate_in.shape[0] // 4
    owner_rows = width // groups

    def own(chunk, owner):
        if chunk < 2 * count:
            ref = (gate_in, up_in)[chunk // count]
            return ref.at[pl.ds(chunk % count * 4, 4), pl.ds(owner * owner_rows, owner_rows)]
        return down_in.at[owner, chunk - 2 * count]

    places = {}

    def step_place(chunk, step, want):
        return step_held.at[chunk, places.setdefault((chunk, step, want), len([k for k in places if k[0] == chunk]))]

    cube = CubeSum(groups, 3 * count, own, lambda chunk, want: pair_held.at[chunk, want], step_place, cube_sems)
    per, hidden, _ = down_out.shape
    subs = 4 // per
    span = hidden // 4 // subs

    def out(chunk, total):
        if chunk < 2 * count:
            return [(total, (gate_out, up_out)[chunk // count].at[pl.ds(chunk % count * 4, 4)])]
        found = []
        for index in range(4):
            row = (chunk - 2 * count) * (hidden // 4) + index % subs * span
            for column in range(width // hidden):
                source = total.at[index, pl.ds(column * span, span)]
                target = down_out.at[index // subs, pl.ds(row, span), pl.ds(column * hidden, hidden)]
                found.append((source, target))
        return found

    stream = Stream(cube, 3, terms, sums, totals, out, term_sem, save_sem)

    back = LineSum(parts, CUTS, held, come, sum_out.at[0], sum_in.at[0])
    loads[0].wait()
    order = far_first(parts)
    for target in order:
        back.begin(back.turned(target))
    for chunk in range(3 * count):
        cube.pair(chunk)
    routers = Share("dp", groups, router_all, share_out.at[0], share_in.at[0], lambda peer: router_part.at[peer])
    routers.begin()
    stream.tick(1)
    for target in order:
        for chunk in range(CUTS):
            back.relay(back.turned(target), chunk)
            stream.tick(1 if target in order[:2] else 0)
    for chunk in range(CUTS):
        back.total(chunk, block_out)
    stage[...] = block_out[...].astype(stage.dtype)
    deal = Exchange(groups, stage, land_back, deal_out.at[0], deal_in.at[0])
    deal.begin()
    back.finish()
    loads[4].wait()
    extra = LineSum(parts, CUTS, mixed, mixed_come, sum_out.at[1], sum_in.at[1])
    extra.begin(extra.turned(order[0]))
    router_line[place] = routers.total()
    router_sums = Share("mp", parts, router_line, share_out.at[1], share_in.at[1], lambda peer: router_line.at[place])
    for turn in range(1, parts):
        router_sums.copy(turn).start()
    sort = sorting(home[...], shard)
    values = middle[...]
    scale = scale_of(values)
    deal.arrive()
    grad_second = mm(sort, land_back[...].astype(low), TN)
    weighted = grad_second * moe_gain[...][None, :]
    inner = jnp.mean(weighted * values, axis=1, keepdims=True)
    gains[0:1, :] = jnp.sum(grad_second * values * scale, axis=0, keepdims=True)
    grad_middle = out_grad[...] + (scale * weighted - values * (scale * scale * scale * inner))
    tokens_grad[...] = grad_middle
    grad[place] = grad_middle.astype(low)
    line = LineGather(parts, CUTS, grad, line_out, line_in)
    for chunk in range(CUTS):
        line.begin(chunk)
    for target in order[1:]:
        extra.begin(extra.turned(target))
    loads[1].wait()

    def mix_back(origin):
        result = mm(grad[origin], weights[:, slots * HD :])
        span = pl.ds(pl.multiple_of(origin * shard, shard), shard)
        for head in range(heads):
            grad_mix[head, span, :] = result[:, head * HD : (head + 1) * HD].astype(low)

    mix_back(place)
    stream.tick(2)
    for distance in range(1, parts):
        for chunk in range(CUTS):
            for way in (0, 1):
                line.step(distance, way, chunk)
            if distance == parts - 1:
                extra.relay(extra.turned(order[0]), chunk)
            stream.tick()
        for way in (0, 1):
            line.from_side(distance, way, mix_back)
    loads[3].wait()

    first_sum = LineSum(parts, CUTS, held, come, sum_out.at[2], sum_in.at[2])
    grad_key[...] = jnp.zeros_like(grad_key)
    grad_value[...] = jnp.zeros_like(grad_value)
    reach = -(-512 // shard)
    for number, target in enumerate(reversed(range(parts))):
        start, stop = target * shard, (target + 1) * shard
        bottom = max(0, target - reach) * shard
        bias[:, : stop - bottom] = bias_of(seg_row, seg_col, start, bottom, stop)

        def attend(head, _):
            group = head // share
            query = qkv[head, start:stop, :]
            keys = qkv[heads + group, bottom:stop, :]
            scores = mm(query, keys, NT) * HD**-0.5 + bias[:, : stop - bottom]
            raised = jnp.exp(scores - jnp.max(scores, axis=1, keepdims=True))
            probs = raised * (1.0 / jnp.sum(raised, axis=1, keepdims=True))
            grad_rows = grad_mix[head, start:stop, :]
            grad_probs = mm(grad_rows, qkv[heads + heads_kv + group, bottom:stop, :], NT)
            inner = jnp.sum(probs * grad_probs, axis=1, keepdims=True)
            grad_scores = (probs * (grad_probs - inner)).astype(low)
            grad_query[head, start:stop, :] = (mm(grad_scores, keys) * HD**-0.5).astype(low)
            grad_key[group, bottom:stop, :] += mm(grad_scores, query, TN)
            grad_value[group, bottom:stop, :] += mm(probs.astype(low), grad_rows, TN)
            return 0

        lax.fori_loop(0, heads, attend, 0)
        pieces = [grad_query[head, start:stop, :] for head in range(heads)]
        pieces += [(grad_key[group, start:stop, :] * HD**-0.5).astype(low) for group in range(heads_kv)]
        pieces += [grad_value[group, start:stop, :].astype(low) for group in range(heads_kv)]
        flat[start:stop, :] = jnp.concatenate(pieces, axis=1)
        held[target] = mm(flat[start:stop, :], weights[:, : slots * HD], NT).astype(low)
        first_sum.begin(target)
        for chunk in range(CUTS):
            if number < parts - 1:
                extra.relay(extra.turned(order[number + 1]), chunk)
            stream.tick(1)
    for target in reversed(range(parts)):
        for chunk in range(CUTS):
            first_sum.relay(target, chunk)
    loads[2].wait()
    mix_flat = jnp.concatenate([mix[head] for head in range(heads)], axis=1)
    pack[:, slots * HD :] = mm(grad[...].reshape(parts * shard, width), mix_flat, TN).astype(low)
    for chunk in range(CUTS):
        extra.total(chunk, block_out)
        stream.tick()
    deal.finish()
    stage[...] = block_out[...].astype(stage.dtype)
    deal_mixed = Exchange(groups, stage, land_mixed, deal_out.at[1], deal_in.at[1])
    deal_mixed.begin()
    extra.finish()
    first_load = pltpu.make_async_copy(first_in, mixed, load_sem.at[5])
    first_load.start()
    stream.tick(2)
    first_load.wait()
    pack[:, : slots * HD] = mm(mixed[...].reshape(parts * shard, width), flat[...], TN).astype(low)
    cut = owner_rows // 2
    pack_places = {}

    def pack_place(chunk, step, want):
        return pack_step.at[chunk, pack_places.setdefault((chunk, step, want), len([k for k in pack_places if k[0] == chunk]))]

    pack_cube = CubeSum(
        groups,
        2,
        lambda chunk, owner: pack.at[pl.ds(owner * owner_rows + chunk * cut, cut)],
        lambda chunk, want: pack_pair.at[chunk, want],
        pack_place,
        pack_sems,
    )
    for chunk in range(2):
        pack_cube.pair(chunk)
    deal_mixed.arrive()
    home_rows = mm(sort, land_mixed[...].astype(low), TN)
    pack_sent = []
    for chunk, want in pack_cube.items(1):
        stream.tick(1)
        refs = pack_cube.terms(chunk, want)
        total = refs[0][...].astype(jnp.float32)
        for ref in refs[1:]:
            total = total + ref[...].astype(jnp.float32)
        if want:
            refs[0][...] = total.astype(low)
            pack_sent.append(pack_cube.send(chunk, want, refs[0]))
        else:
            pack_out[chunk * cut : (chunk + 1) * cut, :] = total
    for chunk in range(CUTS):
        first_sum.total(chunk, block_out)
    grad_first = block_out[...]
    values = tokens[...]
    scale = scale_of(values)
    weighted = grad_first * attn_gain[...][None, :]
    inner = jnp.mean(weighted * values, axis=1, keepdims=True)
    gains[1:2, :] = jnp.sum(grad_first * values * scale, axis=0, keepdims=True)
    gains_lines = Share("mp", parts, gains_line, share_out.at[2], share_in.at[2], lambda peer: gains)
    gains_lines.begin()
    tokens_grad[...] += scale * weighted - values * (scale * scale * scale * inner)
    block_out[...] = middle[...] + home_rows
    router_out[...] = router_sums.total()
    gains[...] = gains_lines.total()
    gains_rest = Share("dp", groups, gains_all, share_out.at[3], share_in.at[3], lambda peer: gains)
    gains_rest.begin()
    stream.finish()
    gains_out[...] = gains_rest.total()
    line.finish()
    first_sum.finish()
    deal_mixed.finish()
    cube.finish()
    pack_cube.finish()
    for wait in pack_sent:
        wait()


def backward(groups, parts, heads, heads_kv, home, seg, attn_gain, moe_gain, tokens, out_grad, middle, router_part,
             back, mixed, first, qkv, mix, weights, gate_grad, up_grad, down_grad):
    shard, width = tokens.shape
    rows = shard * parts
    low = jnp.bfloat16
    slots = heads + 2 * heads_kv
    columns = weights.shape[1]
    owner_rows, hidden = width // groups, gate_grad.shape[2]
    bits = groups.bit_length() - 2
    chunks = 3 * (E // 4)
    cut = owner_rows // 2
    vmem = pl.BlockSpec(memory_space=pltpu.VMEM)
    hbm = pl.BlockSpec(memory_space=pl.ANY)
    dma = pltpu.SemaphoreType.DMA
    f32 = lambda *shape: jax.ShapeDtypeStruct(shape, jnp.float32)
    unit = (4, owner_rows, hidden)
    held = pltpu.VMEM((parts, shard, width), low)
    come = pltpu.VMEM((parts + 1, shard, width), low)
    line = row_type(shard // groups)
    return pl.pallas_call(
        functools.partial(backward_kernel, groups, parts, heads, heads_kv),
        in_specs=[vmem] * 9 + [hbm] * 9,
        out_specs=[vmem] * 5 + [hbm] * 5,
        out_shape=[
            f32(shard, width),
            f32(shard, width),
            f32(8, width),
            f32(E, owner_rows),
            f32(owner_rows, columns),
            f32(E, owner_rows, hidden),
            f32(E, owner_rows, hidden),
            f32(E // groups, hidden, width),
            jax.ShapeDtypeStruct((chunks, 1 << bits, *unit), low),
            jax.ShapeDtypeStruct((chunks, (1 << bits) - 1, *unit), low),
        ],
        scratch_shapes=[
            held,
            come,
            held,
            come,
            held,
            pltpu.VMEM((slots, rows, HD), low),
            pltpu.VMEM((heads, rows, HD), low),
            pltpu.VMEM((width, columns), low),
            pltpu.VMEM((heads, rows, HD), low),
            pltpu.VMEM((heads, rows, HD), low),
            pltpu.VMEM((heads_kv, rows, HD), jnp.float32),
            pltpu.VMEM((heads_kv, rows, HD), jnp.float32),
            pltpu.VMEM((rows, slots * HD), low),
            pltpu.VMEM((shard, shard * (1 - (-512 // shard))), jnp.float32),
            pltpu.VMEM((width, columns), low),
            pltpu.VMEM((2, 1 << bits, cut, columns), low),
            pltpu.VMEM((2, (1 << bits) - 1, cut, columns), low),
            pltpu.VMEM((shard, width), line),
            pltpu.VMEM((shard, width), line),
            pltpu.VMEM((shard, width), line),
            pltpu.VMEM((2, 2 + bits, *unit), low),
            pltpu.VMEM((4, *unit), low),
            pltpu.VMEM((2, *unit), jnp.float32),
            pltpu.VMEM((groups, E, owner_rows), jnp.float32),
            pltpu.VMEM((parts, E, owner_rows), jnp.float32),
            pltpu.VMEM((8, width), jnp.float32),
            pltpu.VMEM((parts, 8, width), jnp.float32),
            pltpu.VMEM((groups, 8, width), jnp.float32),
            dma((6,)),
            sum_sems(groups, chunks),
            sum_sems(groups, 2),
            dma((2, 2 + bits)),
            dma((2,)),
            dma((2, parts, CUTS)),
            dma((parts, CUTS)),
            dma((3, parts, CUTS)),
            dma((3, parts + 1, CUTS)),
            dma((2, groups)),
            dma((2, groups)),
            dma((4, max(groups, parts))),
            dma((4, max(groups, parts))),
        ],
        compiler_params=pltpu.CompilerParams(
            collective_id=1, has_side_effects=True, vmem_limit_bytes=63 * 2**20
        ),
        cost_estimate=pl.CostEstimate(
            flops=24 * rows * width * columns, bytes_accessed=200 * 2**20, transcendentals=rows * rows * heads
        ),
    )(home, seg[None, :], seg[:, None], attn_gain, moe_gain, tokens, out_grad, middle, router_part,
      back, mixed, first, qkv, mix, weights, gate_grad, up_grad, down_grad)


def body(
    tokens,
    attn_gain,
    w_query,
    w_key,
    w_value,
    w_out,
    moe_gain,
    w_router,
    w_gate,
    w_up,
    w_down,
    seq_lengths,
    deal_order,
    expert_ids,
    out_grad,
):
    groups, parts = lax.axis_size("dp"), lax.axis_size("mp")
    rows = tokens.shape[0] * parts
    low_type = jnp.bfloat16
    heads, heads_kv = w_query.shape[1] // HD, w_key.shape[1] // HD
    wpack = jnp.concatenate(
        [w_query, w_key, w_value, w_out.T, jnp.pad(w_router, ((0, 0), (0, 128 - E)))], axis=1
    ).astype(low_type)
    home, code, counts = deal_tables(deal_order, expert_ids, rows)
    segment = segment_of(seq_lengths[0], rows)
    middle, router_w, first_full, qkv, mix, weights, second_full, grad_full, gate_w, up_w, down_w = forward(
        groups, parts, home[None, :], segment, attn_gain, moe_gain, tokens, out_grad, wpack, w_gate, w_up, w_down, heads, heads_kv
    )
    mixed, back, gate_grad, up_grad, down_grad, router_part = experts(
        groups,
        second_full.reshape(rows, D),
        grad_full.reshape(rows, D),
        code,
        counts,
        router_w,
        gate_w,
        up_w,
        down_w,
    )
    block_out, tokens_grad, gains, router_sum, pack_sum, gate_sum, up_sum, down_sum, _, _ = backward(
        groups,
        parts,
        heads,
        heads_kv,
        home[None, :],
        segment,
        attn_gain,
        moe_gain,
        tokens,
        out_grad,
        middle,
        router_part,
        back.reshape(second_full.shape),
        mixed.reshape(second_full.shape),
        first_full,
        qkv,
        mix,
        weights,
        gate_grad,
        up_grad,
        down_grad,
    )
    columns, columns_kv = heads * HD, heads_kv * HD
    return (
        block_out,
        tokens_grad,
        gains[1],
        pack_sum[:, :columns],
        pack_sum[:, columns : columns + columns_kv],
        pack_sum[:, columns + columns_kv : columns + 2 * columns_kv],
        pack_sum[:, columns + 2 * columns_kv :].T,
        gains[0],
        router_sum.T,
        gate_sum,
        up_sum,
        down_sum,
    )


def solution(mesh):
    return jax.shard_map(
        body,
        mesh=mesh,
        in_specs=(
            P(("dp", "mp"), None),
            P(),
            P("dp", "mp"),
            P("dp", "mp"),
            P("dp", "mp"),
            P("mp", "dp"),
            P(),
            P("dp", None),
            P(None, "dp", "mp"),
            P(None, "dp", "mp"),
            P("dp", "mp", None),
            P("dp", None),
            P(),
            P("dp", None),
            P(("dp", "mp"), None),
        ),
        out_specs=(
            P(("dp", "mp"), None),
            P(("dp", "mp"), None),
            P(),
            P("dp", "mp"),
            P("dp", "mp"),
            P("dp", "mp"),
            P("mp", "dp"),
            P(),
            P("dp", None),
            P(None, "dp", "mp"),
            P(None, "dp", "mp"),
            P("dp", "mp", None),
        ),
        check_vma=False,
    )
```

```python
import functools

import jax
import jax.numpy as jnp
from jax import lax
from jax.experimental import pallas as pl
from jax.experimental.pallas import tpu as pltpu
from jax.sharding import PartitionSpec as P

D = 1536
HD = 64
E = 16
CAP = 256
CUTS = 4
MESH = pl.DeviceIdType.MESH


EPS = 1e-05


def deal_tables(deal_order, expert_ids, block):
    groups = lax.axis_size("dp")
    parts = lax.axis_size("mp")
    me_index = lax.axis_index("dp")
    part_index = lax.axis_index("mp")
    shard = block // parts
    own = (me_index * parts + part_index) * shard + jnp.arange(shard, dtype=jnp.int32)
    spots = jnp.arange(deal_order.shape[0], dtype=jnp.int32)
    dealt = jnp.sum(jnp.where(deal_order[:, None] == own[None, :], spots[:, None], 0), axis=0)
    home = jnp.sum((dealt[:, None] < dealt[None, :]).astype(jnp.int32), axis=0)
    mine = lax.dynamic_slice_in_dim(deal_order, me_index * block, block, 0)
    anchor = (mine % block) // shard * groups + mine // block
    key = anchor * block + jnp.arange(block, dtype=jnp.int32)
    arrival = jnp.sum((key[:, None] < key[None, :]).astype(jnp.int32), axis=0)
    pair = expert_ids[:, 0] * E + expert_ids[:, 1]
    hits = arrival[:, None] == jnp.arange(block, dtype=jnp.int32)[None, :]
    code = jnp.sum(jnp.where(hits, pair[:, None], 0), axis=0)
    counts = jnp.sum((expert_ids.reshape(-1)[:, None] == jnp.arange(E, dtype=jnp.int32)[None, :]).astype(jnp.int32), axis=0)
    return (home, code[None, :], counts)


def segment_of(lengths, rows):
    ends = jnp.cumsum(lengths)
    places = jnp.arange(rows, dtype=jnp.int32)
    return jnp.sum((places[:, None] >= ends[None, :]).astype(jnp.int32), axis=1)


def mm(a, b, dims=((1,), (0,))):
    return lax.dot_general(a, b, (dims, ((), ())), preferred_element_type=jnp.float32)


NT = ((1,), (1,))
TN = ((0,), (0,))


def expert_step(width, start, count, refs):
    (x_all, grad_all, gate_all, dots, gate_w, up_w, down_w, gate_out, up_out, down_out) = refs
    low = jnp.bfloat16
    span = pl.ds(start, width)
    valid = lax.broadcasted_iota(jnp.int32, (width, 1), 0) < count
    gate = jnp.where(valid, gate_all[span, :], 0.0)
    x = x_all[span, :]
    grad_rows = grad_all[span, :]
    gate_part = mm(x, gate_w[...])
    up_part = mm(x, up_w[...])
    sigma = jax.nn.sigmoid(gate_part)
    hidden = (gate_part * sigma * up_part).astype(low)
    each = mm(hidden, down_w[...])
    grad_rows_wide = grad_rows.astype(jnp.float32)
    dots[span, :] = jnp.sum(grad_rows_wide * each, axis=1, keepdims=True)
    grad_each = (grad_rows_wide * gate).astype(low)
    grad_all[span, :] = jnp.where(valid, (each * gate).astype(low), grad_rows)
    grad_hidden = mm(grad_each, down_w[...], NT)
    grad_gate = (grad_hidden * up_part * sigma * (1.0 + gate_part * (1.0 - sigma))).astype(low)
    grad_up = (grad_hidden * gate_part * sigma).astype(low)
    down_grad = mm(hidden, grad_each, TN).astype(low)
    high, wide = down_grad.shape
    subs, rows = down_out.shape[2], high // 4 // down_out.shape[2]
    for chunk in range(4):
        for sub in range(subs):
            row = (chunk * subs + sub) * rows
            for column in range(wide // high):
                down_out[0, chunk, sub, column * rows : (column + 1) * rows, :] = down_grad[
                    row : row + rows, column * high : (column + 1) * high
                ]
    gate_out[0] = mm(x, grad_gate, TN).astype(low)
    up_out[0] = mm(x, grad_up, TN).astype(low)
    back_rows = mm(grad_gate, gate_w[...], NT) + mm(grad_up, up_w[...], NT)
    x_all[span, :] = jnp.where(valid, back_rows.astype(low), x)


def expert_kernel(counts, starts, code, base, router, second, grad, gate_w, up_w, down_w,
                  mixed_out, back_out, gate_out, up_out, down_out, router_out,
                  slot, gates, x_all, grad_all, gate_all, dots, gate_held, up_held, down_held, load_sem):
    e = pl.program_id(0)
    depth = gate_held.shape[0]

    def load(expert):
        place = lax.rem(expert, depth)
        return [
            pltpu.make_async_copy(source.at[expert], held.at[place], load_sem.at[place, number])
            for number, (source, held) in enumerate(((gate_w, gate_held), (up_w, up_held), (down_w, down_held)))
        ]

    @pl.when(e == 0)
    def _():
        for expert in range(depth):
            for copy in load(expert):
                copy.start()

    rows = second.shape[0]
    low = jnp.bfloat16
    tile = CAP
    tiles = x_all.shape[0] // tile - 1
    expert = lax.broadcasted_iota(jnp.int32, (E, rows), 0)
    picks = [jnp.where(expert == ids, 1.0, 0.0) for ids in (code[...] // E, code[...] % E)]
    own = lambda pick, values: jnp.sum(pick * values, axis=0, keepdims=True)

    @pl.when(e == 0)
    def _():
        logits = mm(router[...], second[...], NT)
        chosen = [own(pick, logits) for pick in picks]
        top = jnp.maximum(chosen[0], chosen[1])
        raised = [jnp.exp(value - top) for value in chosen]
        total = raised[0] + raised[1]
        earlier = lax.broadcasted_iota(jnp.int32, (rows, rows), 0) < lax.broadcasted_iota(
            jnp.int32, (rows, rows), 1
        )
        before = mm((picks[0] + picks[1]).astype(low), jnp.where(earlier, 1.0, 0.0).astype(low)) + base[...]
        for k in (0, 1):
            gates[k : k + 1, :] = raised[k] / total
            slot[k : k + 1, :] = own(picks[k], before)

        def pick_tile(number, _):
            span = pl.ds(pl.multiple_of(number * tile, tile), tile)
            place = (lax.broadcasted_iota(jnp.int32, (tile, rows), 0) + number * tile).astype(jnp.float32)
            hits = [place == slot[k : k + 1, :] for k in (0, 1)]
            pick = jnp.where(hits[0] | hits[1], 1.0, 0.0).astype(low)
            scaled = jnp.where(hits[0], gates[0:1, :], 0.0) + jnp.where(hits[1], gates[1:2, :], 0.0)
            gate_all[span, :] = jnp.sum(scaled, axis=1, keepdims=True)
            x_all[span, :] = mm(pick, second[...]).astype(low)
            grad_all[span, :] = mm(pick, grad[...]).astype(low)
            return 0

        lax.fori_loop(0, tiles, pick_tile, 0)
        x_all[tiles * tile :, :] = jnp.zeros((tile, D), low)
        grad_all[tiles * tile :, :] = jnp.zeros((tile, D), low)
        gate_all[tiles * tile :, :] = jnp.zeros((tile, 1), jnp.float32)

    held = [ref.at[lax.rem(e, depth)] for ref in (gate_held, up_held, down_held)]
    refs = (x_all, grad_all, gate_all, dots, *held, gate_out, up_out, down_out)
    for copy in load(e):
        copy.wait()
    count = counts[e]
    start = pl.multiple_of(starts[e], 16)
    widths = (CAP // 2, CAP)
    for less, width in zip((-1,) + widths, widths):

        @pl.when((count > less) & (count <= width))
        def _(width=width):
            expert_step(width, start, count, refs)

    @pl.when(e + depth < E)
    def _():
        for copy in load(e + depth):
            copy.start()

    @pl.when(e == E - 1)
    def _():
        def dots_tile(number, totals):
            span = pl.ds(pl.multiple_of(number * tile, tile), tile)
            place = (lax.broadcasted_iota(jnp.int32, (tile, rows), 0) + number * tile).astype(jnp.float32)
            return tuple(
                totals[k] + jnp.sum(jnp.where(place == slot[k : k + 1, :], dots[span, :], 0.0), axis=0, keepdims=True)
                for k in (0, 1)
            )

        zero = jnp.zeros((1, rows), jnp.float32)
        grad_gates = lax.fori_loop(0, tiles, dots_tile, (zero, zero))
        shares = [gates[k : k + 1, :] for k in (0, 1)]
        inner = shares[0] * grad_gates[0] + shares[1] * grad_gates[1]
        grad_logits = picks[0] * (shares[0] * (grad_gates[0] - inner)) + picks[1] * (
            shares[1] * (grad_gates[1] - inner)
        )
        router_grad = mm(grad_logits.astype(low), second[...])
        for owner in range(router_out.shape[0]):
            span = router_out.shape[2]
            router_out[owner] = router_grad[:, owner * span : (owner + 1) * span]
        columns = jnp.transpose(jnp.concatenate([slot[...], grad_logits], axis=0))
        block = rows // 4
        place = lax.broadcasted_iota(jnp.int32, (block, tiles * tile), 1).astype(jnp.float32)
        for number in range(4):
            part = columns[number * block : (number + 1) * block, :]
            hit = (place == part[:, 0:1]) | (place == part[:, 1:2])
            put = jnp.where(hit, 1.0, 0.0).astype(low)
            span = pl.ds(number * block, block)
            mixed_out[span, :] = mm(put, grad_all[: tiles * tile, :]).astype(low)
            routed = mm(part[:, 8:].astype(low), router[...])
            back_out[span, :] = (mm(put, x_all[: tiles * tile, :]) + routed).astype(low)


def experts(groups, second, grad, code, counts, router, gate_w, up_w, down_w):
    per = E // groups
    rows = second.shape[0]
    hidden = gate_w.shape[2]
    low = jnp.bfloat16
    taken = (counts + 15) // 16 * 16
    starts = jnp.cumsum(taken) - taken
    packed = -(-(2 * rows + 16 * E) // CAP) * CAP + CAP
    whole = lambda e, *_: (0, 0)
    by_expert = lambda e, *_: (e, 0, 0)
    wide = pl.BlockSpec((1, D, hidden), by_expert)
    depth = 4
    block = pl.BlockSpec((rows, D), whole, pipeline_mode=pl.Buffered(1))
    out = pl.BlockSpec((rows, D), whole, pipeline_mode=pl.Buffered(1))
    return pl.pallas_call(
        expert_kernel,
        grid_spec=pltpu.PrefetchScalarGridSpec(
            num_scalar_prefetch=2,
            grid=(E,),
            in_specs=[
                pl.BlockSpec((1, rows), whole),
                pl.BlockSpec((E, 1), whole),
                pl.BlockSpec((E, D), whole),
                block,
                block,
                *[pl.BlockSpec(memory_space=pl.ANY)] * 3,
            ],
            out_specs=[
                out,
                out,
                wide,
                wide,
                pl.BlockSpec((1, 4, 4 // per, D // groups, hidden), lambda e, *_: (e // per, 0, e % per, 0, 0)),
                pl.BlockSpec((groups, E, D // groups), lambda e, *_: (0, 0, 0)),
            ],
            scratch_shapes=[
                pltpu.VMEM((8, rows), jnp.float32),
                pltpu.VMEM((8, rows), jnp.float32),
                pltpu.VMEM((packed, D), low),
                pltpu.VMEM((packed, D), low),
                pltpu.VMEM((packed, 1), jnp.float32),
                pltpu.VMEM((packed, 1), jnp.float32),
                pltpu.VMEM((depth, D, hidden), low),
                pltpu.VMEM((depth, D, hidden), low),
                pltpu.VMEM((depth, hidden, D), low),
                pltpu.SemaphoreType.DMA((depth, 3)),
            ],
        ),
        out_shape=[
            jax.ShapeDtypeStruct((rows, D), low),
            jax.ShapeDtypeStruct((rows, D), low),
            jax.ShapeDtypeStruct((E, D, hidden), low),
            jax.ShapeDtypeStruct((E, D, hidden), low),
            jax.ShapeDtypeStruct((groups, 4, 4, D // groups, hidden), low),
            jax.ShapeDtypeStruct((groups, E, D // groups), jnp.float32),
        ],
        compiler_params=pltpu.CompilerParams(
            dimension_semantics=("arbitrary",), vmem_limit_bytes=58 * 2**20
        ),
        cost_estimate=pl.CostEstimate(
            flops=2 * rows * D * (18 * hidden + 8 * rows),
            bytes_accessed=12 * E * D * hidden + 8 * rows * D,
            transcendentals=2 * rows * hidden,
        ),
    )(counts, starts, code, starts.astype(jnp.float32)[:, None], router, second, grad, gate_w, up_w, down_w)


class CubeGather:
    def __init__(self, groups, chunks, block, place, sems):
        self.bits = groups.bit_length() - 2
        self.chunks, self.block, self.place = chunks, block, place
        self.out_sem, self.in_sem, self.pair_out, self.pair_in, self.own_sem = sems
        self.me = lax.axis_index("dp")
        self.waits = []

    def flip(self, index, mask):
        for bit in range(self.bits + 1):
            if mask >> bit & 1:
                index = index + (1 << bit) * (1 - 2 * ((index // (1 << bit)) % 2))
        return index

    def send(self, chunk, have, bit, source):
        slot = have * self.bits + bit
        copy = pltpu.make_async_remote_copy(
            src_ref=source,
            dst_ref=self.place(chunk, self.flip(self.me, have << 1)),
            send_sem=self.out_sem.at[chunk, slot],
            recv_sem=self.in_sem.at[chunk, have ^ (1 << bit)],
            device_id={"dp": self.flip(self.me, 2 << bit)},
            device_id_type=MESH,
        )
        copy.start()
        self.waits.append(copy.wait_send)

    def pair(self, chunk, have, source):
        copy = pltpu.make_async_remote_copy(
            src_ref=source,
            dst_ref=self.place(chunk, self.flip(self.me, have << 1)),
            send_sem=self.pair_out.at[chunk, have],
            recv_sem=self.pair_in.at[chunk, have],
            device_id={"dp": self.flip(self.me, 1)},
            device_id_type=MESH,
        )
        copy.start()
        self.waits.append(copy.wait_send)

    def arrived(self, chunk, have, sem):
        ref = self.place(chunk, self.flip(self.me, have))
        pltpu.make_async_copy(ref, ref, sem).wait()

    def begin(self, chunk):
        for step in range(self.bits):
            self.send(chunk, 0, (chunk + step) % self.bits, self.block(chunk))
        self.pair(chunk, 0, self.block(chunk))
        copy = pltpu.make_async_copy(self.block(chunk), self.place(chunk, self.me), self.own_sem.at[chunk])
        copy.start()
        self.waits.append(copy.wait)

    def events(self):
        found = []
        for have in range(1, 1 << self.bits):
            for chunk in range(self.chunks):
                order = [(chunk + step) % self.bits for step in range(self.bits)]
                last = max(step for step, bit in enumerate(order) if have >> bit & 1)
                found.append((bin(have).count("1"), chunk, have, order[last + 1 :]))

        def event(chunk, have, later):
            self.arrived(chunk, have << 1, self.in_sem.at[chunk, have])
            source = self.place(chunk, self.flip(self.me, have << 1))
            for bit in later:
                self.send(chunk, have, bit, source)
            self.pair(chunk, have, source)

        return [functools.partial(event, *item[1:]) for item in sorted(found)]

    def finish(self):
        for chunk in range(self.chunks):
            for have in range(1 << self.bits):
                self.arrived(chunk, (have << 1) + 1, self.pair_in.at[chunk, have])
        for wait in self.waits:
            wait()


def cube_sems(groups, chunks):
    bits = groups.bit_length() - 2
    dma = pltpu.SemaphoreType.DMA
    return [
        dma((chunks, bits << bits)),
        dma((chunks, 1 << bits)),
        dma((chunks, 1 << bits)),
        dma((chunks, 1 << bits)),
        dma((chunks,)),
    ]


class LineGather:
    def __init__(self, parts, chunks, held, out_sem, in_sem):
        self.parts, self.chunks, self.held = parts, chunks, held
        self.out_sem, self.in_sem = out_sem, in_sem
        self.me = lax.axis_index("mp")
        self.rows = held.shape[1] // chunks

    def copy(self, origin, chunk, way):
        piece = self.held.at[origin, pl.ds(chunk * self.rows, self.rows)]
        return pltpu.make_async_remote_copy(
            src_ref=piece,
            dst_ref=piece,
            send_sem=self.out_sem.at[way, origin, chunk],
            recv_sem=self.in_sem.at[origin, chunk],
            device_id={"mp": self.me + 2 * way - 1},
            device_id_type=MESH,
        )

    def on_way(self, way, do):
        pl.when(self.me > 0 if way == 0 else self.me < self.parts - 1)(do)

    def begin(self, chunk):
        for way in (0, 1):
            self.on_way(way, lambda way=way: self.copy(self.me, chunk, way).start())

    def step(self, distance, way, chunk):
        origin = self.me + distance * (1 - 2 * way)

        @pl.when((origin >= 0) & (origin < self.parts))
        def _():
            self.copy(origin, chunk, way).wait_recv()
            self.on_way(way, lambda: self.copy(origin, chunk, way).start())

    def from_side(self, distance, way, do):
        origin = self.me + distance * (1 - 2 * way)
        pl.when((origin >= 0) & (origin < self.parts))(lambda: do(origin))

    def finish(self):
        for way in (0, 1):
            for distance in range(self.parts):
                origin = self.me + distance * (1 - 2 * way)
                here = (origin >= 0) & (origin < self.parts)
                there = (self.me > 0) if way == 0 else (self.me < self.parts - 1)

                @pl.when(here & there)
                def _():
                    for chunk in range(self.chunks):
                        self.copy(origin, chunk, way).wait_send()


class LineSum:
    def __init__(self, parts, chunks, held, come, out_sem, in_sem):
        self.parts, self.chunks, self.held, self.come = parts, chunks, held, come
        self.out_sem, self.in_sem = out_sem, in_sem
        self.me = lax.axis_index("mp")
        self.rows = held.shape[1] // chunks

    def slot(self, way, target, device):
        return target + (self.parts - target) * ((target == device) & (way == 0)).astype(jnp.int32)

    def copy(self, target, chunk):
        way = (target > self.me).astype(jnp.int32)
        slot = self.slot(way, target, self.me + 2 * way - 1)
        span = pl.ds(chunk * self.rows, self.rows)
        return pltpu.make_async_remote_copy(
            src_ref=self.held.at[target, span],
            dst_ref=self.come.at[slot, span],
            send_sem=self.out_sem.at[target, chunk],
            recv_sem=self.in_sem.at[slot, chunk],
            device_id={"mp": self.me + 2 * way - 1},
            device_id_type=MESH,
        )

    def come_in(self, slot, chunk):
        piece = self.come.at[slot, pl.ds(chunk * self.rows, self.rows)]
        pltpu.make_async_copy(piece, piece, self.in_sem.at[slot, chunk]).wait()

    def turned(self, target):
        right = (2 * self.me >= self.parts).astype(jnp.int32)
        return target + right * (self.parts - 1 - 2 * target)

    def begin(self, target):
        end = ((target < self.me) & (self.me == self.parts - 1)) | ((target > self.me) & (self.me == 0))

        @pl.when(end)
        def _():
            for chunk in range(self.chunks):
                self.copy(target, chunk).start()

    def relay(self, target, chunk):
        between = ((target < self.me) & (self.me < self.parts - 1)) | ((target > self.me) & (self.me > 0))

        @pl.when(between)
        def _():
            span = pl.ds(chunk * self.rows, self.rows)
            self.come_in(target, chunk)
            self.held[target, span, :] = self.held[target, span, :] + self.come[target, span, :]
            self.copy(target, chunk).start()

    def total(self, chunk, out):
        span = pl.ds(chunk * self.rows, self.rows)
        out[span, :] = self.held[self.me, span, :].astype(jnp.float32)
        for slot, there in ((self.parts, self.me < self.parts - 1), (self.me, self.me > 0)):

            @pl.when(there)
            def _():
                self.come_in(slot, chunk)
                out[span, :] = out[span, :] + self.come[slot, span, :].astype(jnp.float32)

    def finish(self):
        for target in range(self.parts):

            @pl.when(self.me != target)
            def _():
                for chunk in range(self.chunks):
                    self.copy(target, chunk).wait_send()


class Exchange:
    def __init__(self, groups, source, held, out_sem, in_sem):
        self.groups, self.source, self.held = groups, source, held
        self.out_sem, self.in_sem = out_sem, in_sem
        self.me = lax.axis_index("dp")
        self.rows = source.shape[0] // groups

    def copy(self, turn):
        peer = lax.rem(self.me + turn, self.groups)
        return pltpu.make_async_remote_copy(
            src_ref=self.source.at[pl.ds(peer * self.rows, self.rows)],
            dst_ref=self.held.at[pl.ds(self.me * self.rows, self.rows)],
            send_sem=self.out_sem.at[turn],
            recv_sem=self.in_sem.at[turn],
            device_id={"dp": peer},
            device_id_type=MESH,
        )

    def begin(self):
        for turn in range(1, self.groups):
            self.copy(turn).start()
        span = pl.ds(pl.multiple_of(self.me * self.rows, self.rows), self.rows)
        self.held[span, :] = self.source[span, :]

    def arrive(self):
        for turn in range(1, self.groups):
            self.copy(turn).wait_recv()

    def finish(self):
        for turn in range(1, self.groups):
            self.copy(turn).wait_send()


def row_type(rows):
    return jnp.bfloat16 if rows % 16 == 0 else jnp.float32


def greet(groups, parts):
    barrier = pltpu.get_barrier_semaphore()
    for axis, size in (("dp", groups), ("mp", parts)):
        for turn in range(1, size):
            peer = lax.rem(lax.axis_index(axis) + turn, size)
            pl.semaphore_signal(barrier, inc=1, device_id={axis: peer}, device_id_type=MESH)
    pl.semaphore_wait(barrier, groups + parts - 2)


def far_first(parts):
    return sorted(range(parts), key=lambda t: (-abs(2 * t - parts + 1), -t))


def scale_of(values):
    return lax.rsqrt(jnp.mean(values * values, axis=1, keepdims=True) + EPS)


def sorting(home, rows):
    place = lax.broadcasted_iota(jnp.int32, (rows, rows), 0)
    return jnp.where(place == home, 1.0, 0.0).astype(jnp.bfloat16)


def bias_of(seg_row, seg_col, start, low, stop):
    span = stop - start
    query = lax.broadcasted_iota(jnp.int32, (span, stop - low), 0) + start
    key = lax.broadcasted_iota(jnp.int32, (span, stop - low), 1) + low
    same = seg_col[start:stop, :] == seg_row[:, low:stop]
    return jnp.where(same & (key <= query), 0.0, -1e30)


def forward_kernel(groups, parts, heads, heads_kv, home, seg_row, seg_col, attn_gain, moe_gain, tokens, out_grad, wpack,
                   gate_in, up_in, down_in,
                   middle, router_out, first_out, qkv_out, mix_out, weights_out, second_out, grad_out, gate_full, up_full, down_full,
                   first, second, grad, weights, qkv, mix, part, come, bias, sorted_second, sorted_grad, dealt_second, dealt_grad,
                   wide_load, tall_load, gate_low, up_low, down_low,
                   gather_sems, moe_sems, line_out, line_in, sum_out, sum_in, deal_out, deal_in, save_sem, load_sem):
    low = jnp.bfloat16
    shard, width = tokens.shape
    me, place = lax.axis_index("dp"), lax.axis_index("mp")
    share = heads // heads_kv
    block = wpack.shape[0]
    cut = block // 2
    saves = []

    def save(number, source, target):
        copy = pltpu.make_async_copy(source, target, save_sem.at[number])
        copy.start()
        saves.append(copy)

    greet(groups, parts)
    gather = CubeGather(
        groups,
        2,
        lambda chunk: wpack.at[pl.ds(chunk * cut, cut)],
        lambda chunk, owner: weights.at[pl.ds(owner * block + chunk * cut, cut)],
        gather_sems,
    )
    for chunk in range(2):
        gather.begin(chunk)
    values = tokens[...]
    first[place] = (values * scale_of(values) * attn_gain[...][None, :]).astype(low)
    lines = [LineGather(parts, CUTS, held, line_out.at[n], line_in.at[n]) for n, held in enumerate((first, grad, second))]
    for chunk in range(CUTS):
        lines[0].begin(chunk)
    sort = sorting(home[...], shard)
    sorted_grad[...] = mm(sort, out_grad[...].astype(low)).astype(sorted_grad.dtype)
    deal_grad = Exchange(groups, sorted_grad, dealt_grad, deal_out.at[0], deal_in.at[0])
    deal_grad.begin()
    events = gather.events()
    for event in events[: 2 * gather.bits]:
        event()
    for chunk in range(CUTS):
        for way in (0, 1):
            lines[0].step(1, way, chunk)
    for event in events[2 * gather.bits :]:
        event()
    gather.finish()

    count = gate_in.shape[0] // 4
    per, hidden, _ = down_in.shape
    high = hidden // 4

    def place_of(chunk, owner):
        if chunk < 2 * count:
            full = (gate_full, up_full)[chunk // count]
            return full.at[pl.ds(chunk % count * 4, 4), pl.ds(owner * block, block)]
        return down_full.at[pl.ds(owner * per, per), pl.ds((chunk - 2 * count) * high, high)]

    def block_of(chunk, arrays):
        if chunk < 2 * count:
            return arrays[chunk // count].at[pl.ds(chunk % count * 4, 4)]
        return arrays[2].at[:, pl.ds((chunk - 2 * count) * high, high)]

    moe = CubeGather(groups, 2 * count + 4, lambda chunk: block_of(chunk, (gate_low, up_low, down_low)), place_of, moe_sems)

    def load(chunk):
        held = (wide_load if chunk < 2 * count else tall_load).at[chunk % 2]
        copy = pltpu.make_async_copy(block_of(chunk, (gate_in, up_in, down_in)), held, load_sem.at[chunk % 2])
        copy.start()
        return copy, held

    loaded = [load(0)]

    def cast(chunk):
        if chunk + 1 < moe.chunks:
            loaded.append(load(chunk + 1))
        copy, held = loaded[chunk]
        copy.wait()
        target = block_of(chunk, (gate_low, up_low, down_low))

        def row(index, _):
            target[index] = held[index].astype(low)
            return 0

        lax.fori_loop(0, held.shape[0], row, 0)
        moe.begin(chunk)

    events = moe.events()
    cast(0)
    save(0, weights.at[:, : weights_out.shape[1]], weights_out)
    router = weights[:, weights_out.shape[1] :].astype(jnp.float32)
    router_out[...] = jnp.transpose(router)[:E, :].astype(low)

    def project(origin):
        result = mm(first[origin], weights[:, : (heads + 2 * heads_kv) * HD])
        span = pl.ds(pl.multiple_of(origin * shard, shard), shard)
        for head in range(heads + 2 * heads_kv):
            qkv[head, span, :] = result[:, head * HD : (head + 1) * HD].astype(low)

    turns = [(distance, chunk) for distance in range(2, parts) for chunk in range(CUTS)]
    done = 1
    for number, (distance, chunk) in enumerate(turns):
        if distance == parts - 1 and chunk == 0:
            deal_grad.arrive()
            grad[place] = dealt_grad[...].astype(low)
            for piece in range(CUTS):
                lines[1].begin(piece)
        for way in (0, 1):
            lines[0].step(distance, way, chunk)
        while done < moe.chunks and done * len(turns) <= (number + 1) * moe.chunks:
            cast(done)
            done += 1
        if number == 0:
            project(place)
        if chunk == CUTS - 1:
            for way in (0, 1):
                lines[0].from_side(distance - 1, way, project)
    for way in (0, 1):
        lines[0].from_side(parts - 1, way, project)
    save(1, first, first_out)
    save(2, qkv, qkv_out)

    sums = LineSum(parts, CUTS, part, come, sum_out, sum_in)
    order = far_first(parts)
    reach = -(-512 // shard)
    for number, target in enumerate(order):
        start, stop = target * shard, (target + 1) * shard
        bottom = max(0, target - reach) * shard
        bias[:, : stop - bottom] = bias_of(seg_row, seg_col, start, bottom, stop)

        def attend(head, _):
            group = head // share
            keys = qkv[heads + group, bottom:stop, :]
            scores = mm(qkv[head, start:stop, :], keys, NT) * HD**-0.5 + bias[:, : stop - bottom]
            raised = jnp.exp(scores - jnp.max(scores, axis=1, keepdims=True))
            probs = (raised * (1.0 / jnp.sum(raised, axis=1, keepdims=True))).astype(low)
            mix[head, start:stop, :] = mm(probs, qkv[heads + heads_kv + group, bottom:stop, :]).astype(low)
            return 0

        lax.fori_loop(0, heads, attend, 0)
        flat = jnp.concatenate([mix[head, start:stop, :] for head in range(heads)], axis=1)
        part[target] = mm(flat, weights[:, (heads + 2 * heads_kv) * HD : weights_out.shape[1]], NT).astype(low)
        sums.begin(target)
    save(3, mix, mix_out)
    for number, target in enumerate(order):
        for chunk in range(CUTS):
            if number < parts - 1:
                for way in (0, 1):
                    lines[1].step(number + 1, way, chunk)
            sums.relay(sums.turned(target), chunk)
    for chunk in range(CUTS):
        sums.total(chunk, middle)
    values = tokens[...] + middle[...]
    middle[...] = values
    normed = (values * scale_of(values) * moe_gain[...][None, :]).astype(low)
    sorted_second[...] = mm(sort, normed).astype(sorted_second.dtype)
    deal = Exchange(groups, sorted_second, dealt_second, deal_out.at[1], deal_in.at[1])
    deal.begin()
    save(4, grad, grad_out)
    singles = moe.bits * moe.chunks
    for event in events[:singles]:
        event()
    deal.arrive()
    second[place] = dealt_second[...].astype(low)
    for chunk in range(CUTS):
        lines[2].begin(chunk)
    rest = events[singles:]
    turns = (parts - 1) * CUTS
    for turn in range(turns):
        for way in (0, 1):
            lines[2].step(1 + turn // CUTS, way, turn % CUTS)
        for event in rest[turn * len(rest) // turns : (turn + 1) * len(rest) // turns]:
            event()
    save(5, second, second_out)
    moe.finish()
    for line in lines:
        line.finish()
    sums.finish()
    deal_grad.finish()
    deal.finish()
    for copy in saves:
        copy.wait()


def forward(groups, parts, home, seg, attn_gain, moe_gain, tokens, out_grad, wpack, w_gate, w_up, w_down, heads, heads_kv):
    shard, width = tokens.shape
    rows = shard * parts
    low = jnp.bfloat16
    slots = heads + 2 * heads_kv
    columns = wpack.shape[1]
    block, hidden = w_gate.shape[1:]
    per = w_down.shape[0]
    chunks = 2 * (E // 4) + 4
    vmem = pl.BlockSpec(memory_space=pltpu.VMEM)
    hbm = pl.BlockSpec(memory_space=pl.ANY)
    dma = pltpu.SemaphoreType.DMA
    held = lambda: pltpu.VMEM((parts, shard, width), low)
    return pl.pallas_call(
        functools.partial(forward_kernel, groups, parts, heads, heads_kv),
        in_specs=[vmem] * 7 + [hbm] * 4,
        out_specs=[vmem] * 2 + [hbm] * 9,
        out_shape=[
            jax.ShapeDtypeStruct((shard, width), jnp.float32),
            jax.ShapeDtypeStruct((E, width), low),
            jax.ShapeDtypeStruct((parts, shard, width), low),
            jax.ShapeDtypeStruct((slots, rows, HD), low),
            jax.ShapeDtypeStruct((heads, rows, HD), low),
            jax.ShapeDtypeStruct((width, columns - 128), low),
            jax.ShapeDtypeStruct((parts, shard, width), low),
            jax.ShapeDtypeStruct((parts, shard, width), low),
            jax.ShapeDtypeStruct((E, width, hidden), low),
            jax.ShapeDtypeStruct((E, width, hidden), low),
            jax.ShapeDtypeStruct((E, hidden, width), low),
        ],
        scratch_shapes=[
            held(),
            held(),
            held(),
            pltpu.VMEM((width, columns), low),
            pltpu.VMEM((slots, rows, HD), low),
            pltpu.VMEM((heads, rows, HD), low),
            held(),
            pltpu.VMEM((parts + 1, shard, width), low),
            pltpu.VMEM((shard, shard * (1 - (-512 // shard))), jnp.float32),
            *[pltpu.VMEM((shard, width), row_type(shard // groups))] * 4,
            pltpu.VMEM((2, 4, block, hidden), jnp.float32),
            pltpu.VMEM((2, per, hidden // 4, width), jnp.float32),
            pltpu.VMEM((E, block, hidden), low),
            pltpu.VMEM((E, block, hidden), low),
            pltpu.VMEM((per, hidden, width), low),
            cube_sems(groups, 2),
            cube_sems(groups, chunks),
            dma((3, 2, parts, CUTS)),
            dma((3, parts, CUTS)),
            dma((parts, CUTS)),
            dma((parts + 1, CUTS)),
            dma((2, groups)),
            dma((2, groups)),
            dma((6,)),
            dma((2,)),
        ],
        compiler_params=pltpu.CompilerParams(
            collective_id=0, has_side_effects=True, vmem_limit_bytes=56 * 2**20
        ),
        cost_estimate=pl.CostEstimate(
            flops=12 * rows * width * columns, bytes_accessed=60 * 2**20, transcendentals=rows * rows * heads
        ),
    )(home, seg[None, :], seg[:, None], attn_gain, moe_gain, tokens, out_grad, wpack,
      w_gate, w_up, w_down)


class CubeSum:
    def __init__(self, groups, chunks, own, pair_held, step_held, sems):
        self.bits = groups.bit_length() - 2
        self.chunks, self.own, self.pair_held, self.step_held = chunks, own, pair_held, step_held
        self.out_sem, self.in_sem, self.pair_out, self.pair_in = sems
        self.me = lax.axis_index("dp")
        self.waits = []

    def flip(self, index, mask):
        for bit in range(self.bits + 1):
            if mask >> bit & 1:
                index = index + (1 << bit) * (1 - 2 * ((index // (1 << bit)) % 2))
        return index

    def step_of(self, chunk, want):
        for step in range(self.bits):
            bit = (chunk + step) % self.bits
            if want >> bit & 1:
                return step, bit
        return self.bits, None

    def pair(self, chunk):
        for want in range(1 << self.bits):
            copy = pltpu.make_async_remote_copy(
                src_ref=self.own(chunk, self.flip(self.me, 2 * want + 1)),
                dst_ref=self.pair_held(chunk, want),
                send_sem=self.pair_out.at[chunk, want],
                recv_sem=self.pair_in.at[chunk, want],
                device_id={"dp": self.flip(self.me, 1)},
                device_id_type=MESH,
            )
            copy.start()
            self.waits.append(copy.wait_send)

    def send(self, chunk, want, source):
        step, bit = self.step_of(chunk, want)
        rest = want ^ (1 << bit)
        copy = pltpu.make_async_remote_copy(
            src_ref=source,
            dst_ref=self.step_held(chunk, step, rest),
            send_sem=self.out_sem.at[chunk, want],
            recv_sem=self.in_sem.at[chunk, step, rest],
            device_id={"dp": self.flip(self.me, 2 << bit)},
            device_id_type=MESH,
        )
        copy.start()
        return copy.wait_send

    def terms(self, chunk, want):
        found = [self.own(chunk, self.flip(self.me, 2 * want)), self.pair_held(chunk, want)]
        pltpu.make_async_copy(found[1], found[1], self.pair_in.at[chunk, want]).wait()
        for step in range(self.step_of(chunk, want)[0]):
            held = self.step_held(chunk, step, want)
            pltpu.make_async_copy(held, held, self.in_sem.at[chunk, step, want]).wait()
            found.append(held)
        return found

    def items(self, lag):
        found = []
        for chunk in range(self.chunks):
            for want in range(1 << self.bits):
                step = self.step_of(chunk, want)[0]
                found.append((chunk + lag * step, step, chunk, want))
        return [item[2:] for item in sorted(found)]

    def finish(self):
        for wait in self.waits:
            wait()


def sum_sems(groups, chunks):
    bits = groups.bit_length() - 2
    dma = pltpu.SemaphoreType.DMA
    return [
        dma((chunks, 1 << bits)),
        dma((chunks, bits, 1 << bits)),
        dma((chunks, 1 << bits)),
        dma((chunks, 1 << bits)),
    ]


class Stream:
    def __init__(self, cube, lag, terms, sums, totals, out, load_sem, save_sem):
        self.cube, self.terms, self.sums, self.totals, self.out = cube, terms, sums, totals, out
        self.load_sem, self.save_sem = load_sem, save_sem
        self.list = cube.items(lag)
        self.at, self.sent, self.saved, self.loads = 0, [], [], None

    def tick(self, times=1):
        for _ in range(times):
            if self.at <= len(self.list):
                loads = self.fetch(self.at) if self.at < len(self.list) else None
                if self.loads is not None:
                    self.add(self.at - 1)
                self.loads = loads
                self.at += 1

    def fetch(self, number):
        slot = number % 2
        loads = []
        for term, ref in enumerate(self.cube.terms(*self.list[number])):
            copy = pltpu.make_async_copy(ref, self.terms.at[slot, term], self.load_sem.at[slot, term])
            copy.start()
            loads.append(copy)
        return loads

    def add(self, number):
        slot = number % 2
        chunk, want = self.list[number]
        for copy in self.loads:
            copy.wait()
        count = len(self.loads)
        if want:
            place = len(self.sent) % self.sums.shape[0]
            if len(self.sent) >= self.sums.shape[0]:
                self.sent[len(self.sent) - self.sums.shape[0]]()
            target = self.sums.at[place]
        else:
            place = len(self.saved) % self.totals.shape[0]
            if len(self.saved) >= self.totals.shape[0]:
                self.saved[len(self.saved) - self.totals.shape[0]]()
            target = self.totals.at[place]

        def row(index, _):
            if count == 2:
                target[index] = self.terms[slot, 0, index] + self.terms[slot, 1, index]
                return 0
            total = self.terms[slot, 0, index].astype(jnp.float32)
            for term in range(1, count):
                total = total + self.terms[slot, term, index].astype(jnp.float32)
            target[index] = total.astype(target.dtype)
            return 0

        lax.fori_loop(0, target.shape[0], row, 0)
        if want:
            self.sent.append(self.cube.send(chunk, want, target))
        else:
            for source, result in self.out(chunk, target):
                pltpu.make_async_copy(source, result, self.save_sem.at[place]).start()
            self.saved.append(pltpu.make_async_copy(target, target, self.save_sem.at[place]).wait)

    def finish(self):
        self.tick(len(self.list) + 1 - self.at)
        for wait in self.sent[-self.sums.shape[0] :] + self.saved[-self.totals.shape[0] :]:
            wait()


class Share:
    def __init__(self, axis, size, held, out_sem, in_sem, source):
        self.axis, self.size, self.held = axis, size, held
        self.out_sem, self.in_sem, self.source = out_sem, in_sem, source
        self.me = lax.axis_index(axis)

    def copy(self, turn):
        peer = lax.rem(self.me + turn, self.size)
        return pltpu.make_async_remote_copy(
            src_ref=self.source(peer),
            dst_ref=self.held.at[self.me],
            send_sem=self.out_sem.at[turn],
            recv_sem=self.in_sem.at[turn],
            device_id={self.axis: peer},
            device_id_type=MESH,
        )

    def begin(self):
        for turn in range(1, self.size):
            self.copy(turn).start()
        self.held[self.me] = self.source(self.me)[...]

    def total(self):
        for turn in range(1, self.size):
            self.copy(turn).wait()
        total = self.held[0]
        for index in range(1, self.size):
            total = total + self.held[index]
        return total


def backward_kernel(groups, parts, heads, heads_kv, home, seg_row, seg_col, attn_gain, moe_gain, tokens, out_grad, middle,
                    router_part, back_in, mixed_in, first_in, qkv_in, mix_in, weights_in, gate_in, up_in, down_in,
                    block_out, tokens_grad, gains_out, router_out, pack_out, gate_out, up_out, down_out, pair_held, step_held,
                    held, come, mixed, mixed_come, grad, qkv, mix, weights, grad_mix, grad_query, grad_key, grad_value,
                    flat, bias, pack, pack_pair, pack_step, stage, land_back, land_mixed, terms, sums, totals,
                    router_all, router_line, gains, gains_line, gains_all,
                    load_sem, cube_sems, pack_sems, term_sem, save_sem, line_out, line_in, sum_out, sum_in, deal_out, deal_in,
                    share_out, share_in):
    low = jnp.bfloat16
    shard, width = tokens.shape
    me, place = lax.axis_index("dp"), lax.axis_index("mp")
    share = heads // heads_kv
    slots = heads + 2 * heads_kv
    bits = groups.bit_length() - 2
    arrays = ((back_in, held), (weights_in, weights), (mix_in, mix), (qkv_in, qkv), (mixed_in, mixed))
    loads = []
    for number, (source, target) in enumerate(arrays):
        loads.append(pltpu.make_async_copy(source, target, load_sem.at[number]))
        loads[-1].start()
    greet(groups, parts)

    gains[...] = jnp.zeros_like(gains)
    count = gate_in.shape[0] // 4
    owner_rows = width // groups

    def own(chunk, owner):
        if chunk < 2 * count:
            ref = (gate_in, up_in)[chunk // count]
            return ref.at[pl.ds(chunk % count * 4, 4), pl.ds(owner * owner_rows, owner_rows)]
        return down_in.at[owner, chunk - 2 * count]

    places = {}

    def step_place(chunk, step, want):
        return step_held.at[chunk, places.setdefault((chunk, step, want), len([k for k in places if k[0] == chunk]))]

    cube = CubeSum(groups, 3 * count, own, lambda chunk, want: pair_held.at[chunk, want], step_place, cube_sems)
    per, hidden, _ = down_out.shape
    subs = 4 // per
    span = hidden // 4 // subs

    def out(chunk, total):
        if chunk < 2 * count:
            return [(total, (gate_out, up_out)[chunk // count].at[pl.ds(chunk % count * 4, 4)])]
        found = []
        for index in range(4):
            row = (chunk - 2 * count) * (hidden // 4) + index % subs * span
            for column in range(width // hidden):
                source = total.at[index, pl.ds(column * span, span)]
                target = down_out.at[index // subs, pl.ds(row, span), pl.ds(column * hidden, hidden)]
                found.append((source, target))
        return found

    stream = Stream(cube, 3, terms, sums, totals, out, term_sem, save_sem)

    back = LineSum(parts, CUTS, held, come, sum_out.at[0], sum_in.at[0])
    loads[0].wait()
    order = far_first(parts)
    for target in order:
        back.begin(back.turned(target))
    for chunk in range(3 * count):
        cube.pair(chunk)
    routers = Share("dp", groups, router_all, share_out.at[0], share_in.at[0], lambda peer: router_part.at[peer])
    routers.begin()
    stream.tick(1)
    for target in order:
        for chunk in range(CUTS):
            back.relay(back.turned(target), chunk)
            stream.tick(1 if target in order[:2] else 0)
    for chunk in range(CUTS):
        back.total(chunk, block_out)
    stage[...] = block_out[...].astype(stage.dtype)
    deal = Exchange(groups, stage, land_back, deal_out.at[0], deal_in.at[0])
    deal.begin()
    back.finish()
    loads[4].wait()
    extra = LineSum(parts, CUTS, mixed, mixed_come, sum_out.at[1], sum_in.at[1])
    extra.begin(extra.turned(order[0]))
    router_line[place] = routers.total()
    router_sums = Share("mp", parts, router_line, share_out.at[1], share_in.at[1], lambda peer: router_line.at[place])
    for turn in range(1, parts):
        router_sums.copy(turn).start()
    sort = sorting(home[...], shard)
    values = middle[...]
    scale = scale_of(values)
    deal.arrive()
    grad_second = mm(sort, land_back[...].astype(low), TN)
    weighted = grad_second * moe_gain[...][None, :]
    inner = jnp.mean(weighted * values, axis=1, keepdims=True)
    gains[0:1, :] = jnp.sum(grad_second * values * scale, axis=0, keepdims=True)
    grad_middle = out_grad[...] + (scale * weighted - values * (scale * scale * scale * inner))
    tokens_grad[...] = grad_middle
    grad[place] = grad_middle.astype(low)
    line = LineGather(parts, CUTS, grad, line_out, line_in)
    for chunk in range(CUTS):
        line.begin(chunk)
    for target in order[1:]:
        extra.begin(extra.turned(target))
    loads[1].wait()

    def mix_back(origin):
        result = mm(grad[origin], weights[:, slots * HD :])
        span = pl.ds(pl.multiple_of(origin * shard, shard), shard)
        for head in range(heads):
            grad_mix[head, span, :] = result[:, head * HD : (head + 1) * HD].astype(low)

    mix_back(place)
    stream.tick(2)
    for distance in range(1, parts):
        for chunk in range(CUTS):
            for way in (0, 1):
                line.step(distance, way, chunk)
            if distance == parts - 1:
                extra.relay(extra.turned(order[0]), chunk)
            stream.tick()
        for way in (0, 1):
            line.from_side(distance, way, mix_back)
    loads[3].wait()

    first_sum = LineSum(parts, CUTS, held, come, sum_out.at[2], sum_in.at[2])
    grad_key[...] = jnp.zeros_like(grad_key)
    grad_value[...] = jnp.zeros_like(grad_value)
    reach = -(-512 // shard)
    for number, target in enumerate(reversed(range(parts))):
        start, stop = target * shard, (target + 1) * shard
        bottom = max(0, target - reach) * shard
        bias[:, : stop - bottom] = bias_of(seg_row, seg_col, start, bottom, stop)

        def attend(head, _):
            group = head // share
            query = qkv[head, start:stop, :]
            keys = qkv[heads + group, bottom:stop, :]
            scores = mm(query, keys, NT) * HD**-0.5 + bias[:, : stop - bottom]
            raised = jnp.exp(scores - jnp.max(scores, axis=1, keepdims=True))
            probs = raised * (1.0 / jnp.sum(raised, axis=1, keepdims=True))
            grad_rows = grad_mix[head, start:stop, :]
            grad_probs = mm(grad_rows, qkv[heads + heads_kv + group, bottom:stop, :], NT)
            inner = jnp.sum(probs * grad_probs, axis=1, keepdims=True)
            grad_scores = (probs * (grad_probs - inner)).astype(low)
            grad_query[head, start:stop, :] = (mm(grad_scores, keys) * HD**-0.5).astype(low)
            grad_key[group, bottom:stop, :] += mm(grad_scores, query, TN)
            grad_value[group, bottom:stop, :] += mm(probs.astype(low), grad_rows, TN)
            return 0

        lax.fori_loop(0, heads, attend, 0)
        pieces = [grad_query[head, start:stop, :] for head in range(heads)]
        pieces += [(grad_key[group, start:stop, :] * HD**-0.5).astype(low) for group in range(heads_kv)]
        pieces += [grad_value[group, start:stop, :].astype(low) for group in range(heads_kv)]
        flat[start:stop, :] = jnp.concatenate(pieces, axis=1)
        held[target] = mm(flat[start:stop, :], weights[:, : slots * HD], NT).astype(low)
        first_sum.begin(target)
        for chunk in range(CUTS):
            if number < parts - 1:
                extra.relay(extra.turned(order[number + 1]), chunk)
            stream.tick(1)
    for target in reversed(range(parts)):
        for chunk in range(CUTS):
            first_sum.relay(target, chunk)
        stream.tick(2)
    loads[2].wait()
    mix_flat = jnp.concatenate([mix[head] for head in range(heads)], axis=1)
    pack[:, slots * HD :] = mm(grad[...].reshape(parts * shard, width), mix_flat, TN).astype(low)
    for chunk in range(CUTS):
        extra.total(chunk, block_out)
        stream.tick()
    deal.finish()
    stage[...] = block_out[...].astype(stage.dtype)
    deal_mixed = Exchange(groups, stage, land_mixed, deal_out.at[1], deal_in.at[1])
    deal_mixed.begin()
    extra.finish()
    first_load = pltpu.make_async_copy(first_in, mixed, load_sem.at[5])
    first_load.start()
    stream.tick(2)
    first_load.wait()
    pack[:, : slots * HD] = mm(mixed[...].reshape(parts * shard, width), flat[...], TN).astype(low)
    cut = owner_rows // 2
    pack_places = {}

    def pack_place(chunk, step, want):
        return pack_step.at[chunk, pack_places.setdefault((chunk, step, want), len([k for k in pack_places if k[0] == chunk]))]

    pack_cube = CubeSum(
        groups,
        2,
        lambda chunk, owner: pack.at[pl.ds(owner * owner_rows + chunk * cut, cut)],
        lambda chunk, want: pack_pair.at[chunk, want],
        pack_place,
        pack_sems,
    )
    for chunk in range(2):
        pack_cube.pair(chunk)
    deal_mixed.arrive()
    home_rows = mm(sort, land_mixed[...].astype(low), TN)
    pack_sent = []
    for chunk, want in pack_cube.items(1):
        stream.tick(1)
        refs = pack_cube.terms(chunk, want)
        total = refs[0][...].astype(jnp.float32)
        for ref in refs[1:]:
            total = total + ref[...].astype(jnp.float32)
        if want:
            refs[0][...] = total.astype(low)
            pack_sent.append(pack_cube.send(chunk, want, refs[0]))
        else:
            pack_out[chunk * cut : (chunk + 1) * cut, :] = total
    for chunk in range(CUTS):
        first_sum.total(chunk, block_out)
    grad_first = block_out[...]
    values = tokens[...]
    scale = scale_of(values)
    weighted = grad_first * attn_gain[...][None, :]
    inner = jnp.mean(weighted * values, axis=1, keepdims=True)
    gains[1:2, :] = jnp.sum(grad_first * values * scale, axis=0, keepdims=True)
    gains_lines = Share("mp", parts, gains_line, share_out.at[2], share_in.at[2], lambda peer: gains)
    gains_lines.begin()
    tokens_grad[...] += scale * weighted - values * (scale * scale * scale * inner)
    block_out[...] = middle[...] + home_rows
    router_out[...] = router_sums.total()
    gains[...] = gains_lines.total()
    gains_rest = Share("dp", groups, gains_all, share_out.at[3], share_in.at[3], lambda peer: gains)
    gains_rest.begin()
    stream.finish()
    gains_out[...] = gains_rest.total()
    line.finish()
    first_sum.finish()
    deal_mixed.finish()
    cube.finish()
    pack_cube.finish()
    for wait in pack_sent:
        wait()


def backward(groups, parts, heads, heads_kv, home, seg, attn_gain, moe_gain, tokens, out_grad, middle, router_part,
             back, mixed, first, qkv, mix, weights, gate_grad, up_grad, down_grad):
    shard, width = tokens.shape
    rows = shard * parts
    low = jnp.bfloat16
    slots = heads + 2 * heads_kv
    columns = weights.shape[1]
    owner_rows, hidden = width // groups, gate_grad.shape[2]
    bits = groups.bit_length() - 2
    chunks = 3 * (E // 4)
    cut = owner_rows // 2
    vmem = pl.BlockSpec(memory_space=pltpu.VMEM)
    hbm = pl.BlockSpec(memory_space=pl.ANY)
    dma = pltpu.SemaphoreType.DMA
    f32 = lambda *shape: jax.ShapeDtypeStruct(shape, jnp.float32)
    unit = (4, owner_rows, hidden)
    held = pltpu.VMEM((parts, shard, width), low)
    come = pltpu.VMEM((parts + 1, shard, width), low)
    line = row_type(shard // groups)
    return pl.pallas_call(
        functools.partial(backward_kernel, groups, parts, heads, heads_kv),
        in_specs=[vmem] * 9 + [hbm] * 9,
        out_specs=[vmem] * 5 + [hbm] * 5,
        out_shape=[
            f32(shard, width),
            f32(shard, width),
            f32(8, width),
            f32(E, owner_rows),
            f32(owner_rows, columns),
            f32(E, owner_rows, hidden),
            f32(E, owner_rows, hidden),
            f32(E // groups, hidden, width),
            jax.ShapeDtypeStruct((chunks, 1 << bits, *unit), low),
            jax.ShapeDtypeStruct((chunks, (1 << bits) - 1, *unit), low),
        ],
        scratch_shapes=[
            held,
            come,
            held,
            come,
            held,
            pltpu.VMEM((slots, rows, HD), low),
            pltpu.VMEM((heads, rows, HD), low),
            pltpu.VMEM((width, columns), low),
            pltpu.VMEM((heads, rows, HD), low),
            pltpu.VMEM((heads, rows, HD), low),
            pltpu.VMEM((heads_kv, rows, HD), jnp.float32),
            pltpu.VMEM((heads_kv, rows, HD), jnp.float32),
            pltpu.VMEM((rows, slots * HD), low),
            pltpu.VMEM((shard, shard * (1 - (-512 // shard))), jnp.float32),
            pltpu.VMEM((width, columns), low),
            pltpu.VMEM((2, 1 << bits, cut, columns), low),
            pltpu.VMEM((2, (1 << bits) - 1, cut, columns), low),
            pltpu.VMEM((shard, width), line),
            pltpu.VMEM((shard, width), line),
            pltpu.VMEM((shard, width), line),
            pltpu.VMEM((2, 2 + bits, *unit), low),
            pltpu.VMEM((4, *unit), low),
            pltpu.VMEM((2, *unit), jnp.float32),
            pltpu.VMEM((groups, E, owner_rows), jnp.float32),
            pltpu.VMEM((parts, E, owner_rows), jnp.float32),
            pltpu.VMEM((8, width), jnp.float32),
            pltpu.VMEM((parts, 8, width), jnp.float32),
            pltpu.VMEM((groups, 8, width), jnp.float32),
            dma((6,)),
            sum_sems(groups, chunks),
            sum_sems(groups, 2),
            dma((2, 2 + bits)),
            dma((2,)),
            dma((2, parts, CUTS)),
            dma((parts, CUTS)),
            dma((3, parts, CUTS)),
            dma((3, parts + 1, CUTS)),
            dma((2, groups)),
            dma((2, groups)),
            dma((4, max(groups, parts))),
            dma((4, max(groups, parts))),
        ],
        compiler_params=pltpu.CompilerParams(
            collective_id=1, has_side_effects=True, vmem_limit_bytes=63 * 2**20
        ),
        cost_estimate=pl.CostEstimate(
            flops=24 * rows * width * columns, bytes_accessed=200 * 2**20, transcendentals=rows * rows * heads
        ),
    )(home, seg[None, :], seg[:, None], attn_gain, moe_gain, tokens, out_grad, middle, router_part,
      back, mixed, first, qkv, mix, weights, gate_grad, up_grad, down_grad)


def body(
    tokens,
    attn_gain,
    w_query,
    w_key,
    w_value,
    w_out,
    moe_gain,
    w_router,
    w_gate,
    w_up,
    w_down,
    seq_lengths,
    deal_order,
    expert_ids,
    out_grad,
):
    groups, parts = lax.axis_size("dp"), lax.axis_size("mp")
    rows = tokens.shape[0] * parts
    low_type = jnp.bfloat16
    heads, heads_kv = w_query.shape[1] // HD, w_key.shape[1] // HD
    wpack = jnp.concatenate(
        [w_query, w_key, w_value, w_out.T, jnp.pad(w_router, ((0, 0), (0, 128 - E)))], axis=1
    ).astype(low_type)
    home, code, counts = deal_tables(deal_order, expert_ids, rows)
    segment = segment_of(seq_lengths[0], rows)
    middle, router_w, first_full, qkv, mix, weights, second_full, grad_full, gate_w, up_w, down_w = forward(
        groups, parts, home[None, :], segment, attn_gain, moe_gain, tokens, out_grad, wpack, w_gate, w_up, w_down, heads, heads_kv
    )
    mixed, back, gate_grad, up_grad, down_grad, router_part = experts(
        groups,
        second_full.reshape(rows, D),
        grad_full.reshape(rows, D),
        code,
        counts,
        router_w,
        gate_w,
        up_w,
        down_w,
    )
    block_out, tokens_grad, gains, router_sum, pack_sum, gate_sum, up_sum, down_sum, _, _ = backward(
        groups,
        parts,
        heads,
        heads_kv,
        home[None, :],
        segment,
        attn_gain,
        moe_gain,
        tokens,
        out_grad,
        middle,
        router_part,
        back.reshape(second_full.shape),
        mixed.reshape(second_full.shape),
        first_full,
        qkv,
        mix,
        weights,
        gate_grad,
        up_grad,
        down_grad,
    )
    columns, columns_kv = heads * HD, heads_kv * HD
    return (
        block_out,
        tokens_grad,
        gains[1],
        pack_sum[:, :columns],
        pack_sum[:, columns : columns + columns_kv],
        pack_sum[:, columns + columns_kv : columns + 2 * columns_kv],
        pack_sum[:, columns + 2 * columns_kv :].T,
        gains[0],
        router_sum.T,
        gate_sum,
        up_sum,
        down_sum,
    )


def solution(mesh):
    return jax.shard_map(
        body,
        mesh=mesh,
        in_specs=(
            P(("dp", "mp"), None),
            P(),
            P("dp", "mp"),
            P("dp", "mp"),
            P("dp", "mp"),
            P("mp", "dp"),
            P(),
            P("dp", None),
            P(None, "dp", "mp"),
            P(None, "dp", "mp"),
            P("dp", "mp", None),
            P("dp", None),
            P(),
            P("dp", None),
            P(("dp", "mp"), None),
        ),
        out_specs=(
            P(("dp", "mp"), None),
            P(("dp", "mp"), None),
            P(),
            P("dp", "mp"),
            P("dp", "mp"),
            P("dp", "mp"),
            P("mp", "dp"),
            P(),
            P("dp", None),
            P(None, "dp", "mp"),
            P(None, "dp", "mp"),
            P("dp", "mp", None),
        ),
        check_vma=False,
    )
```
